512 devices in a mesh: tm: 16 (over z, core), space: 32 (over x, y).
Axes of the slice: x: 4, y: 8, z: 8, core: 2. Of those that a mesh axis runs over, the one named last changes fastest.
Arguments:
- queries: bfloat16 [16, 4096, 1120], P('tm', 'space'), may hold values from -6 to 6
- keys_in: bfloat16 [16, 4096, 1120], P('tm', 'space'), may hold values from -30 to 30
- values_in: bfloat16 [16, 4096, 1120], P('tm', 'space'), may hold values from -10 to 10
- grad_attn: bfloat16 [16, 4096, 1120], P('tm', 'space'), may hold values from -6 to 6
Outputs:
- mixed: bfloat16 [16, 4096, 1120], P('tm', 'space')
- grad_queries: bfloat16 [16, 4096, 1120], P('tm', 'space')
- grad_keys: bfloat16 [16, 4096, 1120], P('tm', 'space')
- values_gradient: bfloat16 [16, 4096, 1120], P('tm', 'space')
The draws below stay inside these ranges and needn't reach their ends.
All inputs are finite; a program needn't handle non-finite values.
Results may differ from the reference program's by a relative error of at most 0.001.
Values sent between devices are 32-bit elements; how exact they have to be, the bound alone decides.
No kernel may reach another device: no remote copies, remote signals or barrier semaphores. Data moves between devices by JAX's collectives and lax.ppermute only.
A program may use at most 64 MiB of HBM per device.

```python
import jax
import jax.numpy as jnp
from jax import lax

HEADS = 10
HEAD_DIM = 112
C = 1120
GROUPS = 16
ROWS = 4096


def draw_keys_in(key, part):
    first, second = jax.random.split(jax.random.fold_in(key, 11))
    blocks = ROWS // 32
    scales = jnp.exp(jax.random.uniform(first, (GROUPS, blocks, 1, HEADS, 1), jnp.float32, jnp.log(0.3), jnp.log(3.0)))
    noise = jnp.clip(jax.random.normal(second, (GROUPS, blocks, 32, HEADS, HEAD_DIM), jnp.float32), -5.0, 5.0)
    return (noise * scales).reshape(GROUPS, ROWS, C).astype(jnp.bfloat16)


def draw_values_in(key, part):
    first, second = jax.random.split(jax.random.fold_in(key, 23))
    blocks = ROWS // 32
    means = jnp.clip(jax.random.normal(first, (GROUPS, blocks, 1, C), jnp.float32), -4.0, 4.0)
    noise = jnp.clip(jax.random.normal(second, (GROUPS, blocks, 32, C), jnp.float32), -4.0, 4.0)
    return (means + noise).reshape(GROUPS, ROWS, C).astype(jnp.bfloat16)


def block_scale(own_key, dims, cuts, low, largest):
    def one(dim, shards_of):
        steps = jax.random.uniform(jax.random.fold_in(jax.random.fold_in(own_key, 6), dim), (shards_of,), jnp.float32, low / len(cuts), largest / len(cuts))
        return jnp.repeat(jnp.exp(steps), dims[dim] // shards_of).reshape((-1,) + (1,) * (len(dims) - dim - 1))

    level = one(*cuts[0])
    for cut in cuts[1:]:
        level = level * one(*cut)
    return level


def centred(stream_key, dims, spread, bound, shards=(), kind=jnp.bfloat16):
    gain = block_scale(stream_key, dims, shards, -0.22, 0.18) if shards else 1.0
    entries = jax.random.normal(stream_key, dims, jnp.float32) * spread * gain
    return jnp.minimum(jnp.maximum(entries, -bound), bound).astype(kind)


def setup_inputs(seed: int = 0) -> dict:
    keys = jax.random.split(jax.random.key(seed), 5)
    queries = centred(keys[0], (GROUPS, ROWS, C), 1.0, 6.0, ((0, 16), (1, 32)))
    keys_in = draw_keys_in(jax.random.fold_in(keys[4], 71), 0)
    values_in = draw_values_in(jax.random.fold_in(keys[4], 71), 0)
    grad_attn = centred(keys[3], (GROUPS, ROWS, C), 1.0, 6.0, ((0, 16), (1, 32)))
    return dict(queries=queries, keys_in=keys_in, values_in=values_in, grad_attn=grad_attn)


HIGH_PRECISION = lax.Precision.HIGHEST


def reference(queries, keys_in, values_in, grad_attn):
    phi_q = jax.nn.relu(queries.astype(jnp.float32)).reshape(GROUPS, ROWS, HEADS, HEAD_DIM)
    phi_k = jax.nn.relu(keys_in.astype(jnp.float32)).reshape(GROUPS, ROWS, HEADS, HEAD_DIM)
    vals = values_in.astype(jnp.float32).reshape(GROUPS, ROWS, HEADS, HEAD_DIM)
    state_local = jnp.einsum("grhk,grhv->ghkv", phi_k, vals, precision=HIGH_PRECISION)
    total_local = jnp.sum(phi_k, axis=1)
    running_state = jnp.cumsum(state_local, axis=0)
    running_total = jnp.cumsum(total_local, axis=0)

    def forward_group(args):
        query_features, step_state, step_total = args
        numerator = jnp.einsum("igx,gxb->igb", query_features, step_state, precision=HIGH_PRECISION)
        denom = jnp.einsum("rhk,hk->rh", query_features, step_total, precision=HIGH_PRECISION) + 1.0
        return numerator / denom[..., None], denom

    attn_f, denom = lax.map(forward_group, (phi_q, running_state, running_total))
    mixed = attn_f.reshape(GROUPS, ROWS, C).astype(jnp.bfloat16)
    g_out = grad_attn.astype(jnp.float32).reshape(GROUPS, ROWS, HEADS, HEAD_DIM)

    def backward_group(args):
        query_features, go, af, dn, step_state, step_total = args
        numerator_gradient = go / dn[..., None]
        denominator_gradient = -jnp.sum(go * af, axis=-1) / dn
        feature_gradient = jnp.einsum("tqd,qwd->tqw", numerator_gradient, step_state, precision=HIGH_PRECISION) + denominator_gradient[..., None] * step_total[None]
        step_state_gradient = jnp.einsum("isp,isz->spz", query_features, numerator_gradient, precision=HIGH_PRECISION)
        gtt = jnp.einsum("rhk,rh->hk", query_features, denominator_gradient, precision=HIGH_PRECISION)
        return feature_gradient, step_state_gradient, gtt

    feature_gradient, gstate_local, gtotal_local = lax.map(backward_group, (phi_q, g_out, attn_f, denom, running_state, running_total))
    grad_queries = jnp.where(queries.reshape(GROUPS, ROWS, HEADS, HEAD_DIM) > 0, feature_gradient, 0.0)
    state_gradient = jnp.flip(jnp.cumsum(jnp.flip(gstate_local, 0), axis=0), 0)
    total_gradient = jnp.flip(jnp.cumsum(jnp.flip(gtotal_local, 0), axis=0), 0)

    def key_group(args):
        key_features, value_block, state_gradient_step, total_gradient_step = args
        value_gradient = jnp.einsum("igx,gxb->igb", key_features, state_gradient_step, precision=HIGH_PRECISION)
        key_gradient = jnp.einsum("tqd,qwd->tqw", value_block, state_gradient_step, precision=HIGH_PRECISION) + total_gradient_step[None]
        return value_gradient, key_gradient

    values_gradient, key_gradient = lax.map(key_group, (phi_k, vals, state_gradient, total_gradient))
    grad_keys = jnp.where(keys_in.reshape(GROUPS, ROWS, HEADS, HEAD_DIM) > 0, key_gradient, 0.0)
    return (mixed,
            grad_queries.reshape(GROUPS, ROWS, C).astype(jnp.bfloat16),
            grad_keys.reshape(GROUPS, ROWS, C).astype(jnp.bfloat16),
            values_gradient.reshape(GROUPS, ROWS, C).astype(jnp.bfloat16))
```

```python
import jax
import jax.numpy as jnp
from jax import lax
from jax.sharding import PartitionSpec as P

HEAD_DIM = 112
HIGH = lax.Precision.HIGHEST


def exchanged(pieces, axis):
    return lax.all_to_all(pieces, axis, 0, 0, tiled=True)


def to_all(piece, axis):
    size = lax.axis_size(axis)
    return exchanged(jnp.broadcast_to(piece[None], (size, *piece.shape)), axis)


def body(queries, keys_in, values_in, grad_attn):
    row_count, channels = queries.shape[1:]
    heads = channels // HEAD_DIM
    spaces, groups = lax.axis_size("space"), lax.axis_size("tm")
    mine = lax.axis_index("tm")
    by_head = (row_count, heads, HEAD_DIM)
    share = channels * HEAD_DIM // spaces
    query_rows, key_rows, value_rows, g_rows = (
        a[0].reshape(by_head) for a in (queries, keys_in, values_in, grad_attn)
    )
    key_pos = jax.nn.relu(key_rows)
    query_pos = jax.nn.relu(query_rows).astype(jnp.float32)
    g_out = g_rows.astype(jnp.float32)

    state_part = jnp.einsum("rhk,rhv->hkv", key_pos, value_rows, preferred_element_type=jnp.float32)
    total_part = jnp.sum(key_pos, axis=0, dtype=jnp.float32).reshape(channels)
    sent = jnp.concatenate(
        [state_part.reshape(spaces, share), jnp.broadcast_to(total_part[None], (spaces, channels))],
        axis=1,
    )
    own = jnp.sum(exchanged(sent, "space"), axis=0)

    earlier = (jnp.arange(groups) <= mine)[:, None]
    prefix = jnp.sum(jnp.where(earlier, to_all(own, "tm"), 0.0), axis=0)
    state_share, total = prefix[:share], prefix[share:].reshape(heads, HEAD_DIM)

    denom = jnp.einsum("rhk,hk->rh", query_pos, total, precision=HIGH) + 1.0
    g_num = g_out / denom[..., None]
    gstate_part = jnp.einsum("rhk,rhv->hkv", query_pos, g_num, precision=HIGH)

    sent = jnp.concatenate(
        [jnp.broadcast_to(state_share[None], (spaces, share)), gstate_part.reshape(spaces, share)],
        axis=1,
    )
    got = exchanged(sent, "space")
    state = got[:, :share].reshape(heads, HEAD_DIM, HEAD_DIM)
    gshare = jnp.sum(got[:, share:], axis=0)

    attn_f = jnp.einsum("rhk,hkv->rhv", query_pos, state, precision=HIGH) / denom[..., None]
    g_den = -jnp.sum(g_out * attn_f, axis=-1) / denom
    gtotal_part = jnp.einsum("rhk,rh->hk", query_pos, g_den, precision=HIGH).reshape(channels)

    later = (jnp.arange(groups) >= mine)[:, None]
    suffix = jnp.sum(
        jnp.where(later, to_all(jnp.concatenate([gshare, gtotal_part]), "tm"), 0.0), axis=0
    )

    got = to_all(suffix, "space")
    gstate = got[:, :share].reshape(heads, HEAD_DIM, HEAD_DIM)
    gtotal = jnp.sum(got[:, share:], axis=0).reshape(heads, HEAD_DIM)

    feature = (
        jnp.einsum("rhv,hkv->rhk", g_num, state, precision=HIGH) + g_den[..., None] * total[None]
    )
    grad_queries = jnp.where(query_rows > 0, feature, 0.0)
    key_wide = key_pos.astype(jnp.float32)
    values_gradient = jnp.einsum("rhk,hkv->rhv", key_wide, gstate, precision=HIGH)
    key_gradient = (
        jnp.einsum("rhv,hkv->rhk", value_rows.astype(jnp.float32), gstate, precision=HIGH)
        + gtotal[None]
    )
    grad_keys = jnp.where(key_rows > 0, key_gradient, 0.0)
    return tuple(
        a.reshape(1, row_count, channels).astype(jnp.bfloat16)
        for a in (attn_f, grad_queries, grad_keys, values_gradient)
    )


def solution(mesh):
    placed = P("tm", "space", None)
    return jax.shard_map(
        body, mesh=mesh, in_specs=(placed,) * 4, out_specs=(placed,) * 4, check_vma=False
    )
```

```python
import functools

import jax
import jax.numpy as jnp
from jax import lax
from jax.experimental import pallas as pl
from jax.experimental.pallas import tpu as pltpu
from jax.sharding import PartitionSpec as P

HEAD_DIM = 112
LANES = 128
SLAB = 8
F32, BF16 = jnp.float32, jnp.bfloat16
VMEM = pl.BlockSpec(memory_space=pltpu.VMEM)
SMEM = pl.BlockSpec(memory_space=pltpu.SMEM)
NT = (((1,), (1,)), ((), ()))


class Tile:
    def __init__(self, j, channels):
        self.j, self.at = j, LANES * j
        self.width = min(LANES, channels - self.at)
        self.first = self.at // HEAD_DIM
        self.last = (self.at + self.width - 1) // HEAD_DIM
        self.here = slice(self.at, self.at + self.width)
        self.cut = min(self.width, HEAD_DIM * (self.first + 1) - self.at)
        self.pair = slice(HEAD_DIM * self.first, HEAD_DIM * (self.last + 1))


def tiles(channels):
    return [Tile(j, channels) for j in range(-(-channels // LANES))]


def dot(a, b):
    return jnp.dot(a, b, preferred_element_type=F32)


def dot_rows(a, b):
    return lax.dot_general(a, b, (((1,), (1,)), ((), ())), preferred_element_type=F32)


def halves(x):
    hi = x.astype(BF16)
    return hi, (x - hi.astype(F32)).astype(BF16)


def thirds(x):
    hi = x.astype(BF16)
    rest = x - hi.astype(F32)
    mid = rest.astype(BF16)
    return hi, mid, (rest - mid.astype(F32)).astype(BF16)


def relu(x):
    return jnp.maximum(x, jnp.zeros_like(x))


def lane(shape):
    return lax.broadcasted_iota(jnp.int32, shape, 1)


def row(shape):
    return lax.broadcasted_iota(jnp.int32, shape, 0)


def of_head(h):
    return slice(HEAD_DIM * h, HEAD_DIM * (h + 1))


def on_own_head(tile, x):
    heads = jnp.where(lane(x.shape) < tile.cut, tile.first, tile.last)
    return jnp.where(row(x.shape) == heads, x, 0.0)


def heads_apart(tile, both):
    if tile.first == tile.last:
        return both
    top, bottom = both[:HEAD_DIM], both[HEAD_DIM:]
    return jnp.where(lane(top.shape) < tile.cut, top, bottom)


class Slabs:
    def __init__(self, pitch, each, base=0):
        self.pitch, self.each, self.base = pitch, each, base

    def rows(self, tile):
        for i in range(HEAD_DIM // SLAB):
            number = HEAD_DIM // SLAB * tile.j + i
            at = self.pitch * (number // self.each) + self.base + SLAB * (number % self.each)
            yield slice(SLAB * i, SLAB * (i + 1)), slice(at, at + SLAB)

    def put(self, ref, tile, value):
        for here, there in self.rows(tile):
            ref[there, : tile.width] = value[here]

    def get(self, ref, tile):
        parts = [ref[there, : tile.width] for _, there in self.rows(tile)]
        return jnp.concatenate(parts, axis=0)


def by_state(flat_ref, rows_ref, h):
    channels = flat_ref.shape[1]
    start = HEAD_DIM * h // LANES * LANES
    stop = min(channels, -(-HEAD_DIM * (h + 1) // LANES) * LANES)
    s = flat_ref[:, start:stop]
    c = lane(s.shape) + start
    hi, lo = halves(jnp.where((c >= HEAD_DIM * h) & (c < HEAD_DIM * (h + 1)), s, 0.0))
    rhs = relu(rows_ref[start:stop, :])
    return dot(hi, rhs) + dot(lo, rhs)


def turn(tile, state, extra, hi_ref, lo_ref):
    hi, lo = halves(jnp.concatenate([state, extra], axis=0).T)
    hi_ref[tile.here, :], lo_ref[tile.here, :] = hi, lo


def with_rows(x, rest):
    return jnp.concatenate([x, rest.astype(BF16)], axis=0)


def states_kernel(slabs, pieces, k_ref, v_ref, out_ref, total_ref):
    channels, rows = k_ref.shape
    out_ref[...] = jnp.zeros_like(out_ref)
    total_ref[...] = jnp.zeros_like(total_ref)
    ones = jnp.ones((16, rows), BF16)
    for t in tiles(channels):
        keys = relu(k_ref[t.here, :])
        slabs.put(out_ref, t, heads_apart(t, dot_rows(v_ref[t.pair, :], keys)))
        total_ref[t.j : t.j + 1, : t.width] = dot_rows(ones, keys)[:1]
    total = total_ref[...]
    for s in range(pieces):
        at = slabs.pitch * s + SLAB * slabs.each
        out_ref[at : at + len(total), :] = total


def sum_kernel(sources, targets, pitch, in_ref, out_ref):
    own = in_ref[0:pitch, :]
    for s in range(1, sources):
        own = own + in_ref[pitch * s : pitch * (s + 1), :]
    for s in range(targets):
        out_ref[pitch * s : pitch * (s + 1), :] = own


def kept(in_ref, groups, pitch, keep):
    total = None
    for g in range(groups):
        part = jnp.where(keep(g), in_ref[pitch * g : pitch * (g + 1), :], 0.0)
        total = part if total is None else total + part
    return total


def suffix_kernel(groups, targets, pitch, mine_ref, in_ref, out_ref):
    mine = mine_ref[0]
    own = kept(in_ref, groups, pitch, lambda g: g >= mine)
    for s in range(targets):
        out_ref[pitch * s : pitch * (s + 1), :] = own


def denominators(q_ref, total, padded):
    den = None
    for t in tiles(q_ref.shape[0]):
        spot = on_own_head(t, jnp.broadcast_to(total[t.j : t.j + 1, : t.width], (padded, t.width)))
        term = dot(jnp.concatenate(thirds(spot), axis=0), relu(q_ref[t.here, :]))
        den = term if den is None else den + term
    return den[:padded] + den[padded : 2 * padded] + den[2 * padded :] + 1.0


def gradient_states(slabs, q_ref, g_ref, rec, out_ref, hi_ref, lo_ref):
    channels = q_ref.shape[0]
    for h in range(channels // HEAD_DIM):
        hi, lo = halves(g_ref[of_head(h), :].astype(F32) * rec[h : h + 1])
        hi_ref[of_head(h), :], lo_ref[of_head(h), :] = hi, lo
    for t in tiles(channels):
        rhs = relu(q_ref[t.here, :])
        both = dot_rows(hi_ref[t.pair, :], rhs) + dot_rows(lo_ref[t.pair, :], rhs)
        slabs.put(out_ref, t, heads_apart(t, both))


def denominator_kernel(groups, spaces, pitch, slabs, mine_ref, in_ref, q_ref, g_ref, out_ref, rec_ref, total_ref, hi_ref, lo_ref):
    mine = mine_ref[0]
    out_ref[...] = jnp.zeros_like(out_ref)
    own = kept(in_ref, groups, pitch, lambda g: g <= mine)
    share, total = own[: slabs.base], own[slabs.base :]
    total_ref[...] = total
    rec = 1.0 / denominators(q_ref, total, rec_ref.shape[0])
    rec_ref[...] = rec
    gradient_states(slabs, q_ref, g_ref, rec, out_ref, hi_ref, lo_ref)
    for s in range(spaces):
        out_ref[slabs.pitch * s : slabs.pitch * s + slabs.base, :] = share


def attention(slabs, in_ref, q_ref, g_ref, rec, mixed_ref, sums_ref, gt_ref, flat_ref):
    channels = q_ref.shape[0]
    padded = rec.shape[0]
    for t in tiles(channels):
        flat_ref[:, t.here] = slabs.get(in_ref, t)
    sums_ref[...] = jnp.zeros_like(sums_ref)
    gt_ref[...] = jnp.zeros_like(gt_ref)
    for h in range(channels // HEAD_DIM):
        attn = by_state(flat_ref, q_ref, h) * rec[h : h + 1]
        mixed_ref[of_head(h), :] = attn.astype(BF16)
        sums_ref[h : h + 1, :] = jnp.sum(g_ref[of_head(h), :].astype(F32) * attn, axis=0, keepdims=True)
    pair = jnp.concatenate(halves(-sums_ref[...] * rec), axis=0)
    for t in tiles(channels):
        term = dot_rows(pair, relu(q_ref[t.here, :]))
        term = on_own_head(t, term[:padded] + term[padded:])
        gt_ref[t.j : t.j + 1, : t.width] = jnp.sum(term, axis=0, keepdims=True)


def attention_kernel(spaces, groups, pitch, slabs, in_ref, q_ref, g_ref, rec_ref, out_ref, mixed_ref, sums_ref, flat_ref, gt_ref):
    attention(slabs, in_ref, q_ref, g_ref, rec_ref[...], mixed_ref, sums_ref, gt_ref, flat_ref)
    size = SLAB * slabs.each
    share = in_ref[size : 2 * size, :]
    for s in range(1, spaces):
        at = slabs.pitch * s + size
        share = share + in_ref[at : at + size, :]
    own = jnp.concatenate([share, gt_ref[...]], axis=0)
    for g in range(groups):
        out_ref[pitch * g : pitch * (g + 1), :] = own


def queries_kernel(slabs, in_ref, q_ref, g_ref, rec_ref, sums_ref, total_ref, out_ref, hi_ref, lo_ref):
    channels, rows = q_ref.shape
    for t in tiles(channels):
        shape = (LANES - HEAD_DIM, t.width)
        extra = jnp.where(row(shape) < 2, jnp.broadcast_to(total_ref[t.j : t.j + 1, : t.width], shape), 0.0)
        turn(t, slabs.get(in_ref, t), extra, hi_ref, lo_ref)
    for h in range(channels // HEAD_DIM):
        hi, lo = halves(-sums_ref[h : h + 1, :])
        shape = (LANES - HEAD_DIM, rows)
        rest = jnp.where(row(shape) == 0, jnp.broadcast_to(hi.astype(F32), shape), 0.0)
        rest = jnp.where(row(shape) == 1, jnp.broadcast_to(lo.astype(F32), shape), rest)
        rhs = with_rows(g_ref[of_head(h), :], rest)
        feature = (dot(hi_ref[of_head(h), :], rhs) + dot(lo_ref[of_head(h), :], rhs)) * rec_ref[h : h + 1, :]
        q = q_ref[of_head(h), :].astype(F32)
        out_ref[of_head(h), :] = jnp.where(q > 0, feature, 0.0).astype(BF16)


def keys(slabs, in_ref, total, k_ref, v_ref, gk_ref, gv_ref, flat_ref, hi_ref, lo_ref):
    channels, rows = k_ref.shape
    for t in tiles(channels):
        shape = (LANES - HEAD_DIM, t.width)
        extra = jnp.where(row(shape) < 1, jnp.broadcast_to(total[t.j : t.j + 1, : t.width], shape), 0.0)
        state = slabs.get(in_ref, t)
        flat_ref[:, t.here] = state
        turn(t, state, extra, hi_ref, lo_ref)
    ones = jnp.ones((LANES - HEAD_DIM, rows), BF16)
    for h in range(channels // HEAD_DIM):
        gv_ref[of_head(h), :] = by_state(flat_ref, k_ref, h).astype(BF16)
        rhs = with_rows(v_ref[of_head(h), :], ones)
        grad = dot(hi_ref[of_head(h), :], rhs) + dot(lo_ref[of_head(h), :], rhs)
        k = k_ref[of_head(h), :].astype(F32)
        gk_ref[of_head(h), :] = jnp.where(k > 0, grad, 0.0).astype(BF16)


def keys_kernel(spaces, slabs, in_ref, k_ref, v_ref, gk_ref, gv_ref, flat_ref, hi_ref, lo_ref):
    base = SLAB * slabs.each
    total = in_ref[base : slabs.pitch, :]
    for s in range(1, spaces):
        total = total + in_ref[slabs.pitch * s + base : slabs.pitch * (s + 1), :]
    keys(slabs, in_ref, total, k_ref, v_ref, gk_ref, gv_ref, flat_ref, hi_ref, lo_ref)


def call(kernel, out, in_specs, scratch=(), flops=10**7, moved=10**6):
    shapes = [jax.ShapeDtypeStruct(s, d) for s, d in out]
    several = len(shapes) > 1
    return pl.pallas_call(
        kernel,
        out_shape=shapes if several else shapes[0],
        in_specs=in_specs,
        out_specs=[VMEM] * len(shapes) if several else VMEM,
        scratch_shapes=[pltpu.VMEM(s, d) for s, d in scratch],
        cost_estimate=pl.CostEstimate(flops=flops, bytes_accessed=moved, transcendentals=0),
        compiler_params=pltpu.CompilerParams(vmem_limit_bytes=24 * 2**20),
    )


def exchanged(message, axis):
    pieces = message.reshape(lax.axis_size(axis), -1)
    return lax.all_to_all(pieces, axis, 0, 0, tiled=True).reshape(message.shape)


def body(queries, keys_in, values_in, grad_attn):
    q, k, v, g = (a[0].T for a in (queries, keys_in, values_in, grad_attn))
    channels, rows = q.shape
    spaces, groups = lax.axis_size("space"), lax.axis_size("tm")
    mine = lax.axis_index("tm").astype(jnp.int32).reshape(1)
    count = len(tiles(channels))
    each = -(-count * (HEAD_DIM // SLAB) // spaces)
    base = SLAB * each
    pitch = base + count
    first, second = Slabs(pitch, each), Slabs(2 * base, each, base)
    flat, line = ((HEAD_DIM, channels), F32), ((count, LANES), F32)
    whole, small = ((channels, rows), BF16), ((16, rows), F32)

    sent = call(
        functools.partial(states_kernel, first, spaces),
        [((spaces * pitch, LANES), F32)], [VMEM] * 2, [line],
    )(k, v)
    sent = call(
        functools.partial(sum_kernel, spaces, groups, pitch),
        [((groups * pitch, LANES), F32)], [VMEM],
    )(exchanged(sent, "space"))
    sent, rec, total = call(
        functools.partial(denominator_kernel, groups, spaces, pitch, second),
        [((spaces * 2 * base, LANES), F32), small, line], [SMEM] + [VMEM] * 3, [whole, whole],
    )(mine, exchanged(sent, "tm"), q, g)
    states = exchanged(sent, "space")
    got = Slabs(2 * base, each)
    sent, mixed, sums = call(
        functools.partial(attention_kernel, spaces, groups, pitch, got),
        [((groups * pitch, LANES), F32), whole, small], [VMEM] * 4, [flat, line],
    )(states, q, g, rec)
    sent = call(
        functools.partial(suffix_kernel, groups, spaces, pitch),
        [((spaces * pitch, LANES), F32)], [SMEM, VMEM],
    )(mine, exchanged(sent, "tm"))
    grad_queries = call(
        functools.partial(queries_kernel, got), [whole], [VMEM] * 6, [whole, whole],
    )(states, q, g, rec, sums, total)
    grad_keys, values_gradient = call(
        functools.partial(keys_kernel, spaces, first), [whole] * 2, [VMEM] * 3, [flat, whole, whole],
    )(exchanged(sent, "space"), k, v)
    return tuple(a.T[None] for a in (mixed, grad_queries, grad_keys, values_gradient))


def solution(mesh):
    placed = P("tm", "space", None)
    return jax.shard_map(
        body, mesh=mesh, in_specs=(placed,) * 4, out_specs=(placed,) * 4, check_vma=False
    )
```

```python
import functools

import jax
import jax.numpy as jnp
from jax import lax
from jax.experimental import pallas as pl
from jax.experimental.pallas import tpu as pltpu
from jax.sharding import Mesh
from jax.sharding import PartitionSpec as P

HEAD_DIM = 112
LANES = 128
SLAB = 8
F32, BF16 = jnp.float32, jnp.bfloat16
VMEM = pl.BlockSpec(memory_space=pltpu.VMEM)
SMEM = pl.BlockSpec(memory_space=pltpu.SMEM)
NT = (((1,), (1,)), ((), ()))


class Tile:
    def __init__(self, j, channels):
        self.j, self.at = j, LANES * j
        self.width = min(LANES, channels - self.at)
        self.first = self.at // HEAD_DIM
        self.last = (self.at + self.width - 1) // HEAD_DIM
        self.here = slice(self.at, self.at + self.width)
        self.cut = min(self.width, HEAD_DIM * (self.first + 1) - self.at)
        self.pair = slice(HEAD_DIM * self.first, HEAD_DIM * (self.last + 1))


def tiles(channels):
    return [Tile(j, channels) for j in range(-(-channels // LANES))]


def dot(a, b):
    return jnp.dot(a, b, preferred_element_type=F32)


def dot_rows(a, b):
    return lax.dot_general(a, b, (((1,), (1,)), ((), ())), preferred_element_type=F32)


def halves(x):
    hi = x.astype(BF16)
    return hi, (x - hi.astype(F32)).astype(BF16)


def thirds(x):
    hi = x.astype(BF16)
    rest = x - hi.astype(F32)
    mid = rest.astype(BF16)
    return hi, mid, (rest - mid.astype(F32)).astype(BF16)


def relu(x):
    return jnp.maximum(x, jnp.zeros_like(x))


def lane(shape):
    return lax.broadcasted_iota(jnp.int32, shape, 1)


def row(shape):
    return lax.broadcasted_iota(jnp.int32, shape, 0)


def of_head(h):
    return slice(HEAD_DIM * h, HEAD_DIM * (h + 1))


def on_own_head(tile, x):
    heads = jnp.where(lane(x.shape) < tile.cut, tile.first, tile.last)
    return jnp.where(row(x.shape) == heads, x, 0.0)


def heads_apart(tile, both):
    if tile.first == tile.last:
        return both
    top, bottom = both[:HEAD_DIM], both[HEAD_DIM:]
    return jnp.where(lane(top.shape) < tile.cut, top, bottom)


class Slabs:
    def __init__(self, pitch, each, base=0):
        self.pitch, self.each, self.base = pitch, each, base

    def rows(self, tile):
        for i in range(HEAD_DIM // SLAB):
            number = HEAD_DIM // SLAB * tile.j + i
            at = self.pitch * (number // self.each) + self.base + SLAB * (number % self.each)
            yield slice(SLAB * i, SLAB * (i + 1)), slice(at, at + SLAB)

    def put(self, ref, tile, value):
        for here, there in self.rows(tile):
            ref[there, : tile.width] = value[here]

    def get(self, ref, tile):
        parts = [ref[there, : tile.width] for _, there in self.rows(tile)]
        return jnp.concatenate(parts, axis=0)


def by_state(flat_ref, rows_ref, h):
    channels = flat_ref.shape[1]
    start = HEAD_DIM * h // LANES * LANES
    stop = min(channels, -(-HEAD_DIM * (h + 1) // LANES) * LANES)
    s = flat_ref[:, start:stop]
    c = lane(s.shape) + start
    hi, lo = halves(jnp.where((c >= HEAD_DIM * h) & (c < HEAD_DIM * (h + 1)), s, 0.0))
    rhs = relu(rows_ref[start:stop, :])
    return dot(hi, rhs) + dot(lo, rhs)


def turn(tile, state, extra, hi_ref, lo_ref):
    hi, lo = halves(jnp.concatenate([state, extra], axis=0).T)
    hi_ref[tile.here, :], lo_ref[tile.here, :] = hi, lo


def with_rows(x, rest):
    return jnp.concatenate([x, rest.astype(BF16)], axis=0)


def states_kernel(slabs, pieces, k_ref, v_ref, out_ref, total_ref):
    channels, rows = k_ref.shape
    out_ref[...] = jnp.zeros_like(out_ref)
    total_ref[...] = jnp.zeros_like(total_ref)
    ones = jnp.ones((16, rows), BF16)
    for t in tiles(channels):
        keys = relu(k_ref[t.here, :])
        slabs.put(out_ref, t, heads_apart(t, dot_rows(v_ref[t.pair, :], keys)))
        total_ref[t.j : t.j + 1, : t.width] = dot_rows(ones, keys)[:1]
    total = total_ref[...]
    for s in range(pieces):
        at = slabs.pitch * s + SLAB * slabs.each
        out_ref[at : at + len(total), :] = total


def total_of(parts):
    parts = list(parts)
    out = parts[0]
    for part in parts[1:]:
        out = out + part
    return out


def cut_rows(ref, pitch, piece, start, size):
    at = pitch * piece + start
    return ref[at : at + size, :]


def to_rows_kernel(sizes, in_ref, out_ref):
    chips, rows, base, pitch = sizes
    height = in_ref.shape[0] // (2 * chips)
    sums = [
        total_of(cut_rows(in_ref, height, chips * c + x, 0, height) for x in range(chips))
        for c in range(2)
    ]
    totals = jnp.concatenate([s[rows * base :] for s in sums], axis=0)
    for y in range(rows):
        for c in range(2):
            at = pitch * y + base * c
            out_ref[at : at + base, :] = sums[c][base * y : base * (y + 1)]
        out_ref[pitch * y + 2 * base : pitch * (y + 1), :] = totals


def to_planes_kernel(pieces, pitch, in_ref, out_ref):
    own = total_of(cut_rows(in_ref, pitch, s, 0, pitch) for s in range(pieces))
    for s in range(pieces):
        out_ref[pitch * s : pitch * (s + 1), :] = own


def suffix_kernel(sizes, mine_ref, in_ref, out_ref):
    planes, rows, base, height, pitch = sizes
    z, core = mine_ref[0], mine_ref[1]
    size = height - 2 * base
    early, late, shared, own = [], [], [], []
    for p in range(planes):
        first, second = (cut_rows(in_ref, height, p, base * c, base) for c in range(2))
        part = cut_rows(in_ref, height, p, 2 * base, size)
        both = jnp.where(p > z, first + second, 0.0)
        early.append(both + jnp.where(p == z, first + second, 0.0))
        late.append(both + jnp.where(p == z, second, 0.0))
        shared.append(jnp.where(p >= z, part, 0.0))
        own.append(jnp.where(p + core > z, part, 0.0))
    message = jnp.concatenate(
        [total_of(early), total_of(late), total_of(shared), total_of(own)], axis=0
    )
    for s in range(rows):
        out_ref[pitch * s : pitch * (s + 1), :] = message


def to_columns_kernel(sizes, in_ref, out_ref):
    chips, rows, base, pitch = sizes
    size = (pitch - 2 * base) // 2
    height = rows * base + size
    for c in range(2):
        parts = [cut_rows(in_ref, pitch, y, base * c, base) for y in range(rows)]
        parts.append(
            total_of(cut_rows(in_ref, pitch, y, 2 * base + size * c, size) for y in range(rows))
        )
        message = jnp.concatenate(parts, axis=0)
        for x in range(chips):
            at = height * (chips * c + x)
            out_ref[at : at + height, :] = message


def denominators(q_ref, total, padded):
    den = None
    for t in tiles(q_ref.shape[0]):
        spot = on_own_head(t, jnp.broadcast_to(total[t.j : t.j + 1, : t.width], (padded, t.width)))
        term = dot(jnp.concatenate(thirds(spot), axis=0), relu(q_ref[t.here, :]))
        den = term if den is None else den + term
    return den[:padded] + den[padded : 2 * padded] + den[2 * padded :] + 1.0


def gradient_states(slabs, q_ref, g_ref, rec, out_ref, hi_ref, lo_ref):
    channels = q_ref.shape[0]
    for h in range(channels // HEAD_DIM):
        hi, lo = halves(g_ref[of_head(h), :].astype(F32) * rec[h : h + 1])
        hi_ref[of_head(h), :], lo_ref[of_head(h), :] = hi, lo
    for t in tiles(channels):
        rhs = relu(q_ref[t.here, :])
        both = dot_rows(hi_ref[t.pair, :], rhs) + dot_rows(lo_ref[t.pair, :], rhs)
        slabs.put(out_ref, t, heads_apart(t, both))


def prefix(planes, pitch, base, mine_ref, in_ref):
    z, core = mine_ref[0], mine_ref[1]
    size = (pitch - 2 * base) // 2
    early, late, own = [], [], []
    for p in range(planes):
        first, second = (cut_rows(in_ref, pitch, p, base * c, base) for c in range(2))
        low, high = (cut_rows(in_ref, pitch, p, 2 * base + size * c, size) for c in range(2))
        both = jnp.where(p < z, first + second, 0.0)
        early.append(both + jnp.where(p == z, first, 0.0))
        late.append(both + jnp.where(p == z, first + second, 0.0))
        own.append(jnp.where(p <= z, low, 0.0) + jnp.where(p < z + core, high, 0.0))
    return total_of(early), total_of(late), total_of(own)


def denominator_kernel(planes, pitch, slabs, mine_ref, in_ref, q_ref, g_ref, out_ref, rec_ref, total_ref, hi_ref, lo_ref):
    out_ref[...] = jnp.zeros_like(out_ref)
    early, late, total = prefix(planes, pitch, slabs.base, mine_ref, in_ref)
    total_ref[...] = total
    rec = 1.0 / denominators(q_ref, total, rec_ref.shape[0])
    rec_ref[...] = rec
    gradient_states(slabs, q_ref, g_ref, rec, out_ref, hi_ref, lo_ref)
    pieces = out_ref.shape[0] // slabs.pitch
    for s in range(pieces):
        at = slabs.pitch * s
        out_ref[at : at + slabs.base, :] = early if 2 * s < pieces else late


def attention(slabs, in_ref, q_ref, g_ref, rec, mixed_ref, sums_ref, gt_ref, flat_ref):
    channels = q_ref.shape[0]
    padded = rec.shape[0]
    for t in tiles(channels):
        flat_ref[:, t.here] = slabs.get(in_ref, t)
    sums_ref[...] = jnp.zeros_like(sums_ref)
    gt_ref[...] = jnp.zeros_like(gt_ref)
    for h in range(channels // HEAD_DIM):
        attn = by_state(flat_ref, q_ref, h) * rec[h : h + 1]
        mixed_ref[of_head(h), :] = attn.astype(BF16)
        sums_ref[h : h + 1, :] = jnp.sum(g_ref[of_head(h), :].astype(F32) * attn, axis=0, keepdims=True)
    pair = jnp.concatenate(halves(-sums_ref[...] * rec), axis=0)
    for t in tiles(channels):
        term = dot_rows(pair, relu(q_ref[t.here, :]))
        term = on_own_head(t, term[:padded] + term[padded:])
        gt_ref[t.j : t.j + 1, : t.width] = jnp.sum(term, axis=0, keepdims=True)


def attention_kernel(planes, slabs, in_ref, q_ref, g_ref, rec_ref, out_ref, mixed_ref, sums_ref, flat_ref, gt_ref):
    attention(slabs, in_ref, q_ref, g_ref, rec_ref[...], mixed_ref, sums_ref, gt_ref, flat_ref)
    size = SLAB * slabs.each
    half = in_ref.shape[0] // slabs.pitch // 2
    sums = [
        total_of(cut_rows(in_ref, slabs.pitch, half * c + s, size, size) for s in range(half))
        for c in range(2)
    ]
    message = jnp.concatenate([*sums, gt_ref[...]], axis=0)
    height = len(message)
    for p in range(planes):
        out_ref[height * p : height * (p + 1), :] = message


def queries_kernel(slabs, in_ref, q_ref, g_ref, rec_ref, sums_ref, total_ref, out_ref, hi_ref, lo_ref):
    channels, rows = q_ref.shape
    for t in tiles(channels):
        shape = (LANES - HEAD_DIM, t.width)
        extra = jnp.where(row(shape) < 2, jnp.broadcast_to(total_ref[t.j : t.j + 1, : t.width], shape), 0.0)
        turn(t, slabs.get(in_ref, t), extra, hi_ref, lo_ref)
    for h in range(channels // HEAD_DIM):
        hi, lo = halves(-sums_ref[h : h + 1, :])
        shape = (LANES - HEAD_DIM, rows)
        rest = jnp.where(row(shape) == 0, jnp.broadcast_to(hi.astype(F32), shape), 0.0)
        rest = jnp.where(row(shape) == 1, jnp.broadcast_to(lo.astype(F32), shape), rest)
        rhs = with_rows(g_ref[of_head(h), :], rest)
        feature = (dot(hi_ref[of_head(h), :], rhs) + dot(lo_ref[of_head(h), :], rhs)) * rec_ref[h : h + 1, :]
        q = q_ref[of_head(h), :].astype(F32)
        out_ref[of_head(h), :] = jnp.where(q > 0, feature, 0.0).astype(BF16)


def keys(slabs, in_ref, total, k_ref, v_ref, gk_ref, gv_ref, flat_ref, hi_ref, lo_ref):
    channels, rows = k_ref.shape
    for t in tiles(channels):
        shape = (LANES - HEAD_DIM, t.width)
        extra = jnp.where(row(shape) < 1, jnp.broadcast_to(total[t.j : t.j + 1, : t.width], shape), 0.0)
        state = slabs.get(in_ref, t)
        flat_ref[:, t.here] = state
        turn(t, state, extra, hi_ref, lo_ref)
    ones = jnp.ones((LANES - HEAD_DIM, rows), BF16)
    for h in range(channels // HEAD_DIM):
        gv_ref[of_head(h), :] = by_state(flat_ref, k_ref, h).astype(BF16)
        rhs = with_rows(v_ref[of_head(h), :], ones)
        grad = dot(hi_ref[of_head(h), :], rhs) + dot(lo_ref[of_head(h), :], rhs)
        k = k_ref[of_head(h), :].astype(F32)
        gk_ref[of_head(h), :] = jnp.where(k > 0, grad, 0.0).astype(BF16)


def keys_kernel(slabs, in_ref, k_ref, v_ref, gk_ref, gv_ref, flat_ref, hi_ref, lo_ref):
    base = SLAB * slabs.each
    pieces = in_ref.shape[0] // slabs.pitch
    total = total_of(cut_rows(in_ref, slabs.pitch, s, base, slabs.pitch - base) for s in range(pieces))
    keys(slabs, in_ref, total, k_ref, v_ref, gk_ref, gv_ref, flat_ref, hi_ref, lo_ref)


def call(kernel, out, in_specs, scratch=(), flops=10**7, moved=10**6):
    shapes = [jax.ShapeDtypeStruct(s, d) for s, d in out]
    several = len(shapes) > 1
    return pl.pallas_call(
        kernel,
        out_shape=shapes if several else shapes[0],
        in_specs=in_specs,
        out_specs=[VMEM] * len(shapes) if several else VMEM,
        scratch_shapes=[pltpu.VMEM(s, d) for s, d in scratch],
        cost_estimate=pl.CostEstimate(flops=flops, bytes_accessed=moved, transcendentals=0),
        compiler_params=pltpu.CompilerParams(vmem_limit_bytes=24 * 2**20),
    )


def exchanged(message, axis):
    pieces = message.reshape(lax.axis_size(axis), -1)
    return lax.all_to_all(pieces, axis, 0, 0, tiled=True).reshape(message.shape)


CHIP, PLANE = ("core", "x"), ("core", "x", "y")


def body(queries, keys_in, values_in, grad_attn):
    q, k, v, g = (a[0].T for a in (queries, keys_in, values_in, grad_attn))
    channels, rows = q.shape
    nx, ny, nz = (lax.axis_size(a) for a in ("x", "y", "z"))
    mine = jnp.stack([lax.axis_index("z"), lax.axis_index("core")]).astype(jnp.int32)
    count = len(tiles(channels))
    each = -(-count * (HEAD_DIM // SLAB) // (2 * nx * ny))
    base = SLAB * each
    tall, pitch, short = ny * base + count, 2 * (base + count), 2 * base + count
    outer, middle = Slabs(tall, ny * each), Slabs(2 * base, each, base)
    got = Slabs(2 * base, each)
    flat, line = ((HEAD_DIM, channels), F32), ((count, LANES), F32)
    whole, small = ((channels, rows), BF16), ((16, rows), F32)

    def message(pieces, height):
        return ((pieces * height, LANES), F32)

    sent = call(
        functools.partial(states_kernel, outer, 2 * nx), [message(2 * nx, tall)], [VMEM] * 2, [line]
    )(k, v)
    sent = call(
        functools.partial(to_rows_kernel, (nx, ny, base, pitch)), [message(ny, pitch)], [VMEM]
    )(exchanged(sent, CHIP))
    sent = call(
        functools.partial(to_planes_kernel, nz, pitch), [message(nz, pitch)], [VMEM]
    )(exchanged(sent, "y"))
    sent, rec, total = call(
        functools.partial(denominator_kernel, nz, pitch, middle),
        [message(2 * nx * ny, 2 * base), small, line], [SMEM] + [VMEM] * 3, [whole, whole],
    )(mine, exchanged(sent, "z"), q, g)
    states = exchanged(sent, PLANE)
    sent, mixed, sums = call(
        functools.partial(attention_kernel, nz, got),
        [message(nz, short), whole, small], [VMEM] * 4, [flat, line],
    )(states, q, g, rec)
    sent = call(
        functools.partial(suffix_kernel, (nz, ny, base, short, pitch)),
        [message(ny, pitch)], [SMEM, VMEM],
    )(mine, exchanged(sent, "z"))
    sent = call(
        functools.partial(to_columns_kernel, (nx, ny, base, pitch)), [message(2 * nx, tall)], [VMEM]
    )(exchanged(sent, "y"))
    grad_queries = call(
        functools.partial(queries_kernel, got), [whole], [VMEM] * 6, [whole, whole]
    )(states, q, g, rec, sums, total)
    grad_keys, values_gradient = call(
        functools.partial(keys_kernel, outer), [whole] * 2, [VMEM] * 3, [flat, whole, whole]
    )(exchanged(sent, CHIP), k, v)
    return tuple(a.T[None] for a in (mixed, grad_queries, grad_keys, values_gradient))


def solution(mesh):
    groups, spaces = mesh.devices.shape
    split = Mesh(
        mesh.devices.reshape(groups // 2, 2, spaces // 8, 8), ("z", "core", "x", "y")
    )
    placed = P(("z", "core"), ("x", "y"), None)
    return jax.shard_map(
        body, mesh=split, in_specs=(placed,) * 4, out_specs=(placed,) * 4, check_vma=False
    )
```

```python
import functools

import jax
import jax.numpy as jnp
from jax import lax
from jax.experimental import pallas as pl
from jax.experimental.pallas import tpu as pltpu
from jax.sharding import Mesh
from jax.sharding import PartitionSpec as P

HEAD_DIM = 112
LANES = 128
SLAB = 8
F32, BF16 = jnp.float32, jnp.bfloat16
VMEM = pl.BlockSpec(memory_space=pltpu.VMEM)
SMEM = pl.BlockSpec(memory_space=pltpu.SMEM)
HBM = pl.BlockSpec(memory_space=pltpu.HBM)
NT = (((1,), (1,)), ((), ()))


class Tile:
    def __init__(self, j, channels):
        self.j, self.at = j, LANES * j
        self.width = min(LANES, channels - self.at)
        self.first = self.at // HEAD_DIM
        self.last = (self.at + self.width - 1) // HEAD_DIM
        self.here = slice(self.at, self.at + self.width)
        self.cut = min(self.width, HEAD_DIM * (self.first + 1) - self.at)
        self.pair = slice(HEAD_DIM * self.first, HEAD_DIM * (self.last + 1))


def tiles(channels):
    return [Tile(j, channels) for j in range(-(-channels // LANES))]


def dot(a, b):
    return jnp.dot(a, b, preferred_element_type=F32)


def dot_rows(a, b):
    return lax.dot_general(a, b, (((1,), (1,)), ((), ())), preferred_element_type=F32)


def halves(x):
    hi = x.astype(BF16)
    return hi, (x - hi.astype(F32)).astype(BF16)


def thirds(x):
    hi = x.astype(BF16)
    rest = x - hi.astype(F32)
    mid = rest.astype(BF16)
    return hi, mid, (rest - mid.astype(F32)).astype(BF16)


def relu(x):
    return jnp.maximum(x, jnp.zeros_like(x))


def lane(shape):
    return lax.broadcasted_iota(jnp.int32, shape, 1)


def row(shape):
    return lax.broadcasted_iota(jnp.int32, shape, 0)


def of_head(h):
    return slice(HEAD_DIM * h, HEAD_DIM * (h + 1))


def on_own_head(tile, x):
    heads = jnp.where(lane(x.shape) < tile.cut, tile.first, tile.last)
    return jnp.where(row(x.shape) == heads, x, 0.0)


def heads_apart(tile, both):
    if tile.first == tile.last:
        return both
    top, bottom = both[:HEAD_DIM], both[HEAD_DIM:]
    return jnp.where(lane(top.shape) < tile.cut, top, bottom)


class Slabs:
    def __init__(self, pitch, each, base=0):
        self.pitch, self.each, self.base = pitch, each, base

    def rows(self, tile):
        for i in range(HEAD_DIM // SLAB):
            number = HEAD_DIM // SLAB * tile.j + i
            at = self.pitch * (number // self.each) + self.base + SLAB * (number % self.each)
            yield slice(SLAB * i, SLAB * (i + 1)), slice(at, at + SLAB)

    def put(self, ref, tile, value):
        for here, there in self.rows(tile):
            ref[there, : tile.width] = value[here]

    def get(self, ref, tile):
        parts = [ref[there, : tile.width] for _, there in self.rows(tile)]
        return jnp.concatenate(parts, axis=0)


def by_state(flat_ref, rows_ref, h):
    channels = flat_ref.shape[1]
    start = HEAD_DIM * h // LANES * LANES
    stop = min(channels, -(-HEAD_DIM * (h + 1) // LANES) * LANES)
    s = flat_ref[:, start:stop]
    c = lane(s.shape) + start
    hi, lo = halves(jnp.where((c >= HEAD_DIM * h) & (c < HEAD_DIM * (h + 1)), s, 0.0))
    rhs = relu(rows_ref[start:stop, :])
    return dot(hi, rhs) + dot(lo, rhs)


def turn(tile, state, extra, hi_ref, lo_ref):
    hi, lo = halves(jnp.concatenate([state, extra], axis=0).T)
    hi_ref[tile.here, :], lo_ref[tile.here, :] = hi, lo


def with_rows(x, rest):
    return jnp.concatenate([x, rest.astype(BF16)], axis=0)


def states_kernel(slabs, pieces, *refs):
    loaded, (out_ref, *held, total_ref, sems) = refs[:4], refs[4:]
    copies = [pltpu.make_async_copy(a, b, sems.at[i]) for i, (a, b) in enumerate(zip(loaded, held))]
    for copy in copies:
        copy.start()
    k_ref, v_ref = held[:2]
    channels, rows = k_ref.shape
    total_ref[...] = jnp.zeros_like(total_ref)
    last = out_ref.shape[0] - slabs.pitch
    out_ref[last:, :] = jnp.zeros((slabs.pitch, LANES), F32)
    ones = jnp.ones((16, rows), BF16)
    copies[0].wait()
    for t in tiles(channels):
        total_ref[t.j : t.j + 1, : t.width] = dot_rows(ones, relu(k_ref[t.here, :]))[:1]
    total = total_ref[...]
    for s in range(pieces):
        at = slabs.pitch * s + SLAB * slabs.each
        out_ref[at : at + len(total), :] = total
    copies[1].wait()
    for t in tiles(channels):
        both = dot_rows(v_ref[t.pair, :], relu(k_ref[t.here, :]))
        slabs.put(out_ref, t, heads_apart(t, both))
    copies[2].wait()
    copies[3].wait()


def total_of(parts):
    parts = list(parts)
    out = parts[0]
    for part in parts[1:]:
        out = out + part
    return out


def cut_rows(ref, pitch, piece, start, size):
    at = pitch * piece + start
    return ref[at : at + size, :]


def to_rows_kernel(sizes, in_ref, out_ref):
    chips, rows, base, pitch = sizes
    height = in_ref.shape[0] // (2 * chips)
    sums = [
        total_of(cut_rows(in_ref, height, chips * c + x, 0, height) for x in range(chips))
        for c in range(2)
    ]
    totals = jnp.concatenate([s[rows * base :] for s in sums], axis=0)
    for y in range(rows):
        for c in range(2):
            at = pitch * y + base * c
            out_ref[at : at + base, :] = sums[c][base * y : base * (y + 1)]
        out_ref[pitch * y + 2 * base : pitch * (y + 1), :] = totals


def to_planes_kernel(sizes, in_ref, out_ref, own_ref):
    planes, base, pitch = sizes
    size = (pitch - 2 * base) // 2
    own = total_of(cut_rows(in_ref, pitch, s, 0, pitch) for s in range(in_ref.shape[0] // pitch))
    own_ref[...] = own
    first, second, low, high = own[:base], own[base : 2 * base], own[2 * base : -size], own[-size:]
    message = jnp.concatenate([first + second, low + high], axis=0)
    for p in range(planes):
        out_ref[len(message) * p : len(message) * (p + 1), :] = message


def suffix_kernel(sizes, mine_ref, in_ref, own_ref, out_ref):
    planes, rows, base = sizes
    z, core = mine_ref[0], mine_ref[1]
    height = in_ref.shape[0] // planes
    after = total_of(
        jnp.where(p > z, cut_rows(in_ref, height, p, 0, height), 0.0) for p in range(planes)
    )
    own = own_ref[...]
    first, second, part = own[:base], own[base : 2 * base], own[2 * base :]
    late = after[:base] + second
    beyond = after[base:]
    message = jnp.concatenate(
        [late + first, late, beyond + part, beyond + jnp.where(core > 0, part, 0.0)], axis=0
    )
    for s in range(rows):
        out_ref[len(message) * s : len(message) * (s + 1), :] = message


def to_columns_kernel(sizes, in_ref, out_ref):
    chips, rows, base, pitch = sizes
    size = (pitch - 2 * base) // 2
    height = rows * base + size
    for c in range(2):
        parts = [cut_rows(in_ref, pitch, y, base * c, base) for y in range(rows)]
        parts.append(
            total_of(cut_rows(in_ref, pitch, y, 2 * base + size * c, size) for y in range(rows))
        )
        message = jnp.concatenate(parts, axis=0)
        for x in range(chips):
            at = height * (chips * c + x)
            out_ref[at : at + height, :] = message


def denominators(q_ref, total, padded):
    den = None
    for t in tiles(q_ref.shape[0]):
        spot = on_own_head(t, jnp.broadcast_to(total[t.j : t.j + 1, : t.width], (padded, t.width)))
        term = dot(jnp.concatenate(thirds(spot), axis=0), relu(q_ref[t.here, :]))
        den = term if den is None else den + term
    return den[:padded] + den[padded : 2 * padded] + den[2 * padded :] + 1.0


def gradient_states(slabs, q_ref, g_ref, rec, out_ref, hi_ref, lo_ref):
    channels = q_ref.shape[0]
    for h in range(channels // HEAD_DIM):
        hi, lo = halves(g_ref[of_head(h), :].astype(F32) * rec[h : h + 1])
        hi_ref[of_head(h), :], lo_ref[of_head(h), :] = hi, lo
    for t in tiles(channels):
        rhs = relu(q_ref[t.here, :])
        both = dot_rows(hi_ref[t.pair, :], rhs) + dot_rows(lo_ref[t.pair, :], rhs)
        slabs.put(out_ref, t, heads_apart(t, both))


def prefix(planes, base, mine_ref, in_ref, own_ref):
    z, core = mine_ref[0], mine_ref[1]
    height = in_ref.shape[0] // planes
    before = total_of(
        jnp.where(p < z, cut_rows(in_ref, height, p, 0, height), 0.0) for p in range(planes)
    )
    own, size = own_ref[...], height - base
    early = before[:base] + own[:base]
    total = before[base:] + own[2 * base : -size] + jnp.where(core > 0, own[-size:], 0.0)
    return early, early + own[base : 2 * base], total


def denominator_kernel(planes, slabs, mine_ref, in_ref, own_ref, q_ref, g_ref, out_ref, rec_ref, total_ref, hi_ref, lo_ref):
    early, late, total = prefix(planes, slabs.base, mine_ref, in_ref, own_ref)
    total_ref[...] = total
    rec = 1.0 / denominators(q_ref, total, rec_ref.shape[0])
    rec_ref[...] = rec
    pieces = out_ref.shape[0] // slabs.pitch
    out_ref[slabs.pitch * (pieces - 1) :, :] = jnp.zeros((slabs.pitch, LANES), F32)
    gradient_states(slabs, q_ref, g_ref, rec, out_ref, hi_ref, lo_ref)
    for s in range(pieces):
        at = slabs.pitch * s
        out_ref[at : at + slabs.base, :] = early if 2 * s < pieces else late


def attention(slabs, in_ref, q_ref, g_ref, rec, mixed_ref, sums_ref, gt_ref, flat_ref):
    channels = q_ref.shape[0]
    padded = rec.shape[0]
    for t in tiles(channels):
        flat_ref[:, t.here] = slabs.get(in_ref, t)
    sums_ref[...] = jnp.zeros_like(sums_ref)
    gt_ref[...] = jnp.zeros_like(gt_ref)
    for h in range(channels // HEAD_DIM):
        attn = by_state(flat_ref, q_ref, h) * rec[h : h + 1]
        mixed_ref[of_head(h), :] = attn.astype(BF16)
        sums_ref[h : h + 1, :] = jnp.sum(g_ref[of_head(h), :].astype(F32) * attn, axis=0, keepdims=True)
    pair = jnp.concatenate(halves(-sums_ref[...] * rec), axis=0)
    for t in tiles(channels):
        term = dot_rows(pair, relu(q_ref[t.here, :]))
        term = on_own_head(t, term[:padded] + term[padded:])
        gt_ref[t.j : t.j + 1, : t.width] = jnp.sum(term, axis=0, keepdims=True)


def attention_kernel(planes, slabs, in_ref, q_ref, g_ref, rec_ref, out_ref, own_ref, mixed_ref, sums_ref, flat_ref, gt_ref):
    attention(slabs, in_ref, q_ref, g_ref, rec_ref[...], mixed_ref, sums_ref, gt_ref, flat_ref)
    size = SLAB * slabs.each
    half = in_ref.shape[0] // slabs.pitch // 2
    sums = [
        total_of(cut_rows(in_ref, slabs.pitch, half * c + s, size, size) for s in range(half))
        for c in range(2)
    ]
    part = gt_ref[...]
    own_ref[...] = jnp.concatenate([*sums, part], axis=0)
    message = jnp.concatenate([sums[0] + sums[1], part], axis=0)
    for p in range(planes):
        out_ref[len(message) * p : len(message) * (p + 1), :] = message


def queries_kernel(slabs, in_ref, q_ref, g_ref, rec_ref, sums_ref, total_ref, attn_ref, out_ref, mixed_ref, hi_ref, lo_ref):
    channels, rows = q_ref.shape
    mixed_ref[...] = attn_ref[...]
    for t in tiles(channels):
        shape = (LANES - HEAD_DIM, t.width)
        extra = jnp.where(row(shape) < 2, jnp.broadcast_to(total_ref[t.j : t.j + 1, : t.width], shape), 0.0)
        turn(t, slabs.get(in_ref, t), extra, hi_ref, lo_ref)
    for h in range(channels // HEAD_DIM):
        hi, lo = halves(-sums_ref[h : h + 1, :])
        shape = (LANES - HEAD_DIM, rows)
        rest = jnp.where(row(shape) == 0, jnp.broadcast_to(hi.astype(F32), shape), 0.0)
        rest = jnp.where(row(shape) == 1, jnp.broadcast_to(lo.astype(F32), shape), rest)
        rhs = with_rows(g_ref[of_head(h), :], rest)
        feature = (dot(hi_ref[of_head(h), :], rhs) + dot(lo_ref[of_head(h), :], rhs)) * rec_ref[h : h + 1, :]
        q = q_ref[of_head(h), :].astype(F32)
        out_ref[of_head(h), :] = jnp.where(q > 0, feature, 0.0).astype(BF16)


def keys(slabs, in_ref, total, k_ref, v_ref, gk_ref, gv_ref, flat_ref, hi_ref, lo_ref):
    channels, rows = k_ref.shape
    for t in tiles(channels):
        shape = (LANES - HEAD_DIM, t.width)
        extra = jnp.where(row(shape) < 1, jnp.broadcast_to(total[t.j : t.j + 1, : t.width], shape), 0.0)
        state = slabs.get(in_ref, t)
        flat_ref[:, t.here] = state
        turn(t, state, extra, hi_ref, lo_ref)
    ones = jnp.ones((LANES - HEAD_DIM, rows), BF16)
    for h in range(channels // HEAD_DIM):
        gv_ref[of_head(h), :] = by_state(flat_ref, k_ref, h).astype(BF16)
        rhs = with_rows(v_ref[of_head(h), :], ones)
        grad = dot(hi_ref[of_head(h), :], rhs) + dot(lo_ref[of_head(h), :], rhs)
        k = k_ref[of_head(h), :].astype(F32)
        gk_ref[of_head(h), :] = jnp.where(k > 0, grad, 0.0).astype(BF16)


def keys_kernel(slabs, in_ref, k_ref, v_ref, gk_ref, gv_ref, flat_ref, hi_ref, lo_ref):
    base = SLAB * slabs.each
    pieces = in_ref.shape[0] // slabs.pitch
    total = total_of(cut_rows(in_ref, slabs.pitch, s, base, slabs.pitch - base) for s in range(pieces))
    keys(slabs, in_ref, total, k_ref, v_ref, gk_ref, gv_ref, flat_ref, hi_ref, lo_ref)


def call(kernel, out, in_specs, scratch=(), more=(), flops=10**7, moved=10**6):
    shapes = [jax.ShapeDtypeStruct(s, d) for s, d in out]
    several = len(shapes) > 1
    return pl.pallas_call(
        kernel,
        out_shape=shapes if several else shapes[0],
        in_specs=in_specs,
        out_specs=[VMEM] * len(shapes) if several else VMEM,
        scratch_shapes=[pltpu.VMEM(s, d) for s, d in scratch] + list(more),
        cost_estimate=pl.CostEstimate(flops=flops, bytes_accessed=moved, transcendentals=0),
        compiler_params=pltpu.CompilerParams(vmem_limit_bytes=24 * 2**20),
    )


def exchanged(message, axis):
    pieces = message.reshape(lax.axis_size(axis), -1)
    return lax.all_to_all(pieces, axis, 0, 0, tiled=True).reshape(message.shape)


CHIP, PLANE = ("core", "x"), ("core", "x", "y")


def body(queries, keys_in, values_in, grad_attn):
    q, k, v, g = (a[0].T for a in (queries, keys_in, values_in, grad_attn))
    channels, rows = q.shape
    nx, ny, nz = (lax.axis_size(a) for a in ("x", "y", "z"))
    mine = jnp.stack([lax.axis_index("z"), lax.axis_index("core")]).astype(jnp.int32)
    count = len(tiles(channels))
    each = -(-count * (HEAD_DIM // SLAB) // (2 * nx * ny))
    base = SLAB * each
    tall, pitch, short = ny * base + count, 2 * (base + count), base + count
    outer, middle = Slabs(tall, ny * each), Slabs(2 * base, each, base)
    got = Slabs(2 * base, each)
    flat, line = ((HEAD_DIM, channels), F32), ((count, LANES), F32)
    whole, small = ((channels, rows), BF16), ((16, rows), F32)

    def message(pieces, height):
        return ((pieces * height, LANES), F32)

    sent, k, v, q, g = call(
        functools.partial(states_kernel, outer, 2 * nx),
        [message(2 * nx, tall)] + [whole] * 4, [HBM] * 4, [line], [pltpu.SemaphoreType.DMA((4,))],
    )(*(pltpu.with_memory_space_constraint(a, pltpu.HBM) for a in (k, v, q, g)))
    sent = call(
        functools.partial(to_rows_kernel, (nx, ny, base, pitch)), [message(ny, pitch)], [VMEM]
    )(exchanged(sent, CHIP))
    sent, own = call(
        functools.partial(to_planes_kernel, (nz, base, pitch)),
        [message(nz, short), message(1, pitch)], [VMEM],
    )(exchanged(sent, "y"))
    sent, rec, total = call(
        functools.partial(denominator_kernel, nz, middle),
        [message(2 * nx * ny, 2 * base), small, line], [SMEM] + [VMEM] * 4, [whole, whole],
    )(mine, exchanged(sent, "z"), own, q, g)
    states = exchanged(sent, PLANE)
    sent, own, attn, sums = call(
        functools.partial(attention_kernel, nz, got),
        [message(nz, short), message(1, base + short), whole, small], [VMEM] * 4, [flat, line],
    )(states, q, g, rec)
    grad_queries, mixed = call(
        functools.partial(queries_kernel, got), [whole] * 2, [VMEM] * 7, [whole, whole]
    )(states, q, g, rec, sums, total, attn)
    sent, grad_queries = lax.optimization_barrier((exchanged(sent, "z"), grad_queries))
    sent = call(
        functools.partial(suffix_kernel, (nz, ny, base)), [message(ny, pitch)], [SMEM, VMEM, VMEM]
    )(mine, sent, own)
    sent = call(
        functools.partial(to_columns_kernel, (nx, ny, base, pitch)), [message(2 * nx, tall)], [VMEM]
    )(exchanged(sent, "y"))
    grad_keys, values_gradient = call(
        functools.partial(keys_kernel, outer), [whole] * 2, [VMEM] * 3, [flat, whole, whole]
    )(exchanged(sent, CHIP), k, v)
    return tuple(a.T[None] for a in (mixed, grad_queries, grad_keys, values_gradient))


def solution(mesh):
    groups, spaces = mesh.devices.shape
    split = Mesh(
        mesh.devices.reshape(groups // 2, 2, spaces // 8, 8), ("z", "core", "x", "y")
    )
    placed = P(("z", "core"), ("x", "y"), None)
    return jax.shard_map(
        body, mesh=split, in_specs=(placed,) * 4, out_specs=(placed,) * 4, check_vma=False
    )
```

```python
import functools

import jax
import jax.numpy as jnp
import numpy as np
from jax import lax
from jax.experimental import pallas as pl
from jax.experimental.pallas import tpu as pltpu
from jax.sharding import Mesh
from jax.sharding import PartitionSpec as P

PLANES = (0, 1, 7, 2, 6, 3, 5, 4)
ROWS = (0, 4, 2, 6, 1, 5, 3, 7)
CHIP = tuple((n % 2, n // 2) for n in (1, 6, 5, 4, 7, 0, 2, 3))
PLANE = tuple((c, x, y) for c in range(2) for y in PLANES for x in (0, 1, 3, 2))

HEAD_DIM = 112
LANES = 128
SLAB = 8
F32, BF16 = jnp.float32, jnp.bfloat16
VMEM = pl.BlockSpec(memory_space=pltpu.VMEM)
HBM = pl.BlockSpec(memory_space=pltpu.HBM)
NT = (((1,), (1,)), ((), ()))


class Tile:
    def __init__(self, j, channels):
        self.j, self.at = j, LANES * j
        self.width = min(LANES, channels - self.at)
        self.first = self.at // HEAD_DIM
        self.last = (self.at + self.width - 1) // HEAD_DIM
        self.here = slice(self.at, self.at + self.width)
        self.cut = min(self.width, HEAD_DIM * (self.first + 1) - self.at)
        self.pair = slice(HEAD_DIM * self.first, HEAD_DIM * (self.last + 1))


def tiles(channels):
    return [Tile(j, channels) for j in range(-(-channels // LANES))]


def dot(a, b):
    return jnp.dot(a, b, preferred_element_type=F32)


def dot_rows(a, b):
    return lax.dot_general(a, b, (((1,), (1,)), ((), ())), preferred_element_type=F32)


def both_halves(by, hi, lo, rhs):
    out = by(jnp.concatenate([hi, lo], axis=0), rhs)
    return out[: len(hi)] + out[len(hi) :]


def halves(x):
    hi = x.astype(BF16)
    return hi, (x - hi.astype(F32)).astype(BF16)


def thirds(x):
    hi = x.astype(BF16)
    rest = x - hi.astype(F32)
    mid = rest.astype(BF16)
    return hi, mid, (rest - mid.astype(F32)).astype(BF16)


def relu(x):
    return jnp.maximum(x, jnp.zeros_like(x))


def lane(shape):
    return lax.broadcasted_iota(jnp.int32, shape, 1)


def row(shape):
    return lax.broadcasted_iota(jnp.int32, shape, 0)


def of_head(h):
    return slice(HEAD_DIM * h, HEAD_DIM * (h + 1))


def on_own_head(tile, x):
    heads = jnp.where(lane(x.shape) < tile.cut, tile.first, tile.last)
    return jnp.where(row(x.shape) == heads, x, 0.0)


def heads_apart(tile, both):
    if tile.first == tile.last:
        return both
    top, bottom = both[:HEAD_DIM], both[HEAD_DIM:]
    return jnp.where(lane(top.shape) < tile.cut, top, bottom)


class Slabs:
    def __init__(self, pitch, each, base=0, places=None):
        self.pitch, self.each, self.base, self.places = pitch, each, base, places

    def rows(self, tile):
        for i in range(HEAD_DIM // SLAB):
            number = HEAD_DIM // SLAB * tile.j + i
            piece = number // self.each
            piece = piece if self.places is None else self.places[piece]
            at = self.pitch * piece + self.base + SLAB * (number % self.each)
            yield slice(SLAB * i, SLAB * (i + 1)), slice(at, at + SLAB)

    def put(self, ref, tile, value):
        for here, there in self.rows(tile):
            ref[there, : tile.width] = value[here]

    def get(self, ref, tile):
        parts = [ref[there, : tile.width] for _, there in self.rows(tile)]
        return jnp.concatenate(parts, axis=0)


def by_state(flat_ref, rows_ref, h):
    channels = flat_ref.shape[1]
    start = HEAD_DIM * h // LANES * LANES
    stop = min(channels, -(-HEAD_DIM * (h + 1) // LANES) * LANES)
    s = flat_ref[:, start:stop]
    c = lane(s.shape) + start
    hi, lo = halves(jnp.where((c >= HEAD_DIM * h) & (c < HEAD_DIM * (h + 1)), s, 0.0))
    return both_halves(dot, hi, lo, relu(rows_ref[start:stop, :]))


def turn(tile, state, extra, hi_ref, lo_ref):
    hi, lo = halves(jnp.concatenate([state, extra], axis=0).T)
    hi_ref[tile.here, :], lo_ref[tile.here, :] = hi, lo


def with_rows(x, rest):
    return jnp.concatenate([x, rest.astype(BF16)], axis=0)


def states_kernel(slabs, pieces, *refs):
    loaded, (out_ref, *held, total_ref, sems) = refs[:4], refs[4:]
    copies = [pltpu.make_async_copy(a, b, sems.at[i]) for i, (a, b) in enumerate(zip(loaded, held))]
    copies[0].start()
    copies[1].start()
    k_ref, v_ref = held[:2]
    channels, rows = k_ref.shape
    total_ref[...] = jnp.zeros_like(total_ref)
    last = out_ref.shape[0] - slabs.pitch
    out_ref[last:, :] = jnp.zeros((slabs.pitch, LANES), F32)
    ones = jnp.ones((16, rows), BF16)
    copies[0].wait()
    copies[2].start()
    copies[3].start()
    for t in tiles(channels):
        total_ref[t.j : t.j + 1, : t.width] = dot_rows(ones, relu(k_ref[t.here, :]))[:1]
    total = total_ref[...]
    for s in range(pieces):
        at = slabs.pitch * s + SLAB * slabs.each
        out_ref[at : at + len(total), :] = total
    copies[1].wait()
    for t in tiles(channels):
        both = dot_rows(v_ref[t.pair, :], relu(k_ref[t.here, :]))
        slabs.put(out_ref, t, heads_apart(t, both))
    copies[2].wait()
    copies[3].wait()


def total_of(parts):
    parts = list(parts)
    out = parts[0]
    for part in parts[1:]:
        out = out + part
    return out


def cut_rows(ref, pitch, piece, start, size):
    at = pitch * piece + start
    return ref[at : at + size, :]


def to_rows_kernel(sizes, in_ref, out_ref):
    rows, base, pitch = sizes
    height = in_ref.shape[0] // len(CHIP)
    sums = [
        total_of(cut_rows(in_ref, height, s, 0, height) for s, d in enumerate(CHIP) if d[0] == c)
        for c in range(2)
    ]
    totals = jnp.concatenate([s[rows * base :] for s in sums], axis=0)
    for y in range(rows):
        for c in range(2):
            at = pitch * y + base * c
            out_ref[at : at + base, :] = sums[c][base * y : base * (y + 1)]
        out_ref[pitch * y + 2 * base : pitch * (y + 1), :] = totals


def to_planes_kernel(sizes, in_ref, out_ref, own_ref):
    planes, base, pitch = sizes
    size = (pitch - 2 * base) // 2
    own = total_of(cut_rows(in_ref, pitch, s, 0, pitch) for s in range(in_ref.shape[0] // pitch))
    own_ref[...] = own
    first, second, low, high = own[:base], own[base : 2 * base], own[2 * base : -size], own[-size:]
    message = jnp.concatenate([first + second, low + high], axis=0)
    for p in range(planes):
        out_ref[len(message) * p : len(message) * (p + 1), :] = message


def suffix_kernel(rows, base, in_ref, own_ref, out_ref):
    z, core = lax.axis_index("z"), lax.axis_index("core")
    height = in_ref.shape[0] // len(PLANES)
    after = total_of(
        jnp.where(p > z, cut_rows(in_ref, height, s, 0, height), 0.0) for s, p in enumerate(PLANES)
    )
    own = own_ref[...]
    first, second, part = own[:base], own[base : 2 * base], own[2 * base :]
    late = after[:base] + second
    beyond = after[base:]
    message = jnp.concatenate(
        [late + first, late, beyond + part, beyond + jnp.where(core > 0, part, 0.0)], axis=0
    )
    for s in range(rows):
        out_ref[len(message) * s : len(message) * (s + 1), :] = message


def to_columns_kernel(sizes, in_ref, out_ref):
    rows, base, pitch = sizes
    size = (pitch - 2 * base) // 2
    height = rows * base + size
    for c in range(2):
        parts = [cut_rows(in_ref, pitch, y, base * c, base) for y in range(rows)]
        parts.append(
            total_of(cut_rows(in_ref, pitch, y, 2 * base + size * c, size) for y in range(rows))
        )
        message = jnp.concatenate(parts, axis=0)
        for s, d in enumerate(CHIP):
            if d[0] == c:
                out_ref[height * s : height * (s + 1), :] = message


def denominators(q_ref, total, padded):
    den = None
    for t in tiles(q_ref.shape[0]):
        spot = on_own_head(t, jnp.broadcast_to(total[t.j : t.j + 1, : t.width], (padded, t.width)))
        term = dot(jnp.concatenate(thirds(spot), axis=0), relu(q_ref[t.here, :]))
        den = term if den is None else den + term
    return den[:padded] + den[padded : 2 * padded] + den[2 * padded :] + 1.0


def gradient_states(slabs, q_ref, g_ref, rec, out_ref, hi_ref, lo_ref):
    channels = q_ref.shape[0]
    for h in range(channels // HEAD_DIM):
        hi, lo = halves(g_ref[of_head(h), :].astype(F32) * rec[h : h + 1])
        hi_ref[of_head(h), :], lo_ref[of_head(h), :] = hi, lo
    for t in tiles(channels):
        rhs = relu(q_ref[t.here, :])
        both = both_halves(dot_rows, hi_ref[t.pair, :], lo_ref[t.pair, :], rhs)
        slabs.put(out_ref, t, heads_apart(t, both))


def prefix(base, in_ref, own_ref):
    z, core = lax.axis_index("z"), lax.axis_index("core")
    height = in_ref.shape[0] // len(PLANES)
    before = total_of(
        jnp.where(p < z, cut_rows(in_ref, height, s, 0, height), 0.0) for s, p in enumerate(PLANES)
    )
    own, size = own_ref[...], height - base
    early = before[:base] + own[:base]
    total = before[base:] + own[2 * base : -size] + jnp.where(core > 0, own[-size:], 0.0)
    return early, early + own[base : 2 * base], total


def denominator_kernel(slabs, in_ref, own_ref, q_ref, g_ref, out_ref, rec_ref, total_ref, hi_ref, lo_ref):
    early, late, total = prefix(slabs.base, in_ref, own_ref)
    total_ref[...] = total
    rec = 1.0 / denominators(q_ref, total, rec_ref.shape[0])
    rec_ref[...] = rec
    pieces = out_ref.shape[0] // slabs.pitch
    spare = slabs.pitch * slabs.places[pieces - 1]
    out_ref[spare : spare + slabs.pitch, :] = jnp.zeros((slabs.pitch, LANES), F32)
    gradient_states(slabs, q_ref, g_ref, rec, out_ref, hi_ref, lo_ref)
    for s in range(pieces):
        at = slabs.pitch * s
        out_ref[at : at + slabs.base, :] = late if PLANE[s][0] else early


def attention(slabs, in_ref, q_ref, g_ref, rec, mixed_ref, sums_ref, gt_ref, flat_ref):
    channels = q_ref.shape[0]
    padded = rec.shape[0]
    for t in tiles(channels):
        flat_ref[:, t.here] = slabs.get(in_ref, t)
    sums_ref[...] = jnp.zeros_like(sums_ref)
    gt_ref[...] = jnp.zeros_like(gt_ref)
    for h in range(channels // HEAD_DIM):
        attn = by_state(flat_ref, q_ref, h) * rec[h : h + 1]
        mixed_ref[of_head(h), :] = attn.astype(BF16)
        sums_ref[h : h + 1, :] = jnp.sum(g_ref[of_head(h), :].astype(F32) * attn, axis=0, keepdims=True)
    pair = jnp.concatenate(halves(-sums_ref[...] * rec), axis=0)
    for t in tiles(channels):
        term = dot_rows(pair, relu(q_ref[t.here, :]))
        term = on_own_head(t, term[:padded] + term[padded:])
        gt_ref[t.j : t.j + 1, : t.width] = jnp.sum(term, axis=0, keepdims=True)


def attention_kernel(planes, slabs, in_ref, q_ref, g_ref, rec_ref, out_ref, own_ref, mixed_ref, sums_ref, flat_ref, gt_ref):
    attention(slabs, in_ref, q_ref, g_ref, rec_ref[...], mixed_ref, sums_ref, gt_ref, flat_ref)
    size = SLAB * slabs.each
    sums = [
        total_of(cut_rows(in_ref, slabs.pitch, s, size, size) for s, d in enumerate(PLANE) if d[0] == c)
        for c in range(2)
    ]
    part = gt_ref[...]
    own_ref[...] = jnp.concatenate([*sums, part], axis=0)
    message = jnp.concatenate([sums[0] + sums[1], part], axis=0)
    for p in range(planes):
        out_ref[len(message) * p : len(message) * (p + 1), :] = message


def queries_kernel(slabs, in_ref, q_ref, g_ref, rec_ref, sums_ref, total_ref, attn_ref, out_ref, mixed_ref, hi_ref, lo_ref):
    channels, rows = q_ref.shape
    mixed_ref[...] = attn_ref[...]
    for t in tiles(channels):
        shape = (LANES - HEAD_DIM, t.width)
        extra = jnp.where(row(shape) < 2, jnp.broadcast_to(total_ref[t.j : t.j + 1, : t.width], shape), 0.0)
        turn(t, slabs.get(in_ref, t), extra, hi_ref, lo_ref)
    for h in range(channels // HEAD_DIM):
        hi, lo = halves(-sums_ref[h : h + 1, :])
        shape = (LANES - HEAD_DIM, rows)
        rest = jnp.where(row(shape) == 0, jnp.broadcast_to(hi.astype(F32), shape), 0.0)
        rest = jnp.where(row(shape) == 1, jnp.broadcast_to(lo.astype(F32), shape), rest)
        rhs = with_rows(g_ref[of_head(h), :], rest)
        feature = both_halves(dot, hi_ref[of_head(h), :], lo_ref[of_head(h), :], rhs) * rec_ref[h : h + 1, :]
        q = q_ref[of_head(h), :].astype(F32)
        out_ref[of_head(h), :] = jnp.where(q > 0, feature, 0.0).astype(BF16)


def keys(slabs, in_ref, total, k_ref, v_ref, gk_ref, gv_ref, flat_ref, hi_ref, lo_ref):
    channels, rows = k_ref.shape
    for t in tiles(channels):
        shape = (LANES - HEAD_DIM, t.width)
        extra = jnp.where(row(shape) < 1, jnp.broadcast_to(total[t.j : t.j + 1, : t.width], shape), 0.0)
        state = slabs.get(in_ref, t)
        flat_ref[:, t.here] = state
        turn(t, state, extra, hi_ref, lo_ref)
    ones = jnp.ones((LANES - HEAD_DIM, rows), BF16)
    for h in range(channels // HEAD_DIM):
        gv_ref[of_head(h), :] = by_state(flat_ref, k_ref, h).astype(BF16)
        rhs = with_rows(v_ref[of_head(h), :], ones)
        grad = both_halves(dot, hi_ref[of_head(h), :], lo_ref[of_head(h), :], rhs)
        k = k_ref[of_head(h), :].astype(F32)
        gk_ref[of_head(h), :] = jnp.where(k > 0, grad, 0.0).astype(BF16)


def keys_kernel(slabs, in_ref, k_ref, v_ref, gk_ref, gv_ref, flat_ref, hi_ref, lo_ref):
    base = SLAB * slabs.each
    pieces = in_ref.shape[0] // slabs.pitch
    total = total_of(cut_rows(in_ref, slabs.pitch, s, base, slabs.pitch - base) for s in range(pieces))
    keys(slabs, in_ref, total, k_ref, v_ref, gk_ref, gv_ref, flat_ref, hi_ref, lo_ref)


def call(kernel, out, in_specs, scratch=(), more=(), flops=10**7, moved=10**6):
    shapes = [jax.ShapeDtypeStruct(s, d) for s, d in out]
    several = len(shapes) > 1
    return pl.pallas_call(
        kernel,
        out_shape=shapes if several else shapes[0],
        in_specs=in_specs,
        out_specs=[VMEM] * len(shapes) if several else VMEM,
        scratch_shapes=[pltpu.VMEM(s, d) for s, d in scratch] + list(more),
        cost_estimate=pl.CostEstimate(flops=flops, bytes_accessed=moved, transcendentals=0),
        compiler_params=pltpu.CompilerParams(vmem_limit_bytes=24 * 2**20),
    )


def exchanged(message, axes, order):
    sizes = [lax.axis_size(a) for a in axes]
    order = [int(np.ravel_multi_index(d, sizes)) for d in order]
    pieces = message.reshape(len(order), -1)
    pieces = lax.all_to_all(pieces, axes, 0, 0, tiled=True, axis_index_groups=[order])
    return pieces.reshape(message.shape)


def over_chips(message):
    return exchanged(message, ("core", "x"), CHIP)


def over_rows(message):
    return exchanged(message, ("y",), [(y,) for y in ROWS])


def over_planes(message):
    return exchanged(message, ("z",), [(z,) for z in PLANES])


def body(queries, keys_in, values_in, grad_attn):
    q, k, v, g = (a[0].T for a in (queries, keys_in, values_in, grad_attn))
    channels, rows = q.shape
    nx, ny, nz = (lax.axis_size(a) for a in ("x", "y", "z"))
    count = len(tiles(channels))
    each = -(-count * (HEAD_DIM // SLAB) // (2 * nx * ny))
    base = SLAB * each
    tall, pitch, short = ny * base + count, 2 * (base + count), base + count
    places = [PLANE.index((*chip, y)) for chip in CHIP for y in ROWS]
    outer, middle = Slabs(tall, ny * each), Slabs(2 * base, each, base, places)
    got = Slabs(2 * base, each, 0, places)
    flat, line = ((HEAD_DIM, channels), F32), ((count, LANES), F32)
    whole, small = ((channels, rows), BF16), ((16, rows), F32)

    def message(pieces, height):
        return ((pieces * height, LANES), F32)

    sent, k, v, q, g = call(
        functools.partial(states_kernel, outer, 2 * nx),
        [message(2 * nx, tall)] + [whole] * 4, [HBM] * 4, [line], [pltpu.SemaphoreType.DMA((4,))],
    )(*(pltpu.with_memory_space_constraint(a, pltpu.HBM) for a in (k, v, q, g)))
    sent = call(
        functools.partial(to_rows_kernel, (ny, base, pitch)), [message(ny, pitch)], [VMEM]
    )(over_chips(sent))
    sent, own = call(
        functools.partial(to_planes_kernel, (nz, base, pitch)),
        [message(nz, short), message(1, pitch)], [VMEM],
    )(over_rows(sent))
    sent, rec, total = call(
        functools.partial(denominator_kernel, middle),
        [message(2 * nx * ny, 2 * base), small, line], [VMEM] * 4, [whole, whole],
    )(over_planes(sent), own, q, g)
    states = exchanged(sent, ("core", "x", "y"), PLANE)
    sent, own, attn, sums = call(
        functools.partial(attention_kernel, nz, got),
        [message(nz, short), message(1, base + short), whole, small], [VMEM] * 4, [flat, line],
    )(states, q, g, rec)
    grad_queries, mixed = call(
        functools.partial(queries_kernel, got), [whole] * 2, [VMEM] * 7, [whole, whole]
    )(states, q, g, rec, sums, total, attn)
    sent, grad_queries = lax.optimization_barrier((over_planes(sent), grad_queries))
    sent = call(
        functools.partial(suffix_kernel, ny, base), [message(ny, pitch)], [VMEM] * 2
    )(sent, own)
    sent = call(
        functools.partial(to_columns_kernel, (ny, base, pitch)), [message(2 * nx, tall)], [VMEM]
    )(over_rows(sent))
    grad_keys, values_gradient = call(
        functools.partial(keys_kernel, outer), [whole] * 2, [VMEM] * 3, [flat, whole, whole]
    )(over_chips(sent), k, v)
    return tuple(a.T[None] for a in (mixed, grad_queries, grad_keys, values_gradient))


def solution(mesh):
    groups, spaces = mesh.devices.shape
    split = Mesh(
        mesh.devices.reshape(groups // 2, 2, spaces // 8, 8), ("z", "core", "x", "y")
    )
    placed = P(("z", "core"), ("x", "y"), None)
    return jax.shard_map(
        body, mesh=split, in_specs=(placed,) * 4, out_specs=(placed,) * 4, check_vma=False
    )
```

```python
import functools

import jax
import jax.numpy as jnp
import numpy as np
from jax import lax
from jax.experimental import pallas as pl
from jax.experimental.pallas import tpu as pltpu
from jax.sharding import Mesh
from jax.sharding import PartitionSpec as P

PLANES = (0, 1, 7, 2, 6, 3, 5, 4)
ROWS = (0, 4, 2, 6, 1, 5, 3, 7)
CHIP = tuple((n % 2, n // 2) for n in (1, 6, 5, 4, 7, 0, 2, 3))
PLANE = tuple((c, x, y) for c in range(2) for y in PLANES for x in (0, 1, 3, 2))

HEAD_DIM = 112
LANES = 128
SLAB = 8
F32, BF16 = jnp.float32, jnp.bfloat16
VMEM = pl.BlockSpec(memory_space=pltpu.VMEM)
HBM = pl.BlockSpec(memory_space=pltpu.HBM)
NT = (((1,), (1,)), ((), ()))


class Tile:
    def __init__(self, j, channels):
        self.j, self.at = j, LANES * j
        self.width = min(LANES, channels - self.at)
        self.first = self.at // HEAD_DIM
        self.last = (self.at + self.width - 1) // HEAD_DIM
        self.here = slice(self.at, self.at + self.width)
        self.cut = min(self.width, HEAD_DIM * (self.first + 1) - self.at)
        self.pair = slice(HEAD_DIM * self.first, HEAD_DIM * (self.last + 1))


def tiles(channels):
    return [Tile(j, channels) for j in range(-(-channels // LANES))]


def dot(a, b):
    return jnp.dot(a, b, preferred_element_type=F32)


def dot_rows(a, b):
    return lax.dot_general(a, b, (((1,), (1,)), ((), ())), preferred_element_type=F32)


def both_halves(by, hi, lo, rhs):
    out = by(jnp.concatenate([hi, lo], axis=0), rhs)
    return out[: len(hi)] + out[len(hi) :]


def halves(x):
    hi = x.astype(BF16)
    return hi, (x - hi.astype(F32)).astype(BF16)


def thirds(x):
    hi = x.astype(BF16)
    rest = x - hi.astype(F32)
    mid = rest.astype(BF16)
    return hi, mid, (rest - mid.astype(F32)).astype(BF16)


def relu(x):
    return jnp.maximum(x, jnp.zeros_like(x))


def lane(shape):
    return lax.broadcasted_iota(jnp.int32, shape, 1)


def row(shape):
    return lax.broadcasted_iota(jnp.int32, shape, 0)


def of_head(h):
    return slice(HEAD_DIM * h, HEAD_DIM * (h + 1))


def on_own_head(tile, x):
    heads = jnp.where(lane(x.shape) < tile.cut, tile.first, tile.last)
    return jnp.where(row(x.shape) == heads, x, 0.0)


def heads_apart(tile, both):
    if tile.first == tile.last:
        return both
    top, bottom = both[:HEAD_DIM], both[HEAD_DIM:]
    return jnp.where(lane(top.shape) < tile.cut, top, bottom)


class Slabs:
    def __init__(self, pitch, each, base=0, places=None):
        self.pitch, self.each, self.base, self.places = pitch, each, base, places

    def rows(self, tile):
        for i in range(HEAD_DIM // SLAB):
            number = HEAD_DIM // SLAB * tile.j + i
            piece = number // self.each
            piece = piece if self.places is None else self.places[piece]
            at = self.pitch * piece + self.base + SLAB * (number % self.each)
            yield slice(SLAB * i, SLAB * (i + 1)), slice(at, at + SLAB)

    def put(self, ref, tile, value):
        for here, there in self.rows(tile):
            ref[there, : tile.width] = value[here]

    def get(self, ref, tile):
        parts = [ref[there, : tile.width] for _, there in self.rows(tile)]
        return jnp.concatenate(parts, axis=0)


def keep_halves(tile, state, hi_ref, lo_ref):
    hi_ref[:, tile.here], lo_ref[:, tile.here] = halves(state)


def by_state(hi_ref, lo_ref, rows_ref, h):
    channels, low, high = hi_ref.shape[1], HEAD_DIM * h, HEAD_DIM * (h + 1)
    start, stop = low // LANES * LANES, min(channels, -(-high // LANES) * LANES)
    own = relu(rows_ref[low:high, :])
    parts = [jnp.zeros((n, own.shape[1]), BF16) for n in (low - start, stop - high)]
    rhs = jnp.concatenate([p for p in (parts[0], own, parts[1]) if len(p)], axis=0)
    return both_halves(dot, hi_ref[:, start:stop], lo_ref[:, start:stop], rhs)


def turn(tile, state, extra, hi_ref, lo_ref):
    hi, lo = halves(jnp.concatenate([state, extra], axis=0).T)
    hi_ref[tile.here, :], lo_ref[tile.here, :] = hi, lo


def with_rows(x, rest):
    return jnp.concatenate([x, rest.astype(BF16)], axis=0)


def states_kernel(slabs, pieces, *refs):
    loaded, (out_ref, *held, total_ref, sems) = refs[:4], refs[4:]
    copies = [pltpu.make_async_copy(a, b, sems.at[i]) for i, (a, b) in enumerate(zip(loaded, held))]
    for copy in copies:
        copy.start()
    k_ref, v_ref = held[:2]
    channels, rows = k_ref.shape
    total_ref[...] = jnp.zeros_like(total_ref)
    last = out_ref.shape[0] - slabs.pitch
    out_ref[last:, :] = jnp.zeros((slabs.pitch, LANES), F32)
    ones = jnp.ones((16, rows), BF16)
    copies[0].wait()
    for t in tiles(channels):
        total_ref[t.j : t.j + 1, : t.width] = dot_rows(ones, relu(k_ref[t.here, :]))[:1]
    total = total_ref[...]
    for s in range(pieces):
        at = slabs.pitch * s + SLAB * slabs.each
        out_ref[at : at + len(total), :] = total
    copies[1].wait()
    for t in tiles(channels):
        both = dot_rows(v_ref[t.pair, :], relu(k_ref[t.here, :]))
        slabs.put(out_ref, t, heads_apart(t, both))
    copies[2].wait()
    copies[3].wait()


def total_of(parts):
    parts = list(parts)
    out = parts[0]
    for part in parts[1:]:
        out = out + part
    return out


def cut_rows(ref, pitch, piece, start, size):
    at = pitch * piece + start
    return ref[at : at + size, :]


def to_rows_kernel(sizes, in_ref, out_ref):
    rows, base, pitch = sizes
    height = in_ref.shape[0] // len(CHIP)
    sums = [
        total_of(cut_rows(in_ref, height, s, 0, height) for s, d in enumerate(CHIP) if d[0] == c)
        for c in range(2)
    ]
    totals = jnp.concatenate([s[rows * base :] for s in sums], axis=0)
    for y in range(rows):
        for c in range(2):
            at = pitch * y + base * c
            out_ref[at : at + base, :] = sums[c][base * y : base * (y + 1)]
        out_ref[pitch * y + 2 * base : pitch * (y + 1), :] = totals


def to_planes_kernel(sizes, in_ref, out_ref, own_ref):
    planes, base, pitch = sizes
    size = (pitch - 2 * base) // 2
    own = total_of(cut_rows(in_ref, pitch, s, 0, pitch) for s in range(in_ref.shape[0] // pitch))
    own_ref[...] = own
    first, second, low, high = own[:base], own[base : 2 * base], own[2 * base : -size], own[-size:]
    message = jnp.concatenate([first + second, low + high], axis=0)
    for p in range(planes):
        out_ref[len(message) * p : len(message) * (p + 1), :] = message


def suffix_kernel(rows, base, in_ref, own_ref, out_ref):
    z, core = lax.axis_index("z"), lax.axis_index("core")
    height = in_ref.shape[0] // len(PLANES)
    after = total_of(
        jnp.where(p > z, cut_rows(in_ref, height, s, 0, height), 0.0) for s, p in enumerate(PLANES)
    )
    own = own_ref[...]
    first, second, part = own[:base], own[base : 2 * base], own[2 * base :]
    late = after[:base] + second
    beyond = after[base:]
    message = jnp.concatenate(
        [late + first, late, beyond + part, beyond + jnp.where(core > 0, part, 0.0)], axis=0
    )
    for s in range(rows):
        out_ref[len(message) * s : len(message) * (s + 1), :] = message


def to_columns_kernel(sizes, in_ref, out_ref):
    rows, base, pitch = sizes
    size = (pitch - 2 * base) // 2
    height = rows * base + size
    for c in range(2):
        parts = [cut_rows(in_ref, pitch, y, base * c, base) for y in range(rows)]
        parts.append(
            total_of(cut_rows(in_ref, pitch, y, 2 * base + size * c, size) for y in range(rows))
        )
        message = jnp.concatenate(parts, axis=0)
        for s, d in enumerate(CHIP):
            if d[0] == c:
                out_ref[height * s : height * (s + 1), :] = message


def denominators(q_ref, total, padded):
    den = None
    for t in tiles(q_ref.shape[0]):
        spot = on_own_head(t, jnp.broadcast_to(total[t.j : t.j + 1, : t.width], (padded, t.width)))
        term = dot(jnp.concatenate(thirds(spot), axis=0), relu(q_ref[t.here, :]))
        den = term if den is None else den + term
    return den[:padded] + den[padded : 2 * padded] + den[2 * padded :] + 1.0


def gradient_states(slabs, q_ref, g_ref, rec, out_ref, hi_ref, lo_ref):
    channels = q_ref.shape[0]
    for h in range(channels // HEAD_DIM):
        hi, lo = halves(g_ref[of_head(h), :].astype(F32) * rec[h : h + 1])
        hi_ref[of_head(h), :], lo_ref[of_head(h), :] = hi, lo
    for t in tiles(channels):
        rhs = relu(q_ref[t.here, :])
        both = both_halves(dot_rows, hi_ref[t.pair, :], lo_ref[t.pair, :], rhs)
        slabs.put(out_ref, t, heads_apart(t, both))


def prefix(base, in_ref, own_ref):
    z, core = lax.axis_index("z"), lax.axis_index("core")
    height = in_ref.shape[0] // len(PLANES)
    before = total_of(
        jnp.where(p < z, cut_rows(in_ref, height, s, 0, height), 0.0) for s, p in enumerate(PLANES)
    )
    own, size = own_ref[...], height - base
    early = before[:base] + own[:base]
    total = before[base:] + own[2 * base : -size] + jnp.where(core > 0, own[-size:], 0.0)
    return early, early + own[base : 2 * base], total


def denominator_kernel(slabs, in_ref, own_ref, q_ref, g_ref, out_ref, rec_ref, total_ref, hi_ref, lo_ref):
    early, late, total = prefix(slabs.base, in_ref, own_ref)
    total_ref[...] = total
    rec = 1.0 / denominators(q_ref, total, rec_ref.shape[0])
    rec_ref[...] = rec
    pieces = out_ref.shape[0] // slabs.pitch
    spare = slabs.pitch * slabs.places[pieces - 1]
    out_ref[spare : spare + slabs.pitch, :] = jnp.zeros((slabs.pitch, LANES), F32)
    gradient_states(slabs, q_ref, g_ref, rec, out_ref, hi_ref, lo_ref)
    for s in range(pieces):
        at = slabs.pitch * s
        out_ref[at : at + slabs.base, :] = late if PLANE[s][0] else early


def attention(slabs, in_ref, q_ref, g_ref, rec, mixed_ref, sums_ref, gt_ref, *flat):
    channels = q_ref.shape[0]
    padded = rec.shape[0]
    for t in tiles(channels):
        keep_halves(t, slabs.get(in_ref, t), *flat)
    sums_ref[...] = jnp.zeros_like(sums_ref)
    gt_ref[...] = jnp.zeros_like(gt_ref)
    for h in range(channels // HEAD_DIM):
        attn = by_state(*flat, q_ref, h) * rec[h : h + 1]
        mixed_ref[of_head(h), :] = attn.astype(BF16)
        sums_ref[h : h + 1, :] = jnp.sum(g_ref[of_head(h), :].astype(F32) * attn, axis=0, keepdims=True)
    pair = jnp.concatenate(halves(-sums_ref[...] * rec), axis=0)
    for t in tiles(channels):
        term = dot_rows(pair, relu(q_ref[t.here, :]))
        term = on_own_head(t, term[:padded] + term[padded:])
        gt_ref[t.j : t.j + 1, : t.width] = jnp.sum(term, axis=0, keepdims=True)


def attention_kernel(planes, slabs, in_ref, q_ref, g_ref, rec_ref, out_ref, own_ref, mixed_ref, sums_ref, flat_hi_ref, flat_lo_ref, gt_ref):
    attention(slabs, in_ref, q_ref, g_ref, rec_ref[...], mixed_ref, sums_ref, gt_ref, flat_hi_ref, flat_lo_ref)
    size = SLAB * slabs.each
    sums = [
        total_of(cut_rows(in_ref, slabs.pitch, s, size, size) for s, d in enumerate(PLANE) if d[0] == c)
        for c in range(2)
    ]
    part = gt_ref[...]
    own_ref[...] = jnp.concatenate([*sums, part], axis=0)
    message = jnp.concatenate([sums[0] + sums[1], part], axis=0)
    for p in range(planes):
        out_ref[len(message) * p : len(message) * (p + 1), :] = message


def queries_kernel(slabs, in_ref, q_ref, g_ref, rec_ref, sums_ref, total_ref, attn_ref, out_ref, mixed_ref, hi_ref, lo_ref):
    channels, rows = q_ref.shape
    mixed_ref[...] = attn_ref[...]
    for t in tiles(channels):
        shape = (LANES - HEAD_DIM, t.width)
        extra = jnp.where(row(shape) < 2, jnp.broadcast_to(total_ref[t.j : t.j + 1, : t.width], shape), 0.0)
        turn(t, slabs.get(in_ref, t), extra, hi_ref, lo_ref)
    for h in range(channels // HEAD_DIM):
        hi, lo = halves(-sums_ref[h : h + 1, :])
        shape = (LANES - HEAD_DIM, rows)
        rest = jnp.where(row(shape) == 0, jnp.broadcast_to(hi.astype(F32), shape), 0.0)
        rest = jnp.where(row(shape) == 1, jnp.broadcast_to(lo.astype(F32), shape), rest)
        rhs = with_rows(g_ref[of_head(h), :], rest)
        feature = both_halves(dot, hi_ref[of_head(h), :], lo_ref[of_head(h), :], rhs) * rec_ref[h : h + 1, :]
        q = q_ref[of_head(h), :].astype(F32)
        out_ref[of_head(h), :] = jnp.where(q > 0, feature, 0.0).astype(BF16)


def keys(slabs, in_ref, total, k_ref, v_ref, gk_ref, gv_ref, flat, hi_ref, lo_ref):
    channels, rows = k_ref.shape
    for t in tiles(channels):
        shape = (LANES - HEAD_DIM, t.width)
        extra = jnp.where(row(shape) < 1, jnp.broadcast_to(total[t.j : t.j + 1, : t.width], shape), 0.0)
        state = slabs.get(in_ref, t)
        keep_halves(t, state, *flat)
        turn(t, state, extra, hi_ref, lo_ref)
    ones = jnp.ones((LANES - HEAD_DIM, rows), BF16)
    for h in range(channels // HEAD_DIM):
        gv_ref[of_head(h), :] = by_state(*flat, k_ref, h).astype(BF16)
        rhs = with_rows(v_ref[of_head(h), :], ones)
        grad = both_halves(dot, hi_ref[of_head(h), :], lo_ref[of_head(h), :], rhs)
        k = k_ref[of_head(h), :].astype(F32)
        gk_ref[of_head(h), :] = jnp.where(k > 0, grad, 0.0).astype(BF16)


def keys_kernel(slabs, in_ref, k_ref, v_ref, gk_ref, gv_ref, flat_hi_ref, flat_lo_ref, hi_ref, lo_ref):
    base = SLAB * slabs.each
    pieces = in_ref.shape[0] // slabs.pitch
    total = total_of(cut_rows(in_ref, slabs.pitch, s, base, slabs.pitch - base) for s in range(pieces))
    flat = flat_hi_ref, flat_lo_ref
    keys(slabs, in_ref, total, k_ref, v_ref, gk_ref, gv_ref, flat, hi_ref, lo_ref)


def call(kernel, out, in_specs, scratch=(), more=(), flops=10**7, moved=10**6):
    shapes = [jax.ShapeDtypeStruct(s, d) for s, d in out]
    several = len(shapes) > 1
    return pl.pallas_call(
        kernel,
        out_shape=shapes if several else shapes[0],
        in_specs=in_specs,
        out_specs=[VMEM] * len(shapes) if several else VMEM,
        scratch_shapes=[pltpu.VMEM(s, d) for s, d in scratch] + list(more),
        cost_estimate=pl.CostEstimate(flops=flops, bytes_accessed=moved, transcendentals=0),
        compiler_params=pltpu.CompilerParams(vmem_limit_bytes=24 * 2**20),
    )


def exchanged(message, axes, order):
    sizes = [lax.axis_size(a) for a in axes]
    order = [int(np.ravel_multi_index(d, sizes)) for d in order]
    pieces = message.reshape(len(order), -1)
    pieces = lax.all_to_all(pieces, axes, 0, 0, tiled=True, axis_index_groups=[order])
    return pieces.reshape(message.shape)


def over_chips(message):
    return exchanged(message, ("core", "x"), CHIP)


def over_rows(message):
    return exchanged(message, ("y",), [(y,) for y in ROWS])


def over_planes(message):
    return exchanged(message, ("z",), [(z,) for z in PLANES])


def body(queries, keys_in, values_in, grad_attn):
    q, k, v, g = (a[0].T for a in (queries, keys_in, values_in, grad_attn))
    channels, rows = q.shape
    nx, ny, nz = (lax.axis_size(a) for a in ("x", "y", "z"))
    count = len(tiles(channels))
    each = -(-count * (HEAD_DIM // SLAB) // (2 * nx * ny))
    base = SLAB * each
    tall, pitch, short = ny * base + count, 2 * (base + count), base + count
    places = [PLANE.index((*chip, y)) for chip in CHIP for y in ROWS]
    outer, middle = Slabs(tall, ny * each), Slabs(2 * base, each, base, places)
    got = Slabs(2 * base, each, 0, places)
    flat, line = ((HEAD_DIM, channels), BF16), ((count, LANES), F32)
    whole, small = ((channels, rows), BF16), ((16, rows), F32)

    def message(pieces, height):
        return ((pieces * height, LANES), F32)

    sent, k, v, q, g = call(
        functools.partial(states_kernel, outer, 2 * nx),
        [message(2 * nx, tall)] + [whole] * 4, [HBM] * 4, [line], [pltpu.SemaphoreType.DMA((4,))],
    )(*(pltpu.with_memory_space_constraint(a, pltpu.HBM) for a in (k, v, q, g)))
    sent = call(
        functools.partial(to_rows_kernel, (ny, base, pitch)), [message(ny, pitch)], [VMEM]
    )(over_chips(sent))
    sent, own = call(
        functools.partial(to_planes_kernel, (nz, base, pitch)),
        [message(nz, short), message(1, pitch)], [VMEM],
    )(over_rows(sent))
    sent, rec, total = call(
        functools.partial(denominator_kernel, middle),
        [message(2 * nx * ny, 2 * base), small, line], [VMEM] * 4, [whole, whole],
    )(over_planes(sent), own, q, g)
    states = exchanged(sent, ("core", "x", "y"), PLANE)
    sent, own, attn, sums = call(
        functools.partial(attention_kernel, nz, got),
        [message(nz, short), message(1, base + short), whole, small], [VMEM] * 4, [flat, flat, line],
    )(states, q, g, rec)
    grad_queries, mixed = call(
        functools.partial(queries_kernel, got), [whole] * 2, [VMEM] * 7, [whole, whole]
    )(states, q, g, rec, sums, total, attn)
    sent, grad_queries = lax.optimization_barrier((sent, grad_queries))
    sent = call(
        functools.partial(suffix_kernel, ny, base), [message(ny, pitch)], [VMEM] * 2
    )(over_planes(sent), own)
    sent = call(
        functools.partial(to_columns_kernel, (ny, base, pitch)), [message(2 * nx, tall)], [VMEM]
    )(over_rows(sent))
    grad_keys, values_gradient = call(
        functools.partial(keys_kernel, outer), [whole] * 2, [VMEM] * 3, [flat, flat, whole, whole]
    )(over_chips(sent), k, v)
    return tuple(a.T[None] for a in (mixed, grad_queries, grad_keys, values_gradient))


def solution(mesh):
    groups, spaces = mesh.devices.shape
    split = Mesh(
        mesh.devices.reshape(groups // 2, 2, spaces // 8, 8), ("z", "core", "x", "y")
    )
    placed = P(("z", "core"), ("x", "y"), None)
    return jax.shard_map(
        body, mesh=split, in_specs=(placed,) * 4, out_specs=(placed,) * 4, check_vma=False
    )
```

```python
import functools

import jax
import jax.numpy as jnp
import numpy as np
from jax import lax
from jax.experimental import pallas as pl
from jax.experimental.pallas import tpu as pltpu
from jax.sharding import Mesh
from jax.sharding import PartitionSpec as P

PLANES = (0, 1, 7, 2, 6, 3, 5, 4)
ROWS = (0, 4, 2, 6, 1, 5, 3, 7)
FULL_ROWS = (0, 4, 1, 5, 2, 6, 3, 7)
CHIP = tuple((n % 2, n // 2) for n in (5, 0, 6, 4, 1, 7, 2, 3))

HEAD_DIM = 112
LANES = 128
SLAB = 8
F32, BF16 = jnp.float32, jnp.bfloat16
VMEM = pl.BlockSpec(memory_space=pltpu.VMEM)
HBM = pl.BlockSpec(memory_space=pltpu.HBM)
NT = (((1,), (1,)), ((), ()))


class Tile:
    def __init__(self, j, channels):
        self.j, self.at = j, LANES * j
        self.width = min(LANES, channels - self.at)
        self.first = self.at // HEAD_DIM
        self.last = (self.at + self.width - 1) // HEAD_DIM
        self.here = slice(self.at, self.at + self.width)
        self.cut = min(self.width, HEAD_DIM * (self.first + 1) - self.at)
        self.pair = slice(HEAD_DIM * self.first, HEAD_DIM * (self.last + 1))


def tiles(channels):
    return [Tile(j, channels) for j in range(-(-channels // LANES))]


def dot(a, b):
    return jnp.dot(a, b, preferred_element_type=F32)


def dot_rows(a, b):
    return lax.dot_general(a, b, (((1,), (1,)), ((), ())), preferred_element_type=F32)


def both_halves(by, hi, lo, rhs):
    out = by(jnp.concatenate([hi, lo], axis=0), rhs)
    return out[: len(hi)] + out[len(hi) :]


def halves(x):
    hi = x.astype(BF16)
    return hi, (x - hi.astype(F32)).astype(BF16)


def thirds(x):
    hi = x.astype(BF16)
    rest = x - hi.astype(F32)
    mid = rest.astype(BF16)
    return hi, mid, (rest - mid.astype(F32)).astype(BF16)


def relu(x):
    return jnp.maximum(x, jnp.zeros_like(x))


def lane(shape):
    return lax.broadcasted_iota(jnp.int32, shape, 1)


def row(shape):
    return lax.broadcasted_iota(jnp.int32, shape, 0)


def of_head(h):
    return slice(HEAD_DIM * h, HEAD_DIM * (h + 1))


def on_own_head(tile, x):
    heads = jnp.where(lane(x.shape) < tile.cut, tile.first, tile.last)
    return jnp.where(row(x.shape) == heads, x, 0.0)


def heads_apart(tile, both):
    if tile.first == tile.last:
        return both
    top, bottom = both[:HEAD_DIM], both[HEAD_DIM:]
    return jnp.where(lane(top.shape) < tile.cut, top, bottom)


class Slabs:
    def __init__(self, start):
        self.start = start

    def rows(self, tile):
        for i in range(HEAD_DIM // SLAB):
            at = self.start(HEAD_DIM // SLAB * tile.j + i)
            yield slice(SLAB * i, SLAB * (i + 1)), slice(at, at + SLAB)

    def put(self, ref, tile, value):
        for here, there in self.rows(tile):
            ref[there, : tile.width] = value[here]

    def get(self, ref, tile):
        parts = [ref[there, : tile.width] for _, there in self.rows(tile)]
        return jnp.concatenate(parts, axis=0)


def keep_halves(tile, state, hi_ref, lo_ref):
    hi_ref[:, tile.here], lo_ref[:, tile.here] = halves(state)


def by_state(hi_ref, lo_ref, rows_ref, h):
    channels, low, high = hi_ref.shape[1], HEAD_DIM * h, HEAD_DIM * (h + 1)
    start, stop = low // LANES * LANES, min(channels, -(-high // LANES) * LANES)
    own = relu(rows_ref[low:high, :])
    parts = [jnp.zeros((n, own.shape[1]), BF16) for n in (low - start, stop - high)]
    rhs = jnp.concatenate([p for p in (parts[0], own, parts[1]) if len(p)], axis=0)
    return both_halves(dot, hi_ref[:, start:stop], lo_ref[:, start:stop], rhs)


def turn(tile, state, extra, hi_ref, lo_ref):
    hi, lo = halves(jnp.concatenate([state, extra], axis=0).T)
    hi_ref[tile.here, :], lo_ref[tile.here, :] = hi, lo


def with_rows(x, rest):
    return jnp.concatenate([x, rest.astype(BF16)], axis=0)


def states_kernel(slabs, height, *refs):
    loaded, (out_ref, *held, total_ref, sems) = refs[:4], refs[4:]
    copies = [pltpu.make_async_copy(a, b, sems.at[i]) for i, (a, b) in enumerate(zip(loaded, held))]
    for copy in copies:
        copy.start()
    k_ref, v_ref = held[:2]
    channels, rows = k_ref.shape
    total_ref[...] = jnp.zeros_like(total_ref)
    pieces = out_ref.shape[0] // height
    out_ref[height * (pieces - 1) :, :] = jnp.zeros((height, LANES), F32)
    ones = jnp.ones((16, rows), BF16)
    copies[0].wait()
    for t in tiles(channels):
        total_ref[t.j : t.j + 1, : t.width] = dot_rows(ones, relu(k_ref[t.here, :]))[:1]
    total = total_ref[...]
    for s in range(pieces):
        at = height * (s + 1)
        out_ref[at - len(total) : at, :] = total
    copies[1].wait()
    for t in tiles(channels):
        both = dot_rows(v_ref[t.pair, :], relu(k_ref[t.here, :]))
        slabs.put(out_ref, t, heads_apart(t, both))
    copies[2].wait()
    copies[3].wait()


def total_of(parts):
    parts = list(parts)
    out = parts[0]
    for part in parts[1:]:
        out = out + part
    return out


def cut_rows(ref, pitch, piece, start, size):
    at = pitch * piece + start
    return ref[at : at + size, :]


def to_rows_kernel(sizes, in_ref, out_ref):
    rows, base, pitch = sizes
    height = in_ref.shape[0] // len(CHIP)
    sums = [
        total_of(cut_rows(in_ref, height, s, 0, height) for s, d in enumerate(CHIP) if d[0] == c)
        for c in range(2)
    ]
    totals = jnp.concatenate([s[rows * base :] for s in sums], axis=0)
    for y in range(rows):
        for c in range(2):
            at = pitch * y + base * c
            out_ref[at : at + base, :] = sums[c][base * y : base * (y + 1)]
        out_ref[pitch * y + 2 * base : pitch * (y + 1), :] = totals


def to_planes_kernel(sizes, in_ref, out_ref, own_ref):
    planes, base, pitch = sizes
    size = (pitch - 2 * base) // 2
    own = total_of(cut_rows(in_ref, pitch, s, 0, pitch) for s in range(in_ref.shape[0] // pitch))
    own_ref[...] = own
    first, second, low, high = own[:base], own[base : 2 * base], own[2 * base : -size], own[-size:]
    message = jnp.concatenate([first + second, low + high], axis=0)
    for p in range(planes):
        out_ref[len(message) * p : len(message) * (p + 1), :] = message


def suffix_kernel(rows, base, in_ref, own_ref, out_ref):
    z, core = lax.axis_index("z"), lax.axis_index("core")
    height = in_ref.shape[0] // len(PLANES)
    after = total_of(
        jnp.where(p > z, cut_rows(in_ref, height, s, 0, height), 0.0) for s, p in enumerate(PLANES)
    )
    own = own_ref[...]
    first, second, part = own[:base], own[base : 2 * base], own[2 * base :]
    late = after[:base] + second
    beyond = after[base:]
    message = jnp.concatenate(
        [late + first, late, beyond + part, beyond + jnp.where(core > 0, part, 0.0)], axis=0
    )
    for s in range(rows):
        out_ref[len(message) * s : len(message) * (s + 1), :] = message


def to_columns_kernel(sizes, in_ref, out_ref):
    rows, base, pitch = sizes
    size = (pitch - 2 * base) // 2
    height = rows * base + size
    for c in range(2):
        parts = [cut_rows(in_ref, pitch, y, base * c, base) for y in range(rows)]
        parts.append(
            total_of(cut_rows(in_ref, pitch, y, 2 * base + size * c, size) for y in range(rows))
        )
        message = jnp.concatenate(parts, axis=0)
        for s, d in enumerate(CHIP):
            if d[0] == c:
                out_ref[height * s : height * (s + 1), :] = message


def denominators(q_ref, total, padded):
    den = None
    for t in tiles(q_ref.shape[0]):
        spot = on_own_head(t, jnp.broadcast_to(total[t.j : t.j + 1, : t.width], (padded, t.width)))
        term = dot(jnp.concatenate(thirds(spot), axis=0), relu(q_ref[t.here, :]))
        den = term if den is None else den + term
    return den[:padded] + den[padded : 2 * padded] + den[2 * padded :] + 1.0


def gradient_states(slabs, q_ref, g_ref, rec, out_ref, hi_ref, lo_ref):
    channels = q_ref.shape[0]
    for h in range(channels // HEAD_DIM):
        hi, lo = halves(g_ref[of_head(h), :].astype(F32) * rec[h : h + 1])
        hi_ref[of_head(h), :], lo_ref[of_head(h), :] = hi, lo
    for t in tiles(channels):
        rhs = relu(q_ref[t.here, :])
        both = both_halves(dot_rows, hi_ref[t.pair, :], lo_ref[t.pair, :], rhs)
        slabs.put(out_ref, t, heads_apart(t, both))


def prefix(base, in_ref, own_ref):
    z, core = lax.axis_index("z"), lax.axis_index("core")
    height = in_ref.shape[0] // len(PLANES)
    before = total_of(
        jnp.where(p < z, cut_rows(in_ref, height, s, 0, height), 0.0) for s, p in enumerate(PLANES)
    )
    own, size = own_ref[...], height - base
    early = before[:base] + own[:base]
    total = before[base:] + own[2 * base : -size] + jnp.where(core > 0, own[-size:], 0.0)
    return early, early + own[base : 2 * base], total


def denominator_kernel(base, slabs, in_ref, own_ref, q_ref, g_ref, out_ref, rec_ref, total_ref, hi_ref, lo_ref):
    early, late, total = prefix(base, in_ref, own_ref)
    total_ref[...] = total
    rec = 1.0 / denominators(q_ref, total, rec_ref.shape[0])
    rec_ref[...] = rec
    pieces = len(FULL_ROWS)
    height = out_ref.shape[0] // pieces
    out_ref[-base:, :] = jnp.zeros((base, LANES), F32)
    gradient_states(slabs, q_ref, g_ref, rec, out_ref, hi_ref, lo_ref)
    for s in range(pieces):
        out_ref[height * s : height * s + base, :] = early
        out_ref[height * s + base : height * s + 2 * base, :] = late


def cross_kernel(base, in_ref, out_ref):
    pieces = len(FULL_ROWS)
    height = in_ref.shape[0] // pieces
    size = pieces * base
    order = [FULL_ROWS.index(y) for y in ROWS]
    states = [
        jnp.concatenate([cut_rows(in_ref, height, s, base * c, base) for s in order], axis=0)
        for c in range(2)
    ]
    share = total_of(cut_rows(in_ref, height, s, 2 * base, size) for s in range(pieces))
    for s, d in enumerate(CHIP):
        at = (size + base) * s
        out_ref[at : at + size, :] = states[d[0]]
        out_ref[at + size : at + size + base, :] = share[base * s : base * (s + 1)]


def attention(slabs, in_ref, q_ref, g_ref, rec, mixed_ref, sums_ref, gt_ref, *flat):
    channels = q_ref.shape[0]
    padded = rec.shape[0]
    for t in tiles(channels):
        keep_halves(t, slabs.get(in_ref, t), *flat)
    sums_ref[...] = jnp.zeros_like(sums_ref)
    gt_ref[...] = jnp.zeros_like(gt_ref)
    for h in range(channels // HEAD_DIM):
        attn = by_state(*flat, q_ref, h) * rec[h : h + 1]
        mixed_ref[of_head(h), :] = attn.astype(BF16)
        sums_ref[h : h + 1, :] = jnp.sum(g_ref[of_head(h), :].astype(F32) * attn, axis=0, keepdims=True)
    pair = jnp.concatenate(halves(-sums_ref[...] * rec), axis=0)
    for t in tiles(channels):
        term = dot_rows(pair, relu(q_ref[t.here, :]))
        term = on_own_head(t, term[:padded] + term[padded:])
        gt_ref[t.j : t.j + 1, : t.width] = jnp.sum(term, axis=0, keepdims=True)


def attention_kernel(planes, base, slabs, in_ref, q_ref, g_ref, rec_ref, out_ref, own_ref, mixed_ref, sums_ref, flat_hi_ref, flat_lo_ref, gt_ref):
    attention(slabs, in_ref, q_ref, g_ref, rec_ref[...], mixed_ref, sums_ref, gt_ref, flat_hi_ref, flat_lo_ref)
    height = in_ref.shape[0] // len(CHIP)
    sums = [
        total_of(cut_rows(in_ref, height, s, height - base, base) for s, d in enumerate(CHIP) if d[0] == c)
        for c in range(2)
    ]
    part = gt_ref[...]
    own_ref[...] = jnp.concatenate([*sums, part], axis=0)
    message = jnp.concatenate([sums[0] + sums[1], part], axis=0)
    for p in range(planes):
        out_ref[len(message) * p : len(message) * (p + 1), :] = message


def queries_kernel(slabs, in_ref, q_ref, g_ref, rec_ref, sums_ref, total_ref, attn_ref, out_ref, mixed_ref, hi_ref, lo_ref):
    channels, rows = q_ref.shape
    mixed_ref[...] = attn_ref[...]
    for t in tiles(channels):
        shape = (LANES - HEAD_DIM, t.width)
        extra = jnp.where(row(shape) < 2, jnp.broadcast_to(total_ref[t.j : t.j + 1, : t.width], shape), 0.0)
        turn(t, slabs.get(in_ref, t), extra, hi_ref, lo_ref)
    for h in range(channels // HEAD_DIM):
        hi, lo = halves(-sums_ref[h : h + 1, :])
        shape = (LANES - HEAD_DIM, rows)
        rest = jnp.where(row(shape) == 0, jnp.broadcast_to(hi.astype(F32), shape), 0.0)
        rest = jnp.where(row(shape) == 1, jnp.broadcast_to(lo.astype(F32), shape), rest)
        rhs = with_rows(g_ref[of_head(h), :], rest)
        feature = both_halves(dot, hi_ref[of_head(h), :], lo_ref[of_head(h), :], rhs) * rec_ref[h : h + 1, :]
        q = q_ref[of_head(h), :].astype(F32)
        out_ref[of_head(h), :] = jnp.where(q > 0, feature, 0.0).astype(BF16)


def keys(slabs, in_ref, total, k_ref, v_ref, gk_ref, gv_ref, flat, hi_ref, lo_ref):
    channels, rows = k_ref.shape
    for t in tiles(channels):
        shape = (LANES - HEAD_DIM, t.width)
        extra = jnp.where(row(shape) < 1, jnp.broadcast_to(total[t.j : t.j + 1, : t.width], shape), 0.0)
        state = slabs.get(in_ref, t)
        keep_halves(t, state, *flat)
        turn(t, state, extra, hi_ref, lo_ref)
    ones = jnp.ones((LANES - HEAD_DIM, rows), BF16)
    for h in range(channels // HEAD_DIM):
        gv_ref[of_head(h), :] = by_state(*flat, k_ref, h).astype(BF16)
        rhs = with_rows(v_ref[of_head(h), :], ones)
        grad = both_halves(dot, hi_ref[of_head(h), :], lo_ref[of_head(h), :], rhs)
        k = k_ref[of_head(h), :].astype(F32)
        gk_ref[of_head(h), :] = jnp.where(k > 0, grad, 0.0).astype(BF16)


def keys_kernel(slabs, in_ref, k_ref, v_ref, gk_ref, gv_ref, flat_hi_ref, flat_lo_ref, hi_ref, lo_ref):
    pieces = len(CHIP)
    height, count = in_ref.shape[0] // pieces, len(tiles(k_ref.shape[0]))
    total = total_of(cut_rows(in_ref, height, s, height - count, count) for s in range(pieces))
    flat = flat_hi_ref, flat_lo_ref
    keys(slabs, in_ref, total, k_ref, v_ref, gk_ref, gv_ref, flat, hi_ref, lo_ref)


def call(kernel, out, in_specs, scratch=(), more=(), flops=10**7, moved=10**6):
    shapes = [jax.ShapeDtypeStruct(s, d) for s, d in out]
    several = len(shapes) > 1
    return pl.pallas_call(
        kernel,
        out_shape=shapes if several else shapes[0],
        in_specs=in_specs,
        out_specs=[VMEM] * len(shapes) if several else VMEM,
        scratch_shapes=[pltpu.VMEM(s, d) for s, d in scratch] + list(more),
        cost_estimate=pl.CostEstimate(flops=flops, bytes_accessed=moved, transcendentals=0),
        compiler_params=pltpu.CompilerParams(vmem_limit_bytes=24 * 2**20),
    )


def exchanged(message, axes, order):
    sizes = [lax.axis_size(a) for a in axes]
    order = [int(np.ravel_multi_index(d, sizes)) for d in order]
    pieces = message.reshape(len(order), -1)
    pieces = lax.all_to_all(pieces, axes, 0, 0, tiled=True, axis_index_groups=[order])
    return pieces.reshape(message.shape)


def over_chips(message):
    return exchanged(message, ("core", "x"), CHIP)


def over_rows(message, order=ROWS):
    return exchanged(message, ("y",), [(y,) for y in order])


def over_planes(message):
    return exchanged(message, ("z",), [(z,) for z in PLANES])


def body(queries, keys_in, values_in, grad_attn):
    q, k, v, g = (a[0].T for a in (queries, keys_in, values_in, grad_attn))
    channels, rows = q.shape
    nx, ny, nz = (lax.axis_size(a) for a in ("x", "y", "z"))
    count = len(tiles(channels))
    each = -(-count * (HEAD_DIM // SLAB) // (2 * nx * ny))
    base = SLAB * each
    size = ny * base
    tall, pitch, short = size + count, 2 * (base + count), base + count
    wide, full = 2 * base + size, size + base

    def in_turn(height, first=0):
        return Slabs(lambda n: height * (n // (ny * each)) + first + SLAB * (n % (ny * each)))

    def last(n):
        row, chip = FULL_ROWS[n // (ny * each)], n % (ny * each) // each
        return tall * chip + base * ROWS.index(row) + SLAB * (n % each)

    outer, got = in_turn(tall), in_turn(full)
    flat, line = ((HEAD_DIM, channels), BF16), ((count, LANES), F32)
    whole, small = ((channels, rows), BF16), ((16, rows), F32)

    def message(pieces, height):
        return ((pieces * height, LANES), F32)

    sent, k, v, q, g = call(
        functools.partial(states_kernel, outer, tall),
        [message(2 * nx, tall)] + [whole] * 4, [HBM] * 4, [line], [pltpu.SemaphoreType.DMA((4,))],
    )(*(pltpu.with_memory_space_constraint(a, pltpu.HBM) for a in (k, v, q, g)))
    sent = call(
        functools.partial(to_rows_kernel, (ny, base, pitch)), [message(ny, pitch)], [VMEM]
    )(over_chips(sent))
    sent, own = call(
        functools.partial(to_planes_kernel, (nz, base, pitch)),
        [message(nz, short), message(1, pitch)], [VMEM],
    )(over_rows(sent))
    sent, rec, total = call(
        functools.partial(denominator_kernel, base, in_turn(wide, 2 * base)),
        [message(ny, wide), small, line], [VMEM] * 4, [whole, whole],
    )(over_planes(sent), own, q, g)
    sent = call(
        functools.partial(cross_kernel, base), [message(2 * nx, full)], [VMEM]
    )(over_rows(sent, FULL_ROWS))
    states = over_chips(sent)
    sent, own, attn, sums = call(
        functools.partial(attention_kernel, nz, base, got),
        [message(nz, short), message(1, base + short), whole, small], [VMEM] * 4, [flat, flat, line],
    )(states, q, g, rec)
    grad_queries, mixed = call(
        functools.partial(queries_kernel, got), [whole] * 2, [VMEM] * 7, [whole, whole]
    )(states, q, g, rec, sums, total, attn)
    sent, grad_queries = lax.optimization_barrier((sent, grad_queries))
    sent = call(
        functools.partial(suffix_kernel, ny, base), [message(ny, pitch)], [VMEM] * 2
    )(over_planes(sent), own)
    sent = call(
        functools.partial(to_columns_kernel, (ny, base, pitch)), [message(2 * nx, tall)], [VMEM]
    )(over_rows(sent))
    grad_keys, values_gradient = call(
        functools.partial(keys_kernel, Slabs(last)), [whole] * 2, [VMEM] * 3, [flat, flat, whole, whole]
    )(over_chips(sent), k, v)
    return tuple(a.T[None] for a in (mixed, grad_queries, grad_keys, values_gradient))


def solution(mesh):
    groups, spaces = mesh.devices.shape
    split = Mesh(
        mesh.devices.reshape(groups // 2, 2, spaces // 8, 8), ("z", "core", "x", "y")
    )
    placed = P(("z", "core"), ("x", "y"), None)
    return jax.shard_map(
        body, mesh=split, in_specs=(placed,) * 4, out_specs=(placed,) * 4, check_vma=False
    )
```

```python
import functools

import jax
import jax.numpy as jnp
import numpy as np
from jax import lax
from jax.experimental import pallas as pl
from jax.experimental.pallas import tpu as pltpu
from jax.sharding import Mesh
from jax.sharding import PartitionSpec as P

PLANES = (0, 4, 1, 5, 2, 6, 3, 7)
ROWS = (0, 1, 7, 2, 6, 3, 5, 4)
FULL_ROWS = (0, 4, 6, 2, 7, 3, 5, 1)
CHIP = tuple((n % 2, n // 2) for n in (3, 0, 6, 7, 1, 5, 2, 4))

HEAD_DIM = 112
LANES = 128
SLAB = 8
F32, BF16 = jnp.float32, jnp.bfloat16
VMEM = pl.BlockSpec(memory_space=pltpu.VMEM)
HBM = pl.BlockSpec(memory_space=pltpu.HBM)
NT = (((1,), (1,)), ((), ()))


class Tile:
    def __init__(self, j, channels):
        self.j, self.at = j, LANES * j
        self.width = min(LANES, channels - self.at)
        self.first = self.at // HEAD_DIM
        self.last = (self.at + self.width - 1) // HEAD_DIM
        self.here = slice(self.at, self.at + self.width)
        self.cut = min(self.width, HEAD_DIM * (self.first + 1) - self.at)
        self.pair = slice(HEAD_DIM * self.first, HEAD_DIM * (self.last + 1))


def tiles(channels):
    return [Tile(j, channels) for j in range(-(-channels // LANES))]


def dot(a, b):
    return jnp.dot(a, b, preferred_element_type=F32)


def dot_rows(a, b):
    return lax.dot_general(a, b, (((1,), (1,)), ((), ())), preferred_element_type=F32)


def both_halves(by, hi, lo, rhs):
    out = by(jnp.concatenate([hi, lo], axis=0), rhs)
    return out[: len(hi)] + out[len(hi) :]


def halves(x):
    hi = x.astype(BF16)
    return hi, (x - hi.astype(F32)).astype(BF16)


def thirds(x):
    hi = x.astype(BF16)
    rest = x - hi.astype(F32)
    mid = rest.astype(BF16)
    return hi, mid, (rest - mid.astype(F32)).astype(BF16)


def relu(x):
    return jnp.maximum(x, jnp.zeros_like(x))


def lane(shape):
    return lax.broadcasted_iota(jnp.int32, shape, 1)


def row(shape):
    return lax.broadcasted_iota(jnp.int32, shape, 0)


def of_head(h):
    return slice(HEAD_DIM * h, HEAD_DIM * (h + 1))


def on_own_head(tile, x):
    heads = jnp.where(lane(x.shape) < tile.cut, tile.first, tile.last)
    return jnp.where(row(x.shape) == heads, x, 0.0)


def heads_apart(tile, both):
    if tile.first == tile.last:
        return both
    top, bottom = both[:HEAD_DIM], both[HEAD_DIM:]
    return jnp.where(lane(top.shape) < tile.cut, top, bottom)


class Slabs:
    def __init__(self, start):
        self.start = start

    def rows(self, tile):
        for i in range(HEAD_DIM // SLAB):
            at = self.start(HEAD_DIM // SLAB * tile.j + i)
            yield slice(SLAB * i, SLAB * (i + 1)), slice(at, at + SLAB)

    def put(self, ref, tile, value):
        for here, there in self.rows(tile):
            ref[there, : tile.width] = value[here]

    def get(self, ref, tile):
        parts = [ref[there, : tile.width] for _, there in self.rows(tile)]
        return jnp.concatenate(parts, axis=0)


def keep_halves(tile, state, hi_ref, lo_ref):
    hi_ref[:, tile.here], lo_ref[:, tile.here] = halves(state)


def by_state(hi_ref, lo_ref, rows_ref, h):
    channels, low, high = hi_ref.shape[1], HEAD_DIM * h, HEAD_DIM * (h + 1)
    start, stop = low // LANES * LANES, min(channels, -(-high // LANES) * LANES)
    own = relu(rows_ref[low:high, :])
    parts = [jnp.zeros((n, own.shape[1]), BF16) for n in (low - start, stop - high)]
    rhs = jnp.concatenate([p for p in (parts[0], own, parts[1]) if len(p)], axis=0)
    return both_halves(dot, hi_ref[:, start:stop], lo_ref[:, start:stop], rhs)


def turn(tile, state, extra, hi_ref, lo_ref):
    hi, lo = halves(jnp.concatenate([state, extra], axis=0).T)
    hi_ref[tile.here, :], lo_ref[tile.here, :] = hi, lo


def with_rows(x, rest):
    return jnp.concatenate([x, rest.astype(BF16)], axis=0)


def parts_of(channels):
    heads = channels // HEAD_DIM
    ends = [HEAD_DIM * (-(-heads * n // 3)) for n in (1, 2, 3)]
    done = 0
    for begin, end in zip([0, *ends], ends):
        ready = [t for t in tiles(channels) if max(t.pair.stop, t.here.stop) <= end]
        yield slice(begin, end), ready[done:]
        done = len(ready)


def states_kernel(slabs, height, *refs):
    loaded, (out_ref, *held, total_ref, sems) = refs[:4], refs[4:]
    channels, rows = loaded[0].shape
    steps = list(parts_of(channels))
    spans = [(i, span) for span, _ in steps for i in range(2)] + [(i, slice(0, channels)) for i in (2, 3)]
    copies = [
        pltpu.make_async_copy(loaded[i].at[span, :], held[i].at[span, :], sems.at[n])
        for n, (i, span) in enumerate(spans)
    ]
    for copy in copies:
        copy.start()
    k_ref, v_ref = held[:2]
    total_ref[...] = jnp.zeros_like(total_ref)
    pieces = out_ref.shape[0] // height
    out_ref[height * (pieces - 1) :, :] = jnp.zeros((height, LANES), F32)
    ones = jnp.ones((16, rows), BF16)
    for n, (_, ready) in enumerate(steps):
        copies[2 * n].wait()
        copies[2 * n + 1].wait()
        for t in ready:
            keys = relu(k_ref[t.here, :])
            total_ref[t.j : t.j + 1, : t.width] = dot_rows(ones, keys)[:1]
            slabs.put(out_ref, t, heads_apart(t, dot_rows(v_ref[t.pair, :], keys)))
    total = total_ref[...]
    for s in range(pieces):
        at = height * (s + 1)
        out_ref[at - len(total) : at, :] = total
    copies[-2].wait()
    copies[-1].wait()


def total_of(parts):
    parts = list(parts)
    out = parts[0]
    for part in parts[1:]:
        out = out + part
    return out


def cut_rows(ref, pitch, piece, start, size):
    at = pitch * piece + start
    return ref[at : at + size, :]


def to_rows_kernel(sizes, in_ref, out_ref):
    rows, base, pitch = sizes
    height = in_ref.shape[0] // len(CHIP)
    sums = [
        total_of(cut_rows(in_ref, height, s, 0, height) for s, d in enumerate(CHIP) if d[0] == c)
        for c in range(2)
    ]
    totals = jnp.concatenate([s[rows * base :] for s in sums], axis=0)
    for y in range(rows):
        for c in range(2):
            at = pitch * y + base * c
            out_ref[at : at + base, :] = sums[c][base * y : base * (y + 1)]
        out_ref[pitch * y + 2 * base : pitch * (y + 1), :] = totals


def to_planes_kernel(sizes, in_ref, out_ref, own_ref):
    planes, base, pitch = sizes
    size = (pitch - 2 * base) // 2
    own = total_of(cut_rows(in_ref, pitch, s, 0, pitch) for s in range(in_ref.shape[0] // pitch))
    own_ref[...] = own
    first, second, low, high = own[:base], own[base : 2 * base], own[2 * base : -size], own[-size:]
    message = jnp.concatenate([first + second, low + high], axis=0)
    for p in range(planes):
        out_ref[len(message) * p : len(message) * (p + 1), :] = message


def suffix_kernel(rows, base, in_ref, own_ref, out_ref):
    z, core = lax.axis_index("z"), lax.axis_index("core")
    height = in_ref.shape[0] // len(PLANES)
    after = total_of(
        jnp.where(p > z, cut_rows(in_ref, height, s, 0, height), 0.0) for s, p in enumerate(PLANES)
    )
    own = own_ref[...]
    first, second, part = own[:base], own[base : 2 * base], own[2 * base :]
    late = after[:base] + second
    beyond = after[base:]
    message = jnp.concatenate(
        [late + first, late, beyond + part, beyond + jnp.where(core > 0, part, 0.0)], axis=0
    )
    for s in range(rows):
        out_ref[len(message) * s : len(message) * (s + 1), :] = message


def to_columns_kernel(sizes, in_ref, out_ref):
    rows, base, pitch = sizes
    size = (pitch - 2 * base) // 2
    height = rows * base + size
    for c in range(2):
        parts = [cut_rows(in_ref, pitch, y, base * c, base) for y in range(rows)]
        parts.append(
            total_of(cut_rows(in_ref, pitch, y, 2 * base + size * c, size) for y in range(rows))
        )
        message = jnp.concatenate(parts, axis=0)
        for s, d in enumerate(CHIP):
            if d[0] == c:
                out_ref[height * s : height * (s + 1), :] = message


def denominators(q_ref, total, padded):
    den = None
    for t in tiles(q_ref.shape[0]):
        spot = on_own_head(t, jnp.broadcast_to(total[t.j : t.j + 1, : t.width], (padded, t.width)))
        term = dot(jnp.concatenate(thirds(spot), axis=0), relu(q_ref[t.here, :]))
        den = term if den is None else den + term
    return den[:padded] + den[padded : 2 * padded] + den[2 * padded :] + 1.0


def gradient_states(slabs, q_ref, g_ref, rec, out_ref, hi_ref, lo_ref):
    channels = q_ref.shape[0]
    for h in range(channels // HEAD_DIM):
        hi, lo = halves(g_ref[of_head(h), :].astype(F32) * rec[h : h + 1])
        hi_ref[of_head(h), :], lo_ref[of_head(h), :] = hi, lo
    for t in tiles(channels):
        rhs = relu(q_ref[t.here, :])
        both = both_halves(dot_rows, hi_ref[t.pair, :], lo_ref[t.pair, :], rhs)
        slabs.put(out_ref, t, heads_apart(t, both))


def prefix(base, in_ref, own_ref):
    z, core = lax.axis_index("z"), lax.axis_index("core")
    height = in_ref.shape[0] // len(PLANES)
    before = total_of(
        jnp.where(p < z, cut_rows(in_ref, height, s, 0, height), 0.0) for s, p in enumerate(PLANES)
    )
    own, size = own_ref[...], height - base
    early = before[:base] + own[:base]
    total = before[base:] + own[2 * base : -size] + jnp.where(core > 0, own[-size:], 0.0)
    return early, early + own[base : 2 * base], total


def denominator_kernel(base, slabs, in_ref, own_ref, q_ref, g_ref, out_ref, rec_ref, total_ref, hi_ref, lo_ref):
    early, late, total = prefix(base, in_ref, own_ref)
    total_ref[...] = total
    rec = 1.0 / denominators(q_ref, total, rec_ref.shape[0])
    rec_ref[...] = rec
    pieces = len(FULL_ROWS)
    height = out_ref.shape[0] // pieces
    out_ref[-base:, :] = jnp.zeros((base, LANES), F32)
    gradient_states(slabs, q_ref, g_ref, rec, out_ref, hi_ref, lo_ref)
    for s in range(pieces):
        out_ref[height * s : height * s + base, :] = early
        out_ref[height * s + base : height * s + 2 * base, :] = late


def cross_kernel(base, in_ref, out_ref):
    pieces = len(FULL_ROWS)
    height = in_ref.shape[0] // pieces
    size = pieces * base
    order = [FULL_ROWS.index(y) for y in ROWS]
    states = [
        jnp.concatenate([cut_rows(in_ref, height, s, base * c, base) for s in order], axis=0)
        for c in range(2)
    ]
    share = total_of(cut_rows(in_ref, height, s, 2 * base, size) for s in range(pieces))
    for s, d in enumerate(CHIP):
        at = (size + base) * s
        out_ref[at : at + size, :] = states[d[0]]
        out_ref[at + size : at + size + base, :] = share[base * s : base * (s + 1)]


def attention(slabs, in_ref, q_ref, g_ref, rec, mixed_ref, sums_ref, gt_ref, *flat):
    channels = q_ref.shape[0]
    padded = rec.shape[0]
    for t in tiles(channels):
        keep_halves(t, slabs.get(in_ref, t), *flat)
    sums_ref[...] = jnp.zeros_like(sums_ref)
    gt_ref[...] = jnp.zeros_like(gt_ref)
    for h in range(channels // HEAD_DIM):
        attn = by_state(*flat, q_ref, h) * rec[h : h + 1]
        mixed_ref[of_head(h), :] = attn.astype(BF16)
        sums_ref[h : h + 1, :] = jnp.sum(g_ref[of_head(h), :].astype(F32) * attn, axis=0, keepdims=True)
    pair = jnp.concatenate(halves(-sums_ref[...] * rec), axis=0)
    for t in tiles(channels):
        term = dot_rows(pair, relu(q_ref[t.here, :]))
        term = on_own_head(t, term[:padded] + term[padded:])
        gt_ref[t.j : t.j + 1, : t.width] = jnp.sum(term, axis=0, keepdims=True)


def attention_kernel(planes, base, slabs, in_ref, q_ref, g_ref, rec_ref, out_ref, own_ref, mixed_ref, sums_ref, flat_hi_ref, flat_lo_ref, gt_ref):
    attention(slabs, in_ref, q_ref, g_ref, rec_ref[...], mixed_ref, sums_ref, gt_ref, flat_hi_ref, flat_lo_ref)
    height = in_ref.shape[0] // len(CHIP)
    sums = [
        total_of(cut_rows(in_ref, height, s, height - base, base) for s, d in enumerate(CHIP) if d[0] == c)
        for c in range(2)
    ]
    part = gt_ref[...]
    own_ref[...] = jnp.concatenate([*sums, part], axis=0)
    message = jnp.concatenate([sums[0] + sums[1], part], axis=0)
    for p in range(planes):
        out_ref[len(message) * p : len(message) * (p + 1), :] = message


def queries_kernel(slabs, in_ref, q_ref, g_ref, rec_ref, sums_ref, total_ref, out_ref, hi_ref, lo_ref):
    channels, rows = q_ref.shape
    for t in tiles(channels):
        shape = (LANES - HEAD_DIM, t.width)
        extra = jnp.where(row(shape) < 2, jnp.broadcast_to(total_ref[t.j : t.j + 1, : t.width], shape), 0.0)
        turn(t, slabs.get(in_ref, t), extra, hi_ref, lo_ref)
    for h in range(channels // HEAD_DIM):
        hi, lo = halves(-sums_ref[h : h + 1, :])
        shape = (LANES - HEAD_DIM, rows)
        rest = jnp.where(row(shape) == 0, jnp.broadcast_to(hi.astype(F32), shape), 0.0)
        rest = jnp.where(row(shape) == 1, jnp.broadcast_to(lo.astype(F32), shape), rest)
        rhs = with_rows(g_ref[of_head(h), :], rest)
        feature = both_halves(dot, hi_ref[of_head(h), :], lo_ref[of_head(h), :], rhs) * rec_ref[h : h + 1, :]
        q = q_ref[of_head(h), :].astype(F32)
        out_ref[of_head(h), :] = jnp.where(q > 0, feature, 0.0).astype(BF16)


def keys_kernel(slabs, in_ref, k_ref, v_ref, attn_ref, gq_ref, mixed_out, gq_out, gk_out, gv_out, gk_ref, gv_ref, flat_hi_ref, flat_lo_ref, hi_ref, lo_ref, sems):
    channels, rows = k_ref.shape
    heads, pieces = channels // HEAD_DIM, len(CHIP)
    middle = HEAD_DIM * (heads // 2)
    moves = [(attn_ref, mixed_out, 0, channels), (gq_ref, gq_out, 0, channels)]
    for begin, end in ((0, middle), (middle, channels)):
        moves += [(gk_ref, gk_out, begin, end), (gv_ref, gv_out, begin, end)]
    copies = [
        pltpu.make_async_copy(a.at[begin:end, :], b.at[begin:end, :], sems.at[n])
        for n, (a, b, begin, end) in enumerate(moves)
    ]
    copies[0].start()
    copies[1].start()
    height, count = in_ref.shape[0] // pieces, len(tiles(channels))
    total = total_of(cut_rows(in_ref, height, s, height - count, count) for s in range(pieces))
    for t in tiles(channels):
        shape = (LANES - HEAD_DIM, t.width)
        extra = jnp.where(row(shape) < 1, jnp.broadcast_to(total[t.j : t.j + 1, : t.width], shape), 0.0)
        state = slabs.get(in_ref, t)
        keep_halves(t, state, flat_hi_ref, flat_lo_ref)
        turn(t, state, extra, hi_ref, lo_ref)
    ones = jnp.ones((LANES - HEAD_DIM, rows), BF16)
    for h in range(heads):
        gv_ref[of_head(h), :] = by_state(flat_hi_ref, flat_lo_ref, k_ref, h).astype(BF16)
        rhs = with_rows(v_ref[of_head(h), :], ones)
        grad = both_halves(dot, hi_ref[of_head(h), :], lo_ref[of_head(h), :], rhs)
        k = k_ref[of_head(h), :].astype(F32)
        gk_ref[of_head(h), :] = jnp.where(k > 0, grad, 0.0).astype(BF16)
        if h == heads // 2 - 1:
            copies[2].start()
            copies[3].start()
    copies[4].start()
    copies[5].start()
    for copy in copies:
        copy.wait()


def call(kernel, out, in_specs, scratch=(), more=(), out_space=VMEM, flops=10**7, moved=10**6):
    shapes = [jax.ShapeDtypeStruct(s, d) for s, d in out]
    several = len(shapes) > 1
    return pl.pallas_call(
        kernel,
        out_shape=shapes if several else shapes[0],
        in_specs=in_specs,
        out_specs=[out_space] * len(shapes) if several else out_space,
        scratch_shapes=[pltpu.VMEM(s, d) for s, d in scratch] + list(more),
        cost_estimate=pl.CostEstimate(flops=flops, bytes_accessed=moved, transcendentals=0),
        compiler_params=pltpu.CompilerParams(vmem_limit_bytes=24 * 2**20),
    )


def exchanged(message, axes, order):
    sizes = [lax.axis_size(a) for a in axes]
    order = [int(np.ravel_multi_index(d, sizes)) for d in order]
    pieces = message.reshape(len(order), -1)
    pieces = lax.all_to_all(pieces, axes, 0, 0, tiled=True, axis_index_groups=[order])
    return pieces.reshape(message.shape)


def over_chips(message):
    return exchanged(message, ("core", "x"), CHIP)


def over_rows(message, order=ROWS):
    return exchanged(message, ("y",), [(y,) for y in order])


def over_planes(message):
    return exchanged(message, ("z",), [(z,) for z in PLANES])


def body(queries, keys_in, values_in, grad_attn):
    q, k, v, g = (a[0].T for a in (queries, keys_in, values_in, grad_attn))
    channels, rows = q.shape
    nx, ny, nz = (lax.axis_size(a) for a in ("x", "y", "z"))
    count = len(tiles(channels))
    each = -(-count * (HEAD_DIM // SLAB) // (2 * nx * ny))
    base = SLAB * each
    size = ny * base
    tall, pitch, short = size + count, 2 * (base + count), base + count
    wide, full = 2 * base + size, size + base

    def in_turn(height, first=0):
        return Slabs(lambda n: height * (n // (ny * each)) + first + SLAB * (n % (ny * each)))

    def last(n):
        row, chip = FULL_ROWS[n // (ny * each)], n % (ny * each) // each
        return tall * chip + base * ROWS.index(row) + SLAB * (n % each)

    outer, got = in_turn(tall), in_turn(full)
    flat, line = ((HEAD_DIM, channels), BF16), ((count, LANES), F32)
    whole, small = ((channels, rows), BF16), ((16, rows), F32)

    def message(pieces, height):
        return ((pieces * height, LANES), F32)

    sent, k, v, q, g = call(
        functools.partial(states_kernel, outer, tall),
        [message(2 * nx, tall)] + [whole] * 4, [HBM] * 4, [line], [pltpu.SemaphoreType.DMA((8,))],
    )(*(pltpu.with_memory_space_constraint(a, pltpu.HBM) for a in (k, v, q, g)))
    sent = call(
        functools.partial(to_rows_kernel, (ny, base, pitch)), [message(ny, pitch)], [VMEM]
    )(over_chips(sent))
    sent, own = call(
        functools.partial(to_planes_kernel, (nz, base, pitch)),
        [message(nz, short), message(1, pitch)], [VMEM],
    )(over_rows(sent))
    sent, rec, total = call(
        functools.partial(denominator_kernel, base, in_turn(wide, 2 * base)),
        [message(ny, wide), small, line], [VMEM] * 4, [whole, whole],
    )(over_planes(sent), own, q, g)
    sent = call(
        functools.partial(cross_kernel, base), [message(2 * nx, full)], [VMEM]
    )(over_rows(sent, FULL_ROWS))
    states = over_chips(sent)
    sent, own, attn, sums = call(
        functools.partial(attention_kernel, nz, base, got),
        [message(nz, short), message(1, base + short), whole, small], [VMEM] * 4, [flat, flat, line],
    )(states, q, g, rec)
    grad_queries = call(
        functools.partial(queries_kernel, got), [whole], [VMEM] * 6, [whole, whole]
    )(states, q, g, rec, sums, total)
    sent, grad_queries = lax.optimization_barrier((sent, grad_queries))
    sent = call(
        functools.partial(suffix_kernel, ny, base), [message(ny, pitch)], [VMEM] * 2
    )(over_planes(sent), own)
    sent = call(
        functools.partial(to_columns_kernel, (ny, base, pitch)), [message(2 * nx, tall)], [VMEM]
    )(over_rows(sent))
    outs = call(
        functools.partial(keys_kernel, Slabs(last)),
        [whole] * 4, [VMEM] * 5, [whole, whole, flat, flat, whole, whole],
        [pltpu.SemaphoreType.DMA((6,))], HBM,
    )(over_chips(sent), k, v, attn, grad_queries)
    return tuple(a.T[None] for a in outs)


def solution(mesh):
    groups, spaces = mesh.devices.shape
    split = Mesh(
        mesh.devices.reshape(groups // 2, 2, spaces // 8, 8), ("z", "core", "x", "y")
    )
    placed = P(("z", "core"), ("x", "y"), None)
    return jax.shard_map(
        body, mesh=split, in_specs=(placed,) * 4, out_specs=(placed,) * 4, check_vma=False
    )
```

```python
import functools

import jax
import jax.numpy as jnp
import numpy as np
from jax import lax
from jax.experimental import pallas as pl
from jax.experimental.pallas import tpu as pltpu
from jax.sharding import Mesh
from jax.sharding import PartitionSpec as P

PLANES = (0, 4, 1, 5, 2, 6, 3, 7)
ROWS = (0, 4, 2, 6, 1, 5, 3, 7)
FULL_ROWS = (0, 4, 6, 2, 7, 3, 5, 1)
CHIP = tuple((n % 2, n // 2) for n in (3, 0, 6, 7, 1, 5, 2, 4))

HEAD_DIM = 112
LANES = 128
SLAB = 8
F32, BF16 = jnp.float32, jnp.bfloat16
VMEM = pl.BlockSpec(memory_space=pltpu.VMEM)
HBM = pl.BlockSpec(memory_space=pltpu.HBM)
NT = (((1,), (1,)), ((), ()))


class Tile:
    def __init__(self, j, channels):
        self.j, self.at = j, LANES * j
        self.width = min(LANES, channels - self.at)
        self.first = self.at // HEAD_DIM
        self.last = (self.at + self.width - 1) // HEAD_DIM
        self.here = slice(self.at, self.at + self.width)
        self.cut = min(self.width, HEAD_DIM * (self.first + 1) - self.at)
        self.pair = slice(HEAD_DIM * self.first, HEAD_DIM * (self.last + 1))


def tiles(channels):
    return [Tile(j, channels) for j in range(-(-channels // LANES))]


def dot(a, b):
    return jnp.dot(a, b, preferred_element_type=F32)


def dot_rows(a, b):
    return lax.dot_general(a, b, (((1,), (1,)), ((), ())), preferred_element_type=F32)


def both_halves(by, hi, lo, rhs):
    out = by(jnp.concatenate([hi, lo], axis=0), rhs)
    return out[: len(hi)] + out[len(hi) :]


def halves(x):
    hi = x.astype(BF16)
    return hi, (x - hi.astype(F32)).astype(BF16)


def thirds(x):
    hi = x.astype(BF16)
    rest = x - hi.astype(F32)
    mid = rest.astype(BF16)
    return hi, mid, (rest - mid.astype(F32)).astype(BF16)


def relu(x):
    return jnp.maximum(x, jnp.zeros_like(x))


def lane(shape):
    return lax.broadcasted_iota(jnp.int32, shape, 1)


def row(shape):
    return lax.broadcasted_iota(jnp.int32, shape, 0)


def of_head(h):
    return slice(HEAD_DIM * h, HEAD_DIM * (h + 1))


def on_own_head(tile, x):
    heads = jnp.where(lane(x.shape) < tile.cut, tile.first, tile.last)
    return jnp.where(row(x.shape) == heads, x, 0.0)


def heads_apart(tile, both):
    if tile.first == tile.last:
        return both
    top, bottom = both[:HEAD_DIM], both[HEAD_DIM:]
    return jnp.where(lane(top.shape) < tile.cut, top, bottom)


class Slabs:
    def __init__(self, start):
        self.start = start

    def rows(self, tile):
        for i in range(HEAD_DIM // SLAB):
            at = self.start(HEAD_DIM // SLAB * tile.j + i)
            yield slice(SLAB * i, SLAB * (i + 1)), slice(at, at + SLAB)

    def put(self, ref, tile, value):
        for here, there in self.rows(tile):
            ref[there, : tile.width] = value[here]

    def get(self, ref, tile):
        parts = [ref[there, : tile.width] for _, there in self.rows(tile)]
        return jnp.concatenate(parts, axis=0)


def keep_halves(tile, state, hi_ref, lo_ref):
    hi_ref[:, tile.here], lo_ref[:, tile.here] = halves(state)


def by_state(hi_ref, lo_ref, rows_ref, h):
    channels, low, high = hi_ref.shape[1], HEAD_DIM * h, HEAD_DIM * (h + 1)
    start, stop = low // LANES * LANES, min(channels, -(-high // LANES) * LANES)
    own = relu(rows_ref[low:high, :])
    parts = [jnp.zeros((n, own.shape[1]), BF16) for n in (low - start, stop - high)]
    rhs = jnp.concatenate([p for p in (parts[0], own, parts[1]) if len(p)], axis=0)
    return both_halves(dot, hi_ref[:, start:stop], lo_ref[:, start:stop], rhs)


def turn(tile, state, extra, hi_ref, lo_ref):
    hi, lo = halves(jnp.concatenate([state, extra], axis=0).T)
    hi_ref[tile.here, :], lo_ref[tile.here, :] = hi, lo


def with_rows(x, rest):
    return jnp.concatenate([x, rest.astype(BF16)], axis=0)


def states_kernel(slabs, height, *refs):
    loaded, (out_ref, *held, total_ref, sems) = refs[:4], refs[4:]
    copies = [pltpu.make_async_copy(a, b, sems.at[i]) for i, (a, b) in enumerate(zip(loaded, held))]
    for copy in copies:
        copy.start()
    k_ref, v_ref = held[:2]
    channels, rows = k_ref.shape
    total_ref[...] = jnp.zeros_like(total_ref)
    pieces = out_ref.shape[0] // height
    out_ref[height * (pieces - 1) :, :] = jnp.zeros((height, LANES), F32)
    ones = jnp.ones((16, rows), BF16)
    copies[0].wait()
    for t in tiles(channels):
        total_ref[t.j : t.j + 1, : t.width] = dot_rows(ones, relu(k_ref[t.here, :]))[:1]
    total = total_ref[...]
    for s in range(pieces):
        at = height * (s + 1)
        out_ref[at - len(total) : at, :] = total
    copies[1].wait()
    for t in tiles(channels):
        both = dot_rows(v_ref[t.pair, :], relu(k_ref[t.here, :]))
        slabs.put(out_ref, t, heads_apart(t, both))
    copies[2].wait()
    copies[3].wait()


def total_of(parts):
    parts = list(parts)
    out = parts[0]
    for part in parts[1:]:
        out = out + part
    return out


def cut_rows(ref, pitch, piece, start, size):
    at = pitch * piece + start
    return ref[at : at + size, :]


def to_rows_kernel(sizes, in_ref, out_ref):
    rows, base, pitch = sizes
    height = in_ref.shape[0] // len(CHIP)
    sums = [
        total_of(cut_rows(in_ref, height, s, 0, height) for s, d in enumerate(CHIP) if d[0] == c)
        for c in range(2)
    ]
    totals = jnp.concatenate([s[rows * base :] for s in sums], axis=0)
    for y in range(rows):
        for c in range(2):
            at = pitch * y + base * c
            out_ref[at : at + base, :] = sums[c][base * y : base * (y + 1)]
        out_ref[pitch * y + 2 * base : pitch * (y + 1), :] = totals


def to_planes_kernel(sizes, in_ref, out_ref, own_ref):
    planes, base, pitch = sizes
    size = (pitch - 2 * base) // 2
    own = total_of(cut_rows(in_ref, pitch, s, 0, pitch) for s in range(in_ref.shape[0] // pitch))
    own_ref[...] = own
    first, second, low, high = own[:base], own[base : 2 * base], own[2 * base : -size], own[-size:]
    message = jnp.concatenate([first + second, low + high], axis=0)
    for p in range(planes):
        out_ref[len(message) * p : len(message) * (p + 1), :] = message


def suffix_kernel(rows, base, in_ref, own_ref, out_ref):
    z, core = lax.axis_index("z"), lax.axis_index("core")
    height = in_ref.shape[0] // len(PLANES)
    after = total_of(
        jnp.where(p > z, cut_rows(in_ref, height, s, 0, height), 0.0) for s, p in enumerate(PLANES)
    )
    own = own_ref[...]
    first, second, part = own[:base], own[base : 2 * base], own[2 * base :]
    late = after[:base] + second
    beyond = after[base:]
    message = jnp.concatenate(
        [late + first, late, beyond + part, beyond + jnp.where(core > 0, part, 0.0)], axis=0
    )
    for s in range(rows):
        out_ref[len(message) * s : len(message) * (s + 1), :] = message


def to_columns_kernel(sizes, in_ref, out_ref):
    rows, base, pitch = sizes
    size = (pitch - 2 * base) // 2
    height = rows * base + size
    for c in range(2):
        parts = [cut_rows(in_ref, pitch, y, base * c, base) for y in range(rows)]
        parts.append(
            total_of(cut_rows(in_ref, pitch, y, 2 * base + size * c, size) for y in range(rows))
        )
        message = jnp.concatenate(parts, axis=0)
        for s, d in enumerate(CHIP):
            if d[0] == c:
                out_ref[height * s : height * (s + 1), :] = message


def denominators(q_ref, total, padded):
    den = None
    for t in tiles(q_ref.shape[0]):
        spot = on_own_head(t, jnp.broadcast_to(total[t.j : t.j + 1, : t.width], (padded, t.width)))
        term = dot(jnp.concatenate(thirds(spot), axis=0), relu(q_ref[t.here, :]))
        den = term if den is None else den + term
    return den[:padded] + den[padded : 2 * padded] + den[2 * padded :] + 1.0


def gradient_states(slabs, q_ref, g_ref, rec, out_ref, hi_ref, lo_ref):
    channels = q_ref.shape[0]
    for h in range(channels // HEAD_DIM):
        hi, lo = halves(g_ref[of_head(h), :].astype(F32) * rec[h : h + 1])
        hi_ref[of_head(h), :], lo_ref[of_head(h), :] = hi, lo
    for t in tiles(channels):
        rhs = relu(q_ref[t.here, :])
        both = both_halves(dot_rows, hi_ref[t.pair, :], lo_ref[t.pair, :], rhs)
        slabs.put(out_ref, t, heads_apart(t, both))


def prefix(base, in_ref, own_ref):
    z, core = lax.axis_index("z"), lax.axis_index("core")
    height = in_ref.shape[0] // len(PLANES)
    before = total_of(
        jnp.where(p < z, cut_rows(in_ref, height, s, 0, height), 0.0) for s, p in enumerate(PLANES)
    )
    own, size = own_ref[...], height - base
    early = before[:base] + own[:base]
    total = before[base:] + own[2 * base : -size] + jnp.where(core > 0, own[-size:], 0.0)
    return early, early + own[base : 2 * base], total


def denominator_kernel(base, slabs, in_ref, own_ref, q_ref, g_ref, out_ref, rec_ref, total_ref, hi_ref, lo_ref):
    early, late, total = prefix(base, in_ref, own_ref)
    total_ref[...] = total
    rec = 1.0 / denominators(q_ref, total, rec_ref.shape[0])
    rec_ref[...] = rec
    pieces = len(FULL_ROWS)
    height = out_ref.shape[0] // pieces
    out_ref[-base:, :] = jnp.zeros((base, LANES), F32)
    gradient_states(slabs, q_ref, g_ref, rec, out_ref, hi_ref, lo_ref)
    for s in range(pieces):
        out_ref[height * s : height * s + base, :] = early
        out_ref[height * s + base : height * s + 2 * base, :] = late


def cross_kernel(base, in_ref, out_ref):
    pieces = len(FULL_ROWS)
    height = in_ref.shape[0] // pieces
    size = pieces * base
    order = [FULL_ROWS.index(y) for y in ROWS]
    states = [
        jnp.concatenate([cut_rows(in_ref, height, s, base * c, base) for s in order], axis=0)
        for c in range(2)
    ]
    share = total_of(cut_rows(in_ref, height, s, 2 * base, size) for s in range(pieces))
    for s, d in enumerate(CHIP):
        at = (size + base) * s
        out_ref[at : at + size, :] = states[d[0]]
        out_ref[at + size : at + size + base, :] = share[base * s : base * (s + 1)]


def attention(slabs, in_ref, q_ref, g_ref, rec, mixed_ref, sums_ref, gt_ref, *flat):
    channels = q_ref.shape[0]
    padded = rec.shape[0]
    for t in tiles(channels):
        keep_halves(t, slabs.get(in_ref, t), *flat)
    sums_ref[...] = jnp.zeros_like(sums_ref)
    gt_ref[...] = jnp.zeros_like(gt_ref)
    for h in range(channels // HEAD_DIM):
        attn = by_state(*flat, q_ref, h) * rec[h : h + 1]
        mixed_ref[of_head(h), :] = attn.astype(BF16)
        sums_ref[h : h + 1, :] = jnp.sum(g_ref[of_head(h), :].astype(F32) * attn, axis=0, keepdims=True)
    pair = jnp.concatenate(halves(-sums_ref[...] * rec), axis=0)
    for t in tiles(channels):
        term = dot_rows(pair, relu(q_ref[t.here, :]))
        term = on_own_head(t, term[:padded] + term[padded:])
        gt_ref[t.j : t.j + 1, : t.width] = jnp.sum(term, axis=0, keepdims=True)


def attention_kernel(planes, base, slabs, in_ref, q_ref, g_ref, rec_ref, out_ref, own_ref, mixed_ref, sums_ref, flat_hi_ref, flat_lo_ref, gt_ref):
    attention(slabs, in_ref, q_ref, g_ref, rec_ref[...], mixed_ref, sums_ref, gt_ref, flat_hi_ref, flat_lo_ref)
    height = in_ref.shape[0] // len(CHIP)
    sums = [
        total_of(cut_rows(in_ref, height, s, height - base, base) for s, d in enumerate(CHIP) if d[0] == c)
        for c in range(2)
    ]
    part = gt_ref[...]
    own_ref[...] = jnp.concatenate([*sums, part], axis=0)
    message = jnp.concatenate([sums[0] + sums[1], part], axis=0)
    for p in range(planes):
        out_ref[len(message) * p : len(message) * (p + 1), :] = message


def queries_kernel(slabs, in_ref, q_ref, g_ref, rec_ref, sums_ref, total_ref, out_ref, hi_ref, lo_ref):
    channels, rows = q_ref.shape
    for t in tiles(channels):
        shape = (LANES - HEAD_DIM, t.width)
        extra = jnp.where(row(shape) < 2, jnp.broadcast_to(total_ref[t.j : t.j + 1, : t.width], shape), 0.0)
        turn(t, slabs.get(in_ref, t), extra, hi_ref, lo_ref)
    for h in range(channels // HEAD_DIM):
        hi, lo = halves(-sums_ref[h : h + 1, :])
        shape = (LANES - HEAD_DIM, rows)
        rest = jnp.where(row(shape) == 0, jnp.broadcast_to(hi.astype(F32), shape), 0.0)
        rest = jnp.where(row(shape) == 1, jnp.broadcast_to(lo.astype(F32), shape), rest)
        rhs = with_rows(g_ref[of_head(h), :], rest)
        feature = both_halves(dot, hi_ref[of_head(h), :], lo_ref[of_head(h), :], rhs) * rec_ref[h : h + 1, :]
        q = q_ref[of_head(h), :].astype(F32)
        out_ref[of_head(h), :] = jnp.where(q > 0, feature, 0.0).astype(BF16)


def keys_kernel(slabs, in_ref, k_ref, v_ref, attn_ref, gq_ref, mixed_out, gq_out, gk_out, gv_out, gk_ref, gv_ref, flat_hi_ref, flat_lo_ref, hi_ref, lo_ref, sems):
    channels, rows = k_ref.shape
    heads, pieces = channels // HEAD_DIM, len(CHIP)
    middle = HEAD_DIM * (heads // 2)
    moves = [(attn_ref, mixed_out, 0, channels), (gq_ref, gq_out, 0, channels)]
    for begin, end in ((0, middle), (middle, channels)):
        moves += [(gk_ref, gk_out, begin, end), (gv_ref, gv_out, begin, end)]
    copies = [
        pltpu.make_async_copy(a.at[begin:end, :], b.at[begin:end, :], sems.at[n])
        for n, (a, b, begin, end) in enumerate(moves)
    ]
    copies[0].start()
    copies[1].start()
    height, count = in_ref.shape[0] // pieces, len(tiles(channels))
    total = total_of(cut_rows(in_ref, height, s, height - count, count) for s in range(pieces))
    for t in tiles(channels):
        shape = (LANES - HEAD_DIM, t.width)
        extra = jnp.where(row(shape) < 1, jnp.broadcast_to(total[t.j : t.j + 1, : t.width], shape), 0.0)
        state = slabs.get(in_ref, t)
        keep_halves(t, state, flat_hi_ref, flat_lo_ref)
        turn(t, state, extra, hi_ref, lo_ref)
    ones = jnp.ones((LANES - HEAD_DIM, rows), BF16)
    for h in range(heads):
        gv_ref[of_head(h), :] = by_state(flat_hi_ref, flat_lo_ref, k_ref, h).astype(BF16)
        rhs = with_rows(v_ref[of_head(h), :], ones)
        grad = both_halves(dot, hi_ref[of_head(h), :], lo_ref[of_head(h), :], rhs)
        k = k_ref[of_head(h), :].astype(F32)
        gk_ref[of_head(h), :] = jnp.where(k > 0, grad, 0.0).astype(BF16)
        if h == heads // 2 - 1:
            copies[2].start()
            copies[3].start()
    copies[4].start()
    copies[5].start()
    for copy in copies:
        copy.wait()


def call(kernel, out, in_specs, scratch=(), more=(), out_space=VMEM, flops=10**7, moved=10**6):
    shapes = [jax.ShapeDtypeStruct(s, d) for s, d in out]
    several = len(shapes) > 1
    return pl.pallas_call(
        kernel,
        out_shape=shapes if several else shapes[0],
        in_specs=in_specs,
        out_specs=[out_space] * len(shapes) if several else out_space,
        scratch_shapes=[pltpu.VMEM(s, d) for s, d in scratch] + list(more),
        cost_estimate=pl.CostEstimate(flops=flops, bytes_accessed=moved, transcendentals=0),
        compiler_params=pltpu.CompilerParams(vmem_limit_bytes=24 * 2**20),
    )


def exchanged(message, axes, order):
    sizes = [lax.axis_size(a) for a in axes]
    order = [int(np.ravel_multi_index(d, sizes)) for d in order]
    pieces = message.reshape(len(order), -1)
    pieces = lax.all_to_all(pieces, axes, 0, 0, tiled=True, axis_index_groups=[order])
    return pieces.reshape(message.shape)


def over_chips(message):
    return exchanged(message, ("core", "x"), CHIP)


def over_rows(message, order=ROWS):
    return exchanged(message, ("y",), [(y,) for y in order])


def over_planes(message):
    return exchanged(message, ("z",), [(z,) for z in PLANES])


def body(queries, keys_in, values_in, grad_attn):
    q, k, v, g = (a[0].T for a in (queries, keys_in, values_in, grad_attn))
    channels, rows = q.shape
    nx, ny, nz = (lax.axis_size(a) for a in ("x", "y", "z"))
    count = len(tiles(channels))
    each = -(-count * (HEAD_DIM // SLAB) // (2 * nx * ny))
    base = SLAB * each
    size = ny * base
    tall, pitch, short = size + count, 2 * (base + count), base + count
    wide, full = 2 * base + size, size + base

    def in_turn(height, first=0):
        return Slabs(lambda n: height * (n // (ny * each)) + first + SLAB * (n % (ny * each)))

    def last(n):
        row, chip = FULL_ROWS[n // (ny * each)], n % (ny * each) // each
        return tall * chip + base * ROWS.index(row) + SLAB * (n % each)

    outer, got = in_turn(tall), in_turn(full)
    flat, line = ((HEAD_DIM, channels), BF16), ((count, LANES), F32)
    whole, small = ((channels, rows), BF16), ((16, rows), F32)

    def message(pieces, height):
        return ((pieces * height, LANES), F32)

    sent, k, v, q, g = call(
        functools.partial(states_kernel, outer, tall),
        [message(2 * nx, tall)] + [whole] * 4, [HBM] * 4, [line], [pltpu.SemaphoreType.DMA((4,))],
    )(*(pltpu.with_memory_space_constraint(a, pltpu.HBM) for a in (k, v, q, g)))
    sent = call(
        functools.partial(to_rows_kernel, (ny, base, pitch)), [message(ny, pitch)], [VMEM]
    )(over_chips(sent))
    sent, own = call(
        functools.partial(to_planes_kernel, (nz, base, pitch)),
        [message(nz, short), message(1, pitch)], [VMEM],
    )(over_rows(sent))
    sent, rec, total = call(
        functools.partial(denominator_kernel, base, in_turn(wide, 2 * base)),
        [message(ny, wide), small, line], [VMEM] * 4, [whole, whole],
    )(over_planes(sent), own, q, g)
    sent = call(
        functools.partial(cross_kernel, base), [message(2 * nx, full)], [VMEM]
    )(over_rows(sent, FULL_ROWS))
    states = over_chips(sent)
    sent, own, attn, sums = call(
        functools.partial(attention_kernel, nz, base, got),
        [message(nz, short), message(1, base + short), whole, small], [VMEM] * 4, [flat, flat, line],
    )(states, q, g, rec)
    grad_queries = call(
        functools.partial(queries_kernel, got), [whole], [VMEM] * 6, [whole, whole]
    )(states, q, g, rec, sums, total)
    sent, grad_queries = lax.optimization_barrier((sent, grad_queries))
    sent = call(
        functools.partial(suffix_kernel, ny, base), [message(ny, pitch)], [VMEM] * 2
    )(over_planes(sent), own)
    sent = call(
        functools.partial(to_columns_kernel, (ny, base, pitch)), [message(2 * nx, tall)], [VMEM]
    )(over_rows(sent))
    outs = call(
        functools.partial(keys_kernel, Slabs(last)),
        [whole] * 4, [VMEM] * 5, [whole, whole, flat, flat, whole, whole],
        [pltpu.SemaphoreType.DMA((6,))], HBM,
    )(over_chips(sent), k, v, attn, grad_queries)
    return tuple(a.T[None] for a in outs)


def solution(mesh):
    groups, spaces = mesh.devices.shape
    split = Mesh(
        mesh.devices.reshape(groups // 2, 2, spaces // 8, 8), ("z", "core", "x", "y")
    )
    placed = P(("z", "core"), ("x", "y"), None)
    return jax.shard_map(
        body, mesh=split, in_specs=(placed,) * 4, out_specs=(placed,) * 4, check_vma=False
    )
```

```python
import functools

import jax
import jax.numpy as jnp
import numpy as np
from jax import lax
from jax.experimental import pallas as pl
from jax.experimental.pallas import tpu as pltpu
from jax.sharding import Mesh
from jax.sharding import PartitionSpec as P

PLANES = (0, 4, 1, 5, 2, 6, 3, 7)
ROWS = (0, 4, 2, 6, 1, 5, 3, 7)
FULL_ROWS = (0, 4, 1, 5, 2, 6, 3, 7)
CHIP = tuple((n % 2, n // 2) for n in (5, 0, 6, 4, 1, 7, 2, 3))

HEAD_DIM = 112
LANES = 128
SLAB = 8
F32, BF16 = jnp.float32, jnp.bfloat16
VMEM = pl.BlockSpec(memory_space=pltpu.VMEM)
HBM = pl.BlockSpec(memory_space=pltpu.HBM)
NT = (((1,), (1,)), ((), ()))


class Tile:
    def __init__(self, j, channels):
        self.j, self.at = j, LANES * j
        self.width = min(LANES, channels - self.at)
        self.first = self.at // HEAD_DIM
        self.last = (self.at + self.width - 1) // HEAD_DIM
        self.here = slice(self.at, self.at + self.width)
        self.cut = min(self.width, HEAD_DIM * (self.first + 1) - self.at)
        self.pair = slice(HEAD_DIM * self.first, HEAD_DIM * (self.last + 1))


def tiles(channels):
    return [Tile(j, channels) for j in range(-(-channels // LANES))]


def dot(a, b):
    return jnp.dot(a, b, preferred_element_type=F32)


def dot_rows(a, b):
    return lax.dot_general(a, b, (((1,), (1,)), ((), ())), preferred_element_type=F32)


def both_halves(by, hi, lo, rhs):
    out = by(jnp.concatenate([hi, lo], axis=0), rhs)
    return out[: len(hi)] + out[len(hi) :]


def halves(x):
    hi = x.astype(BF16)
    return hi, (x - hi.astype(F32)).astype(BF16)


def thirds(x):
    hi = x.astype(BF16)
    rest = x - hi.astype(F32)
    mid = rest.astype(BF16)
    return hi, mid, (rest - mid.astype(F32)).astype(BF16)


def relu(x):
    return jnp.maximum(x, jnp.zeros_like(x))


def lane(shape):
    return lax.broadcasted_iota(jnp.int32, shape, 1)


def row(shape):
    return lax.broadcasted_iota(jnp.int32, shape, 0)


def of_head(h):
    return slice(HEAD_DIM * h, HEAD_DIM * (h + 1))


def on_own_head(tile, x):
    heads = jnp.where(lane(x.shape) < tile.cut, tile.first, tile.last)
    return jnp.where(row(x.shape) == heads, x, 0.0)


def heads_apart(tile, both):
    if tile.first == tile.last:
        return both
    top, bottom = both[:HEAD_DIM], both[HEAD_DIM:]
    return jnp.where(lane(top.shape) < tile.cut, top, bottom)


class Slabs:
    def __init__(self, start):
        self.start = start

    def rows(self, tile):
        for i in range(HEAD_DIM // SLAB):
            at = self.start(HEAD_DIM // SLAB * tile.j + i)
            yield slice(SLAB * i, SLAB * (i + 1)), slice(at, at + SLAB)

    def put(self, ref, tile, value):
        for here, there in self.rows(tile):
            ref[there, : tile.width] = value[here]

    def get(self, ref, tile):
        parts = [ref[there, : tile.width] for _, there in self.rows(tile)]
        return jnp.concatenate(parts, axis=0)


def keep_halves(tile, state, hi_ref, lo_ref):
    hi_ref[:, tile.here], lo_ref[:, tile.here] = halves(state)


def by_state(hi_ref, lo_ref, rows_ref, h):
    channels, low, high = hi_ref.shape[1], HEAD_DIM * h, HEAD_DIM * (h + 1)
    start, stop = low // LANES * LANES, min(channels, -(-high // LANES) * LANES)
    own = relu(rows_ref[low:high, :])
    parts = [jnp.zeros((n, own.shape[1]), BF16) for n in (low - start, stop - high)]
    rhs = jnp.concatenate([p for p in (parts[0], own, parts[1]) if len(p)], axis=0)
    return both_halves(dot, hi_ref[:, start:stop], lo_ref[:, start:stop], rhs)


def turn(tile, state, extra, hi_ref, lo_ref):
    hi, lo = halves(jnp.concatenate([state, extra], axis=0).T)
    hi_ref[tile.here, :], lo_ref[tile.here, :] = hi, lo


def with_rows(x, rest):
    return jnp.concatenate([x, rest.astype(BF16)], axis=0)


def states_kernel(slabs, height, *refs):
    loaded, (out_ref, *held, total_ref, sems) = refs[:4], refs[4:]
    copies = [pltpu.make_async_copy(a, b, sems.at[i]) for i, (a, b) in enumerate(zip(loaded, held))]
    for copy in copies:
        copy.start()
    k_ref, v_ref = held[:2]
    channels, rows = k_ref.shape
    total_ref[...] = jnp.zeros_like(total_ref)
    pieces = out_ref.shape[0] // height
    out_ref[height * (pieces - 1) :, :] = jnp.zeros((height, LANES), F32)
    ones = jnp.ones((16, rows), BF16)
    copies[0].wait()
    for t in tiles(channels):
        total_ref[t.j : t.j + 1, : t.width] = dot_rows(ones, relu(k_ref[t.here, :]))[:1]
    total = total_ref[...]
    for s in range(pieces):
        at = height * (s + 1)
        out_ref[at - len(total) : at, :] = total
    copies[1].wait()
    for t in tiles(channels):
        both = dot_rows(v_ref[t.pair, :], relu(k_ref[t.here, :]))
        slabs.put(out_ref, t, heads_apart(t, both))
    copies[2].wait()
    copies[3].wait()


def total_of(parts):
    parts = list(parts)
    out = parts[0]
    for part in parts[1:]:
        out = out + part
    return out


def cut_rows(ref, pitch, piece, start, size):
    at = pitch * piece + start
    return ref[at : at + size, :]


def to_rows_kernel(sizes, in_ref, out_ref):
    rows, base, pitch = sizes
    height = in_ref.shape[0] // len(CHIP)
    sums = [
        total_of(cut_rows(in_ref, height, s, 0, height) for s, d in enumerate(CHIP) if d[0] == c)
        for c in range(2)
    ]
    totals = jnp.concatenate([s[rows * base :] for s in sums], axis=0)
    for y in range(rows):
        for c in range(2):
            at = pitch * y + base * c
            out_ref[at : at + base, :] = sums[c][base * y : base * (y + 1)]
        out_ref[pitch * y + 2 * base : pitch * (y + 1), :] = totals


def to_planes_kernel(sizes, in_ref, out_ref, own_ref):
    planes, base, pitch = sizes
    size = (pitch - 2 * base) // 2
    own = total_of(cut_rows(in_ref, pitch, s, 0, pitch) for s in range(in_ref.shape[0] // pitch))
    own_ref[...] = own
    first, second, low, high = own[:base], own[base : 2 * base], own[2 * base : -size], own[-size:]
    message = jnp.concatenate([first + second, low + high], axis=0)
    for p in range(planes):
        out_ref[len(message) * p : len(message) * (p + 1), :] = message


def suffix_kernel(rows, base, in_ref, own_ref, out_ref):
    z, core = lax.axis_index("z"), lax.axis_index("core")
    height = in_ref.shape[0] // len(PLANES)
    after = total_of(
        jnp.where(p > z, cut_rows(in_ref, height, s, 0, height), 0.0) for s, p in enumerate(PLANES)
    )
    own = own_ref[...]
    first, second, part = own[:base], own[base : 2 * base], own[2 * base :]
    late = after[:base] + second
    beyond = after[base:]
    message = jnp.concatenate(
        [late + first, late, beyond + part, beyond + jnp.where(core > 0, part, 0.0)], axis=0
    )
    for s in range(rows):
        out_ref[len(message) * s : len(message) * (s + 1), :] = message


def to_columns_kernel(sizes, in_ref, out_ref):
    rows, base, pitch = sizes
    size = (pitch - 2 * base) // 2
    height = rows * base + size
    for c in range(2):
        parts = [cut_rows(in_ref, pitch, y, base * c, base) for y in range(rows)]
        parts.append(
            total_of(cut_rows(in_ref, pitch, y, 2 * base + size * c, size) for y in range(rows))
        )
        message = jnp.concatenate(parts, axis=0)
        for s, d in enumerate(CHIP):
            if d[0] == c:
                out_ref[height * s : height * (s + 1), :] = message


def denominators(q_ref, total, padded):
    den = None
    for t in tiles(q_ref.shape[0]):
        spot = on_own_head(t, jnp.broadcast_to(total[t.j : t.j + 1, : t.width], (padded, t.width)))
        term = dot(jnp.concatenate(thirds(spot), axis=0), relu(q_ref[t.here, :]))
        den = term if den is None else den + term
    return den[:padded] + den[padded : 2 * padded] + den[2 * padded :] + 1.0


def gradient_states(slabs, q_ref, g_ref, rec, out_ref, hi_ref, lo_ref):
    channels = q_ref.shape[0]
    for h in range(channels // HEAD_DIM):
        hi, lo = halves(g_ref[of_head(h), :].astype(F32) * rec[h : h + 1])
        hi_ref[of_head(h), :], lo_ref[of_head(h), :] = hi, lo
    for t in tiles(channels):
        rhs = relu(q_ref[t.here, :])
        both = both_halves(dot_rows, hi_ref[t.pair, :], lo_ref[t.pair, :], rhs)
        slabs.put(out_ref, t, heads_apart(t, both))


def prefix(base, in_ref, own_ref):
    z, core = lax.axis_index("z"), lax.axis_index("core")
    height = in_ref.shape[0] // len(PLANES)
    before = total_of(
        jnp.where(p < z, cut_rows(in_ref, height, s, 0, height), 0.0) for s, p in enumerate(PLANES)
    )
    own, size = own_ref[...], height - base
    early = before[:base] + own[:base]
    total = before[base:] + own[2 * base : -size] + jnp.where(core > 0, own[-size:], 0.0)
    return early, early + own[base : 2 * base], total


def denominator_kernel(base, slabs, in_ref, own_ref, q_ref, g_ref, out_ref, rec_ref, total_ref, hi_ref, lo_ref):
    early, late, total = prefix(base, in_ref, own_ref)
    total_ref[...] = total
    rec = 1.0 / denominators(q_ref, total, rec_ref.shape[0])
    rec_ref[...] = rec
    pieces = len(FULL_ROWS)
    height = out_ref.shape[0] // pieces
    out_ref[-base:, :] = jnp.zeros((base, LANES), F32)
    gradient_states(slabs, q_ref, g_ref, rec, out_ref, hi_ref, lo_ref)
    for s in range(pieces):
        out_ref[height * s : height * s + base, :] = early
        out_ref[height * s + base : height * s + 2 * base, :] = late


def cross_kernel(base, in_ref, out_ref):
    pieces = len(FULL_ROWS)
    height = in_ref.shape[0] // pieces
    size = pieces * base
    order = [FULL_ROWS.index(y) for y in ROWS]
    states = [
        jnp.concatenate([cut_rows(in_ref, height, s, base * c, base) for s in order], axis=0)
        for c in range(2)
    ]
    share = total_of(cut_rows(in_ref, height, s, 2 * base, size) for s in range(pieces))
    for s, d in enumerate(CHIP):
        at = (size + base) * s
        out_ref[at : at + size, :] = states[d[0]]
        out_ref[at + size : at + size + base, :] = share[base * s : base * (s + 1)]


def attention(slabs, in_ref, q_ref, g_ref, rec, mixed_ref, sums_ref, gt_ref, *flat):
    channels = q_ref.shape[0]
    padded = rec.shape[0]
    for t in tiles(channels):
        keep_halves(t, slabs.get(in_ref, t), *flat)
    sums_ref[...] = jnp.zeros_like(sums_ref)
    gt_ref[...] = jnp.zeros_like(gt_ref)
    for h in range(channels // HEAD_DIM):
        attn = by_state(*flat, q_ref, h) * rec[h : h + 1]
        mixed_ref[of_head(h), :] = attn.astype(BF16)
        sums_ref[h : h + 1, :] = jnp.sum(g_ref[of_head(h), :].astype(F32) * attn, axis=0, keepdims=True)
    pair = jnp.concatenate(halves(-sums_ref[...] * rec), axis=0)
    for t in tiles(channels):
        term = dot_rows(pair, relu(q_ref[t.here, :]))
        term = on_own_head(t, term[:padded] + term[padded:])
        gt_ref[t.j : t.j + 1, : t.width] = jnp.sum(term, axis=0, keepdims=True)


def attention_kernel(planes, base, slabs, in_ref, q_ref, g_ref, rec_ref, total_ref, out_ref, own_ref, mixed_ref, gq_ref, sums_ref, flat_hi_ref, flat_lo_ref, gt_ref, hi_ref, lo_ref):
    attention(slabs, in_ref, q_ref, g_ref, rec_ref[...], mixed_ref, sums_ref, gt_ref, flat_hi_ref, flat_lo_ref)
    height = in_ref.shape[0] // len(CHIP)
    sums = [
        total_of(cut_rows(in_ref, height, s, height - base, base) for s, d in enumerate(CHIP) if d[0] == c)
        for c in range(2)
    ]
    part = gt_ref[...]
    own_ref[...] = jnp.concatenate([*sums, part], axis=0)
    message = jnp.concatenate([sums[0] + sums[1], part], axis=0)
    for p in range(planes):
        out_ref[len(message) * p : len(message) * (p + 1), :] = message
    queries(slabs, in_ref, q_ref, g_ref, rec_ref, sums_ref, total_ref, gq_ref, hi_ref, lo_ref)


def queries(slabs, in_ref, q_ref, g_ref, rec_ref, sums_ref, total_ref, out_ref, hi_ref, lo_ref):
    channels, rows = q_ref.shape
    for t in tiles(channels):
        shape = (LANES - HEAD_DIM, t.width)
        extra = jnp.where(row(shape) < 2, jnp.broadcast_to(total_ref[t.j : t.j + 1, : t.width], shape), 0.0)
        turn(t, slabs.get(in_ref, t), extra, hi_ref, lo_ref)
    for h in range(channels // HEAD_DIM):
        hi, lo = halves(-sums_ref[h : h + 1, :])
        shape = (LANES - HEAD_DIM, rows)
        rest = jnp.where(row(shape) == 0, jnp.broadcast_to(hi.astype(F32), shape), 0.0)
        rest = jnp.where(row(shape) == 1, jnp.broadcast_to(lo.astype(F32), shape), rest)
        rhs = with_rows(g_ref[of_head(h), :], rest)
        feature = both_halves(dot, hi_ref[of_head(h), :], lo_ref[of_head(h), :], rhs) * rec_ref[h : h + 1, :]
        q = q_ref[of_head(h), :].astype(F32)
        out_ref[of_head(h), :] = jnp.where(q > 0, feature, 0.0).astype(BF16)


def keys_kernel(slabs, in_ref, k_ref, v_ref, attn_ref, gq_ref, mixed_out, gq_out, gk_out, gv_out, gk_ref, gv_ref, flat_hi_ref, flat_lo_ref, hi_ref, lo_ref, sems):
    channels, rows = k_ref.shape
    heads, pieces = channels // HEAD_DIM, len(CHIP)
    ends = [HEAD_DIM * h for h in (heads // 2, heads - heads // 5, heads)]
    moves = [(attn_ref, mixed_out, 0, channels), (gq_ref, gq_out, 0, channels)]
    for begin, end in zip([0, *ends], ends):
        moves += [(gk_ref, gk_out, begin, end), (gv_ref, gv_out, begin, end)]
    copies = [
        pltpu.make_async_copy(a.at[begin:end, :], b.at[begin:end, :], sems.at[n])
        for n, (a, b, begin, end) in enumerate(moves)
    ]
    copies[0].start()
    copies[1].start()
    height, count = in_ref.shape[0] // pieces, len(tiles(channels))
    total = total_of(cut_rows(in_ref, height, s, height - count, count) for s in range(pieces))
    for t in tiles(channels):
        shape = (LANES - HEAD_DIM, t.width)
        extra = jnp.where(row(shape) < 1, jnp.broadcast_to(total[t.j : t.j + 1, : t.width], shape), 0.0)
        state = slabs.get(in_ref, t)
        keep_halves(t, state, flat_hi_ref, flat_lo_ref)
        turn(t, state, extra, hi_ref, lo_ref)
    ones = jnp.ones((LANES - HEAD_DIM, rows), BF16)
    for h in range(heads):
        gv_ref[of_head(h), :] = by_state(flat_hi_ref, flat_lo_ref, k_ref, h).astype(BF16)
        rhs = with_rows(v_ref[of_head(h), :], ones)
        grad = both_halves(dot, hi_ref[of_head(h), :], lo_ref[of_head(h), :], rhs)
        k = k_ref[of_head(h), :].astype(F32)
        gk_ref[of_head(h), :] = jnp.where(k > 0, grad, 0.0).astype(BF16)
        if HEAD_DIM * (h + 1) in ends:
            n = 2 + 2 * ends.index(HEAD_DIM * (h + 1))
            copies[n].start()
            copies[n + 1].start()
    for copy in copies:
        copy.wait()


def call(kernel, out, in_specs, scratch=(), more=(), out_space=VMEM, flops=10**7, moved=10**6):
    shapes = [jax.ShapeDtypeStruct(s, d) for s, d in out]
    several = len(shapes) > 1
    return pl.pallas_call(
        kernel,
        out_shape=shapes if several else shapes[0],
        in_specs=in_specs,
        out_specs=[out_space] * len(shapes) if several else out_space,
        scratch_shapes=[pltpu.VMEM(s, d) for s, d in scratch] + list(more),
        cost_estimate=pl.CostEstimate(flops=flops, bytes_accessed=moved, transcendentals=0),
        compiler_params=pltpu.CompilerParams(vmem_limit_bytes=24 * 2**20),
    )


def exchanged(message, axes, order):
    sizes = [lax.axis_size(a) for a in axes]
    order = [int(np.ravel_multi_index(d, sizes)) for d in order]
    pieces = message.reshape(len(order), -1)
    pieces = lax.all_to_all(pieces, axes, 0, 0, tiled=True, axis_index_groups=[order])
    return pieces.reshape(message.shape)


def over_chips(message):
    return exchanged(message, ("core", "x"), CHIP)


def over_rows(message, order=ROWS):
    return exchanged(message, ("y",), [(y,) for y in order])


def over_planes(message):
    return exchanged(message, ("z",), [(z,) for z in PLANES])


def body(queries, keys_in, values_in, grad_attn):
    q, k, v, g = (a[0].T for a in (queries, keys_in, values_in, grad_attn))
    channels, rows = q.shape
    nx, ny, nz = (lax.axis_size(a) for a in ("x", "y", "z"))
    count = len(tiles(channels))
    each = -(-count * (HEAD_DIM // SLAB) // (2 * nx * ny))
    base = SLAB * each
    size = ny * base
    tall, pitch, short = size + count, 2 * (base + count), base + count
    wide, full = 2 * base + size, size + base

    def in_turn(height, first=0):
        return Slabs(lambda n: height * (n // (ny * each)) + first + SLAB * (n % (ny * each)))

    def last(n):
        row, chip = FULL_ROWS[n // (ny * each)], n % (ny * each) // each
        return tall * chip + base * ROWS.index(row) + SLAB * (n % each)

    outer, got = in_turn(tall), in_turn(full)
    flat, line = ((HEAD_DIM, channels), BF16), ((count, LANES), F32)
    whole, small = ((channels, rows), BF16), ((16, rows), F32)

    def message(pieces, height):
        return ((pieces * height, LANES), F32)

    sent, k, v, q, g = call(
        functools.partial(states_kernel, outer, tall),
        [message(2 * nx, tall)] + [whole] * 4, [HBM] * 4, [line], [pltpu.SemaphoreType.DMA((4,))],
    )(*(pltpu.with_memory_space_constraint(a, pltpu.HBM) for a in (k, v, q, g)))
    sent = call(
        functools.partial(to_rows_kernel, (ny, base, pitch)), [message(ny, pitch)], [VMEM]
    )(over_chips(sent))
    sent, own = call(
        functools.partial(to_planes_kernel, (nz, base, pitch)),
        [message(nz, short), message(1, pitch)], [VMEM],
    )(over_rows(sent))
    sent, rec, total = call(
        functools.partial(denominator_kernel, base, in_turn(wide, 2 * base)),
        [message(ny, wide), small, line], [VMEM] * 4, [whole, whole],
    )(over_planes(sent), own, q, g)
    sent = call(
        functools.partial(cross_kernel, base), [message(2 * nx, full)], [VMEM]
    )(over_rows(sent, FULL_ROWS))
    states = over_chips(sent)
    sent, own, attn, grad_queries = call(
        functools.partial(attention_kernel, nz, base, got),
        [message(nz, short), message(1, base + short), whole, whole], [VMEM] * 5,
        [small, flat, flat, line, whole, whole],
    )(states, q, g, rec, total)
    sent = call(
        functools.partial(suffix_kernel, ny, base), [message(ny, pitch)], [VMEM] * 2
    )(over_planes(sent), own)
    sent = call(
        functools.partial(to_columns_kernel, (ny, base, pitch)), [message(2 * nx, tall)], [VMEM]
    )(over_rows(sent))
    outs = call(
        functools.partial(keys_kernel, Slabs(last)),
        [whole] * 4, [VMEM] * 5, [whole, whole, flat, flat, whole, whole],
        [pltpu.SemaphoreType.DMA((8,))], HBM,
    )(over_chips(sent), k, v, attn, grad_queries)
    return tuple(a.T[None] for a in outs)


def solution(mesh):
    groups, spaces = mesh.devices.shape
    split = Mesh(
        mesh.devices.reshape(groups // 2, 2, spaces // 8, 8), ("z", "core", "x", "y")
    )
    placed = P(("z", "core"), ("x", "y"), None)
    return jax.shard_map(
        body, mesh=split, in_specs=(placed,) * 4, out_specs=(placed,) * 4, check_vma=False
    )
```

```python
import functools

import jax
import jax.numpy as jnp
import numpy as np
from jax import lax
from jax.experimental import pallas as pl
from jax.experimental.pallas import tpu as pltpu
from jax.sharding import Mesh
from jax.sharding import PartitionSpec as P

PLANES = (0, 4, 1, 5, 2, 6, 3, 7)
ROWS = (0, 4, 2, 6, 1, 5, 3, 7)
FULL_ROWS = (0, 4, 1, 5, 2, 6, 3, 7)
CHIP = tuple((n % 2, n // 2) for n in (5, 0, 6, 4, 1, 7, 2, 3))

HEAD_DIM = 112
LANES = 128
SLAB = 8
F32, BF16 = jnp.float32, jnp.bfloat16
VMEM = pl.BlockSpec(memory_space=pltpu.VMEM)
HBM = pl.BlockSpec(memory_space=pltpu.HBM)
NT = (((1,), (1,)), ((), ()))


class Tile:
    def __init__(self, j, channels):
        self.j, self.at = j, LANES * j
        self.width = min(LANES, channels - self.at)
        self.first = self.at // HEAD_DIM
        self.last = (self.at + self.width - 1) // HEAD_DIM
        self.here = slice(self.at, self.at + self.width)
        self.cut = min(self.width, HEAD_DIM * (self.first + 1) - self.at)
        self.pair = slice(HEAD_DIM * self.first, HEAD_DIM * (self.last + 1))


def tiles(channels):
    return [Tile(j, channels) for j in range(-(-channels // LANES))]


def dot(a, b):
    return jnp.dot(a, b, preferred_element_type=F32)


def dot_rows(a, b):
    return lax.dot_general(a, b, (((1,), (1,)), ((), ())), preferred_element_type=F32)


def both_halves(by, hi, lo, rhs):
    out = by(jnp.concatenate([hi, lo], axis=0), rhs)
    return out[: len(hi)] + out[len(hi) :]


def halves(x):
    hi = x.astype(BF16)
    return hi, (x - hi.astype(F32)).astype(BF16)


def thirds(x):
    hi = x.astype(BF16)
    rest = x - hi.astype(F32)
    mid = rest.astype(BF16)
    return hi, mid, (rest - mid.astype(F32)).astype(BF16)


def relu(x):
    return jnp.maximum(x, jnp.zeros_like(x))


def lane(shape):
    return lax.broadcasted_iota(jnp.int32, shape, 1)


def row(shape):
    return lax.broadcasted_iota(jnp.int32, shape, 0)


def of_head(h):
    return slice(HEAD_DIM * h, HEAD_DIM * (h + 1))


def on_own_head(tile, x):
    heads = jnp.where(lane(x.shape) < tile.cut, tile.first, tile.last)
    return jnp.where(row(x.shape) == heads, x, 0.0)


def heads_apart(tile, both):
    if tile.first == tile.last:
        return both
    top, bottom = both[:HEAD_DIM], both[HEAD_DIM:]
    return jnp.where(lane(top.shape) < tile.cut, top, bottom)


class Slabs:
    def __init__(self, start):
        self.start = start

    def rows(self, tile):
        for i in range(HEAD_DIM // SLAB):
            at = self.start(HEAD_DIM // SLAB * tile.j + i)
            yield slice(SLAB * i, SLAB * (i + 1)), slice(at, at + SLAB)

    def put(self, ref, tile, value):
        for here, there in self.rows(tile):
            ref[there, : tile.width] = value[here]

    def get(self, ref, tile):
        parts = [ref[there, : tile.width] for _, there in self.rows(tile)]
        return jnp.concatenate(parts, axis=0)


def keep_halves(tile, state, hi_ref, lo_ref):
    hi_ref[:, tile.here], lo_ref[:, tile.here] = halves(state)


def by_state(hi_ref, lo_ref, rows_ref, h):
    channels, low, high = hi_ref.shape[1], HEAD_DIM * h, HEAD_DIM * (h + 1)
    start, stop = low // LANES * LANES, min(channels, -(-high // LANES) * LANES)
    own = relu(rows_ref[low:high, :])
    parts = [jnp.zeros((n, own.shape[1]), BF16) for n in (low - start, stop - high)]
    rhs = jnp.concatenate([p for p in (parts[0], own, parts[1]) if len(p)], axis=0)
    return both_halves(dot, hi_ref[:, start:stop], lo_ref[:, start:stop], rhs)


def turn(tile, state, extra, hi_ref, lo_ref):
    hi, lo = halves(jnp.concatenate([state, extra], axis=0).T)
    hi_ref[tile.here, :], lo_ref[tile.here, :] = hi, lo


def with_rows(x, rest):
    return jnp.concatenate([x, rest.astype(BF16)], axis=0)


def states_kernel(slabs, height, *refs):
    loaded, (out_ref, *held, total_ref, sems) = refs[:4], refs[4:]
    copies = [pltpu.make_async_copy(a, b, sems.at[i]) for i, (a, b) in enumerate(zip(loaded, held))]
    for copy in copies:
        copy.start()
    k_ref, v_ref = held[:2]
    channels, rows = k_ref.shape
    total_ref[...] = jnp.zeros_like(total_ref)
    pieces = out_ref.shape[0] // height
    out_ref[height * (pieces - 1) :, :] = jnp.zeros((height, LANES), F32)
    ones = jnp.ones((16, rows), BF16)
    copies[0].wait()
    for t in tiles(channels):
        total_ref[t.j : t.j + 1, : t.width] = dot_rows(ones, relu(k_ref[t.here, :]))[:1]
    total = total_ref[...]
    for s in range(pieces):
        at = height * (s + 1)
        out_ref[at - len(total) : at, :] = total
    copies[1].wait()
    for t in tiles(channels):
        both = dot_rows(v_ref[t.pair, :], relu(k_ref[t.here, :]))
        slabs.put(out_ref, t, heads_apart(t, both))
    copies[2].wait()
    copies[3].wait()


def total_of(parts):
    parts = list(parts)
    out = parts[0]
    for part in parts[1:]:
        out = out + part
    return out


def cut_rows(ref, pitch, piece, start, size):
    at = pitch * piece + start
    return ref[at : at + size, :]


def to_rows_kernel(sizes, in_ref, out_ref):
    rows, base, pitch = sizes
    height = in_ref.shape[0] // len(CHIP)
    sums = [
        total_of(cut_rows(in_ref, height, s, 0, height) for s, d in enumerate(CHIP) if d[0] == c)
        for c in range(2)
    ]
    totals = jnp.concatenate([s[rows * base :] for s in sums], axis=0)
    for y in range(rows):
        for c in range(2):
            at = pitch * y + base * c
            out_ref[at : at + base, :] = sums[c][base * y : base * (y + 1)]
        out_ref[pitch * y + 2 * base : pitch * (y + 1), :] = totals


def to_planes_kernel(sizes, in_ref, out_ref, own_ref):
    planes, base, pitch = sizes
    size = (pitch - 2 * base) // 2
    own = total_of(cut_rows(in_ref, pitch, s, 0, pitch) for s in range(in_ref.shape[0] // pitch))
    own_ref[...] = own
    first, second, low, high = own[:base], own[base : 2 * base], own[2 * base : -size], own[-size:]
    message = jnp.concatenate([first + second, low + high], axis=0)
    for p in range(planes):
        out_ref[len(message) * p : len(message) * (p + 1), :] = message


def suffix_kernel(rows, base, in_ref, own_ref, out_ref):
    z, core = lax.axis_index("z"), lax.axis_index("core")
    height = in_ref.shape[0] // len(PLANES)
    after = total_of(
        jnp.where(p > z, cut_rows(in_ref, height, s, 0, height), 0.0) for s, p in enumerate(PLANES)
    )
    own = own_ref[...]
    first, second, part = own[:base], own[base : 2 * base], own[2 * base :]
    late = after[:base] + second
    beyond = after[base:]
    message = jnp.concatenate(
        [late + first, late, beyond + part, beyond + jnp.where(core > 0, part, 0.0)], axis=0
    )
    for s in range(rows):
        out_ref[len(message) * s : len(message) * (s + 1), :] = message


def to_columns_kernel(sizes, in_ref, out_ref):
    rows, base, pitch = sizes
    size = (pitch - 2 * base) // 2
    height = rows * base + size
    for c in range(2):
        parts = [cut_rows(in_ref, pitch, y, base * c, base) for y in range(rows)]
        parts.append(
            total_of(cut_rows(in_ref, pitch, y, 2 * base + size * c, size) for y in range(rows))
        )
        message = jnp.concatenate(parts, axis=0)
        for s, d in enumerate(CHIP):
            if d[0] == c:
                out_ref[height * s : height * (s + 1), :] = message


def denominators(q_ref, total, padded):
    den = None
    for t in tiles(q_ref.shape[0]):
        spot = on_own_head(t, jnp.broadcast_to(total[t.j : t.j + 1, : t.width], (padded, t.width)))
        term = dot(jnp.concatenate(thirds(spot), axis=0), relu(q_ref[t.here, :]))
        den = term if den is None else den + term
    return den[:padded] + den[padded : 2 * padded] + den[2 * padded :] + 1.0


def gradient_states(slabs, q_ref, g_ref, rec, out_ref, hi_ref, lo_ref):
    channels = q_ref.shape[0]
    for h in range(channels // HEAD_DIM):
        hi, lo = halves(g_ref[of_head(h), :].astype(F32) * rec[h : h + 1])
        hi_ref[of_head(h), :], lo_ref[of_head(h), :] = hi, lo
    for t in tiles(channels):
        rhs = relu(q_ref[t.here, :])
        both = both_halves(dot_rows, hi_ref[t.pair, :], lo_ref[t.pair, :], rhs)
        slabs.put(out_ref, t, heads_apart(t, both))


def prefix(base, in_ref, own_ref):
    z, core = lax.axis_index("z"), lax.axis_index("core")
    height = in_ref.shape[0] // len(PLANES)
    before = total_of(
        jnp.where(p < z, cut_rows(in_ref, height, s, 0, height), 0.0) for s, p in enumerate(PLANES)
    )
    own, size = own_ref[...], height - base
    early = before[:base] + own[:base]
    total = before[base:] + own[2 * base : -size] + jnp.where(core > 0, own[-size:], 0.0)
    return early, early + own[base : 2 * base], total


def denominator_kernel(base, slabs, in_ref, own_ref, q_ref, g_ref, out_ref, rec_ref, total_ref, hi_ref, lo_ref):
    early, late, total = prefix(base, in_ref, own_ref)
    total_ref[...] = total
    rec = 1.0 / denominators(q_ref, total, rec_ref.shape[0])
    rec_ref[...] = rec
    pieces = len(FULL_ROWS)
    height = out_ref.shape[0] // pieces
    out_ref[-base:, :] = jnp.zeros((base, LANES), F32)
    gradient_states(slabs, q_ref, g_ref, rec, out_ref, hi_ref, lo_ref)
    for s in range(pieces):
        out_ref[height * s : height * s + base, :] = early
        out_ref[height * s + base : height * s + 2 * base, :] = late


def cross_kernel(base, in_ref, out_ref):
    pieces = len(FULL_ROWS)
    height = in_ref.shape[0] // pieces
    size = pieces * base
    order = [FULL_ROWS.index(y) for y in ROWS]
    states = [
        jnp.concatenate([cut_rows(in_ref, height, s, base * c, base) for s in order], axis=0)
        for c in range(2)
    ]
    share = total_of(cut_rows(in_ref, height, s, 2 * base, size) for s in range(pieces))
    for s, d in enumerate(CHIP):
        at = (size + base) * s
        out_ref[at : at + size, :] = states[d[0]]
        out_ref[at + size : at + size + base, :] = share[base * s : base * (s + 1)]


def attention(slabs, in_ref, q_ref, g_ref, rec, mixed_ref, sums_ref, gt_ref, *flat):
    channels = q_ref.shape[0]
    padded = rec.shape[0]
    for t in tiles(channels):
        keep_halves(t, slabs.get(in_ref, t), *flat)
    sums_ref[...] = jnp.zeros_like(sums_ref)
    gt_ref[...] = jnp.zeros_like(gt_ref)
    for h in range(channels // HEAD_DIM):
        attn = by_state(*flat, q_ref, h) * rec[h : h + 1]
        mixed_ref[of_head(h), :] = attn.astype(BF16)
        sums_ref[h : h + 1, :] = jnp.sum(g_ref[of_head(h), :].astype(F32) * attn, axis=0, keepdims=True)
    pair = jnp.concatenate(halves(-sums_ref[...] * rec), axis=0)
    for t in tiles(channels):
        term = dot_rows(pair, relu(q_ref[t.here, :]))
        term = on_own_head(t, term[:padded] + term[padded:])
        gt_ref[t.j : t.j + 1, : t.width] = jnp.sum(term, axis=0, keepdims=True)


def attention_kernel(planes, base, slabs, in_ref, q_ref, g_ref, rec_ref, total_ref, out_ref, own_ref, mixed_ref, gq_ref, sums_ref, flat_hi_ref, flat_lo_ref, gt_ref, hi_ref, lo_ref):
    attention(slabs, in_ref, q_ref, g_ref, rec_ref[...], mixed_ref, sums_ref, gt_ref, flat_hi_ref, flat_lo_ref)
    height = in_ref.shape[0] // len(CHIP)
    sums = [
        total_of(cut_rows(in_ref, height, s, height - base, base) for s, d in enumerate(CHIP) if d[0] == c)
        for c in range(2)
    ]
    part = gt_ref[...]
    own_ref[...] = jnp.concatenate([*sums, part], axis=0)
    message = jnp.concatenate([sums[0] + sums[1], part], axis=0)
    for p in range(planes):
        out_ref[len(message) * p : len(message) * (p + 1), :] = message
    queries(slabs, in_ref, q_ref, g_ref, rec_ref, sums_ref, total_ref, gq_ref, hi_ref, lo_ref)


def queries(slabs, in_ref, q_ref, g_ref, rec_ref, sums_ref, total_ref, out_ref, hi_ref, lo_ref):
    channels, rows = q_ref.shape
    for t in tiles(channels):
        shape = (LANES - HEAD_DIM, t.width)
        extra = jnp.where(row(shape) < 2, jnp.broadcast_to(total_ref[t.j : t.j + 1, : t.width], shape), 0.0)
        turn(t, slabs.get(in_ref, t), extra, hi_ref, lo_ref)
    for h in range(channels // HEAD_DIM):
        hi, lo = halves(-sums_ref[h : h + 1, :])
        shape = (LANES - HEAD_DIM, rows)
        rest = jnp.where(row(shape) == 0, jnp.broadcast_to(hi.astype(F32), shape), 0.0)
        rest = jnp.where(row(shape) == 1, jnp.broadcast_to(lo.astype(F32), shape), rest)
        rhs = with_rows(g_ref[of_head(h), :], rest)
        feature = both_halves(dot, hi_ref[of_head(h), :], lo_ref[of_head(h), :], rhs) * rec_ref[h : h + 1, :]
        q = q_ref[of_head(h), :].astype(F32)
        out_ref[of_head(h), :] = jnp.where(q > 0, feature, 0.0).astype(BF16)


def keys_kernel(slabs, in_ref, k_ref, v_ref, attn_ref, gq_ref, mixed_out, gq_out, gk_out, gv_out, gk_ref, gv_ref, flat_hi_ref, flat_lo_ref, hi_ref, lo_ref, sems):
    channels, rows = k_ref.shape
    heads, pieces = channels // HEAD_DIM, len(CHIP)
    ends = [HEAD_DIM * h for h in (heads // 2, heads - heads // 5, heads)]
    moves = [(attn_ref, mixed_out, 0, channels), (gq_ref, gq_out, 0, channels)]
    for a, b in ((gv_ref, gv_out), (gk_ref, gk_out)):
        moves += [(a, b, begin, end) for begin, end in zip([0, *ends], ends)]
    copies = [
        pltpu.make_async_copy(a.at[begin:end, :], b.at[begin:end, :], sems.at[n])
        for n, (a, b, begin, end) in enumerate(moves)
    ]
    copies[0].start()
    copies[1].start()
    height, count = in_ref.shape[0] // pieces, len(tiles(channels))
    total = total_of(cut_rows(in_ref, height, s, height - count, count) for s in range(pieces))
    for t in tiles(channels):
        keep_halves(t, slabs.get(in_ref, t), flat_hi_ref, flat_lo_ref)
    for h in range(heads):
        gv_ref[of_head(h), :] = by_state(flat_hi_ref, flat_lo_ref, k_ref, h).astype(BF16)
        if HEAD_DIM * (h + 1) in ends:
            copies[2 + ends.index(HEAD_DIM * (h + 1))].start()
    for t in tiles(channels):
        shape = (LANES - HEAD_DIM, t.width)
        extra = jnp.where(row(shape) < 1, jnp.broadcast_to(total[t.j : t.j + 1, : t.width], shape), 0.0)
        turn(t, slabs.get(in_ref, t), extra, hi_ref, lo_ref)
    ones = jnp.ones((LANES - HEAD_DIM, rows), BF16)
    for h in range(heads):
        rhs = with_rows(v_ref[of_head(h), :], ones)
        grad = both_halves(dot, hi_ref[of_head(h), :], lo_ref[of_head(h), :], rhs)
        k = k_ref[of_head(h), :].astype(F32)
        gk_ref[of_head(h), :] = jnp.where(k > 0, grad, 0.0).astype(BF16)
        if HEAD_DIM * (h + 1) in ends:
            copies[5 + ends.index(HEAD_DIM * (h + 1))].start()
    for copy in copies:
        copy.wait()


def call(kernel, out, in_specs, scratch=(), more=(), out_space=VMEM, flops=10**7, moved=10**6):
    shapes = [jax.ShapeDtypeStruct(s, d) for s, d in out]
    several = len(shapes) > 1
    return pl.pallas_call(
        kernel,
        out_shape=shapes if several else shapes[0],
        in_specs=in_specs,
        out_specs=[out_space] * len(shapes) if several else out_space,
        scratch_shapes=[pltpu.VMEM(s, d) for s, d in scratch] + list(more),
        cost_estimate=pl.CostEstimate(flops=flops, bytes_accessed=moved, transcendentals=0),
        compiler_params=pltpu.CompilerParams(vmem_limit_bytes=24 * 2**20),
    )


def exchanged(message, axes, order):
    sizes = [lax.axis_size(a) for a in axes]
    order = [int(np.ravel_multi_index(d, sizes)) for d in order]
    pieces = message.reshape(len(order), -1)
    pieces = lax.all_to_all(pieces, axes, 0, 0, tiled=True, axis_index_groups=[order])
    return pieces.reshape(message.shape)


def over_chips(message):
    return exchanged(message, ("core", "x"), CHIP)


def over_rows(message, order=ROWS):
    return exchanged(message, ("y",), [(y,) for y in order])


def over_planes(message):
    return exchanged(message, ("z",), [(z,) for z in PLANES])


def body(queries, keys_in, values_in, grad_attn):
    q, k, v, g = (a[0].T for a in (queries, keys_in, values_in, grad_attn))
    channels, rows = q.shape
    nx, ny, nz = (lax.axis_size(a) for a in ("x", "y", "z"))
    count = len(tiles(channels))
    each = -(-count * (HEAD_DIM // SLAB) // (2 * nx * ny))
    base = SLAB * each
    size = ny * base
    tall, pitch, short = size + count, 2 * (base + count), base + count
    wide, full = 2 * base + size, size + base

    def in_turn(height, first=0):
        return Slabs(lambda n: height * (n // (ny * each)) + first + SLAB * (n % (ny * each)))

    def last(n):
        row, chip = FULL_ROWS[n // (ny * each)], n % (ny * each) // each
        return tall * chip + base * ROWS.index(row) + SLAB * (n % each)

    outer, got = in_turn(tall), in_turn(full)
    flat, line = ((HEAD_DIM, channels), BF16), ((count, LANES), F32)
    whole, small = ((channels, rows), BF16), ((16, rows), F32)

    def message(pieces, height):
        return ((pieces * height, LANES), F32)

    sent, k, v, q, g = call(
        functools.partial(states_kernel, outer, tall),
        [message(2 * nx, tall)] + [whole] * 4, [HBM] * 4, [line], [pltpu.SemaphoreType.DMA((4,))],
    )(*(pltpu.with_memory_space_constraint(a, pltpu.HBM) for a in (k, v, q, g)))
    sent = call(
        functools.partial(to_rows_kernel, (ny, base, pitch)), [message(ny, pitch)], [VMEM]
    )(over_chips(sent))
    sent, own = call(
        functools.partial(to_planes_kernel, (nz, base, pitch)),
        [message(nz, short), message(1, pitch)], [VMEM],
    )(over_rows(sent))
    sent, rec, total = call(
        functools.partial(denominator_kernel, base, in_turn(wide, 2 * base)),
        [message(ny, wide), small, line], [VMEM] * 4, [whole, whole],
    )(over_planes(sent), own, q, g)
    sent = call(
        functools.partial(cross_kernel, base), [message(2 * nx, full)], [VMEM]
    )(over_rows(sent, FULL_ROWS))
    states = over_chips(sent)
    sent, own, attn, grad_queries = call(
        functools.partial(attention_kernel, nz, base, got),
        [message(nz, short), message(1, base + short), whole, whole], [VMEM] * 5,
        [small, flat, flat, line, whole, whole],
    )(states, q, g, rec, total)
    sent = call(
        functools.partial(suffix_kernel, ny, base), [message(ny, pitch)], [VMEM] * 2
    )(over_planes(sent), own)
    sent = call(
        functools.partial(to_columns_kernel, (ny, base, pitch)), [message(2 * nx, tall)], [VMEM]
    )(over_rows(sent))
    outs = call(
        functools.partial(keys_kernel, Slabs(last)),
        [whole] * 4, [VMEM] * 5, [whole, whole, flat, flat, whole, whole],
        [pltpu.SemaphoreType.DMA((8,))], HBM,
    )(over_chips(sent), k, v, attn, grad_queries)
    return tuple(a.T[None] for a in outs)


def solution(mesh):
    groups, spaces = mesh.devices.shape
    split = Mesh(
        mesh.devices.reshape(groups // 2, 2, spaces // 8, 8), ("z", "core", "x", "y")
    )
    placed = P(("z", "core"), ("x", "y"), None)
    return jax.shard_map(
        body, mesh=split, in_specs=(placed,) * 4, out_specs=(placed,) * 4, check_vma=False
    )
```
